256 devices in a mesh: dp: 16 (over z_lo, x, core), tensor: 16 (over y, z_hi).
Axes of the slice: x: 4, y: 4, z: 8 (z_hi: 4, z_lo: 2; z = z_hi * 2 + z_lo), core: 2. Of those that a mesh axis runs over, the one named last changes fastest.
Arguments:
- hidden: bfloat16 [6144, 8192], P('dp', 'tensor'), may hold values from -6 to 6
- base_weight: bfloat16 [8192, 8192], P(None, 'tensor'), may hold values from -0.0625 to 0.0625
- generators: float32 [8, 64, 8192], P(None, None, 'tensor'), may hold values from -0.24 to 0.24
- cotangent: bfloat16 [6144, 8192], P('dp', 'tensor'), may hold values from -6 to 6
Outputs:
- query: bfloat16 [6144, 8192], P('dp', 'tensor')
- input_grad: bfloat16 [6144, 8192], P('dp', 'tensor')
- factor_grad: float32 [8, 64, 8192], P(None, None, 'tensor')
The draws below stay inside these ranges and needn't reach their ends.
All inputs are finite; a program needn't handle non-finite values.
Results may differ from the reference program's by a relative error of at most 0.0065.
Values may be sent and summed in bfloat16 or wider, within the bound.
A program may use at most 128 MiB of HBM per device.

```python
import math
import jax
import jax.numpy as jnp
from jax import lax

D = 8192
GROUP = 32
FACTORS = 8
TOK_DEV = 384
TOKENS = 6144
N_DP = 16


def steps_of(own_key, dims, pieces, smallest, largest):
    factor_of, own = 1.0, jax.random.fold_in(own_key, 6)
    for dim, blocks in pieces:
        heights = jnp.exp(jax.random.uniform(jax.random.fold_in(own, dim), (blocks,), jnp.float32, smallest / len(pieces), largest / len(pieces)))
        factor_of = factor_of * jnp.repeat(heights, dims[dim] // blocks).reshape([-1 if axis == dim else 1 for axis in range(len(dims))])
    return factor_of


def noise(stream_key, shape, width, bound, shards=(), dtype=jnp.bfloat16):
    drawn = width * jax.random.normal(stream_key, shape, jnp.float32)
    if shards:
        drawn = drawn * steps_of(stream_key, shape, shards, -0.22, 0.18)
    return jnp.clip(drawn, -bound, bound).astype(dtype)


def setup_inputs(seed: int = 0) -> dict:
    key_of = jax.random.split(jax.random.key(seed), 5)
    return {
        "hidden": noise(key_of[0], (TOKENS, D), 1.0, 6.0, ((0, 16), (1, 16))),
        "base_weight": noise(key_of[1], (D, D), D ** -0.5, 0.0625, ((1, 16),)),
        "generators": noise(key_of[2], (FACTORS, 2 * GROUP, D), 0.04, 0.24, ((2, 16),), jnp.float32),
        "cotangent": noise(key_of[3], (TOKENS, D), 1.0, 6.0, ((0, 16), (1, 16))),
    }


def pair_flip(values, stride):
    count, groups, half_block = values.shape
    shaped = values.reshape(count, groups // (2 * stride), 2, stride, half_block)
    return shaped[:, :, ::-1].reshape(count, groups, half_block)

def apply_factor(values, factor, stride):
    count, groups, half_block = values.shape
    partner = pair_flip(values, stride)
    upper_mask = (jnp.arange(groups) // stride % 2 == 1)[None, :, None]
    low_half = jnp.where(upper_mask, partner, values)
    high_half = jnp.where(upper_mask, values, partner)
    mixed = jnp.einsum('nci,icr->ncr', low_half, factor[:half_block], precision=lax.Precision.HIGHEST)
    mixed = mixed + jnp.einsum('nci,icr->ncr', high_half, factor[half_block:], precision=lax.Precision.HIGHEST)
    return values + mixed

def butterfly(values, generators):
    groups = D // GROUP
    for factor_idx in range(FACTORS):
        factor = generators[factor_idx].reshape(2 * GROUP, groups, GROUP)
        values = apply_factor(values, factor, 2 ** factor_idx)
    return values

def reference(hidden, base_weight, generators, cotangent):
    groups = D // GROUP
    hidden_blocks = hidden.reshape(N_DP, TOK_DEV, D)
    cot_blocks = cotangent.reshape(N_DP, TOK_DEV, D)

    def step(acc, block):
        tok_block, cot_block = block
        base = jnp.dot(tok_block, base_weight, preferred_element_type=jnp.float32)
        states, pullback = jax.vjp(butterfly, base.reshape(TOK_DEV, groups, GROUP), generators)
        base_grad, gen_grad = pullback(cot_block.astype(jnp.float32).reshape(TOK_DEV, groups, GROUP))
        base_grad_b = base_grad.reshape(TOK_DEV, D).astype(jnp.bfloat16)
        in_grad = jnp.dot(base_grad_b, base_weight.T, preferred_element_type=jnp.float32).astype(jnp.bfloat16)
        return (acc + gen_grad, (states.reshape(TOK_DEV, D).astype(jnp.bfloat16), in_grad))
    total, outputs = lax.scan(step, jnp.zeros(generators.shape, jnp.float32), (hidden_blocks, cot_blocks))
    query = outputs[0].reshape(TOKENS, D)
    input_grad = outputs[1].reshape(TOKENS, D)
    factor_grad = total * (1.0 / math.sqrt(TOKENS))
    return (query, input_grad, factor_grad)
```

```python
import functools
import math

import jax
import jax.numpy as jnp
from jax import lax
from jax.experimental import pallas as pl
from jax.experimental.pallas import tpu as pltpu
from jax.sharding import PartitionSpec as P

MESH = pl.DeviceIdType.MESH
F32 = jnp.float32
BF16 = jnp.bfloat16
SIDE = 4
LANES = 128
HALF = 32
VMEM_BYTES = 60 * 1024 * 1024


def wrap(value, n):
    return lax.rem(value + n, n)


def dot(a, b):
    return jnp.dot(a, b, preferred_element_type=F32)


def dot_nt(a, b):
    return lax.dot_general(a, b, (((1,), (1,)), ((), ())), preferred_element_type=F32)


def dot_tn(a, b):
    return lax.dot_general(a, b, (((0,), (0,)), ((), ())), preferred_element_type=F32)


def groups_of(shape):
    rows = lax.broadcasted_iota(jnp.int32, shape, 0) >> 5
    cols = lax.broadcasted_iota(jnp.int32, shape, 1) >> 5
    return rows, cols


def spread(block, mask, copies):
    return jnp.where(mask, jnp.concatenate([block] * copies, axis=0), 0.0)


def pair_matrix(gen_a, gen_b):
    both = jnp.concatenate([gen_a, gen_b], axis=1)
    rows, cols = groups_of((LANES, 2 * LANES))
    mask = rows == (cols & 3)
    return jnp.concatenate(
        [spread(both[:HALF], mask, 4), spread(both[HALF:], mask, 4)], axis=0
    ).astype(BF16)


def pair_extract(grad):
    cols = (lax.broadcasted_iota(jnp.int32, (HALF, 2 * LANES), 1) >> 5) & 3
    parts = []
    for h in range(2):
        total = jnp.zeros((HALF, 2 * LANES), F32)
        for g in range(4):
            start = h * LANES + g * HALF
            total = total + jnp.where(cols == g, grad[start : start + HALF], 0.0)
        parts.append(total)
    return jnp.concatenate(parts, axis=0)


def near_matrix(gen, k):
    rows, cols = groups_of((256, 256))
    low = cols & ~(1 << k)
    return (
        spread(gen[:HALF], rows == low, 8) + spread(gen[HALF:], rows == (low | (1 << k)), 8)
    ).astype(BF16)


def near_extract(grad, k):
    cols = lax.broadcasted_iota(jnp.int32, (HALF, 256), 1) >> 5
    low = cols & ~(1 << k)
    parts = []
    for want in (low, low | (1 << k)):
        total = jnp.zeros((HALF, 256), F32)
        for g in range(8):
            total = total + jnp.where(want == g, grad[g * HALF : (g + 1) * HALF], 0.0)
        parts.append(total)
    return jnp.concatenate(parts, axis=0)


def diag_matrix(block):
    rows, cols = groups_of((256, 256))
    return spread(block, rows == cols, 8).astype(BF16)


def diag_extract(grad):
    cols = lax.broadcasted_iota(jnp.int32, (HALF, 256), 1) >> 5
    total = jnp.zeros((HALF, 256), F32)
    for g in range(8):
        total = total + jnp.where(cols == g, grad[g * HALF : (g + 1) * HALF], 0.0)
    return total


class Ids:
    def __init__(self):
        self.next = 0

    def take(self, n=1):
        first = self.next
        self.next += n
        return first


IDS = Ids()
AG_Z = IDS.take(4)
AG_Y = [IDS.take(4) for _ in range(4)]
RS_Y = [IDS.take(4) for _ in range(4)]
RS_Z = IDS.take(4)
GEN_Z = IDS.take(4)
GEN_Y = IDS.take(4)
COT_Y = IDS.take(4)
BWD_T = IDS.take(4)
BWD_Z = IDS.take(4)
FWD_Z = IDS.take(4)
FWD_T = IDS.take(4)
FWD_Y = IDS.take(4)
OUT_Z = IDS.take(4)
OUT_Y = IDS.take(4)
N_SEMS = IDS.next


def main_kernel(
    hid, wt, gen, cot, query, igrad, ggrad,
    w_v, hbuf, base, gz, gy, gyb, gzb, ghome, gsave_y, gsave_z, glocal, slocal,
    szb, ssend, syb, qsend, qb, s5b, s7b, zsend, gsend_t, gsend_z, gb,
    rs_s2, rs_r2, rs_s1, rs_s3, rs_r1, rs_r3, q_s2, q_r2, q_s1, q_s3, q_r1, q_r3,
    gp, gp_z, gp_y, mats_loc, mats_z, mats_y,
    send_sem, recv_sem, w_sem, l_sem,
):
    tokens = hid.shape[0]
    half = tokens // 2
    me = lax.axis_index("tensor")
    y, z = me // SIDE, lax.rem(me, SIDE)
    upper, lower = pl.ds(0, half), pl.ds(half, half)
    pending = []

    def at(dy, dz):
        return wrap(y + dy, SIDE) * SIDE + wrap(z + dz, SIDE)

    def copy(src, dst, index, dev, slot=None):
        return pltpu.make_async_remote_copy(
            src_ref=src,
            dst_ref=dst,
            send_sem=send_sem.at[index],
            recv_sem=recv_sem.at[index if slot is None else slot],
            device_id={"tensor": dev},
            device_id_type=MESH,
        )

    def send(src, dst, index, dev):
        c = copy(src, dst, index, dev)
        c.start()
        pending.append(c)
        return c

    def w_rows(dy, dz):
        block = at(dy, dz)
        return w_v[pl.ds(pl.multiple_of(block * 512, 512), 512), :]

    w_copy = pltpu.make_async_copy(wt, w_v, w_sem)
    w_copy.start()

    barrier = pltpu.get_barrier_semaphore()
    for d in range(1, 16):
        pl.semaphore_signal(
            barrier, inc=1, device_id={"tensor": lax.rem(me + d, 16)}, device_id_type=MESH
        )
    pl.semaphore_wait(barrier, 15)

    cot_in, genz_in, geny_in = [], [], []
    for d in range(1, 4):
        chunk = lax.rem(y + d + z, SIDE)
        cols = pl.ds(pl.multiple_of(chunk * LANES, LANES), LANES)
        cot_in.append(send(cot.at[:, cols], gyb.at[y], COT_Y + d, at(d, 0)))
        geny_in.append(send(gen.at[pl.ds(6, 2), :, cols], gy.at[y], GEN_Y + d, at(d, 0)))
    own_cols_y = pl.ds(pl.multiple_of(lax.rem(y + z, SIDE) * LANES, LANES), LANES)
    own_cols_z = pl.ds(pl.multiple_of(z * LANES, LANES), LANES)
    for d in range(1, 4):
        cols = pl.ds(pl.multiple_of(wrap(z + d, SIDE) * LANES, LANES), LANES)
        genz_in.append(send(gen.at[pl.ds(4, 2), :, cols], gz.at[z], GEN_Z + d, at(0, d)))

    ag_z = [
        send(hid, hbuf.at[0, 1], AG_Z + 0, at(0, 1)),
        send(hid, hbuf.at[0, 3], AG_Z + 1, at(0, 3)),
    ]
    ag_y = {}

    def ag_spread(dz):
        src = hid if dz == 0 else hbuf.at[0, dz]
        ag_y[dz] = [
            send(src, hbuf.at[1, dz], AG_Y[dz] + 0, at(1, 0)),
            send(src, hbuf.at[3, dz], AG_Y[dz] + 1, at(3, 0)),
        ]

    def ag_forward(dz):
        ag_y[dz][0].wait_recv()
        ag_y[dz].append(
            send(hbuf.at[1, dz, upper], hbuf.at[2, dz, upper], AG_Y[dz] + 2, at(1, 0))
        )
        ag_y[dz][1].wait_recv()
        ag_y[dz].append(
            send(hbuf.at[3, dz, lower], hbuf.at[2, dz, lower], AG_Y[dz] + 3, at(3, 0))
        )

    def accumulate(dy, dz):
        base[...] += dot(hbuf[dy, dz], w_rows(-dy, -dz))

    ag_spread(0)

    gyb[y] = cot[:, own_cols_y]
    gy[y] = gen[6:8, :, own_cols_y]
    gz[z] = gen[4:6, :, own_cols_z]

    for k in range(3):
        for s in range(2):
            mats_loc[k, s] = near_matrix(gen[k, :, 256 * s : 256 * s + 256], k)
    for s in range(2):
        for h in range(2):
            mats_loc[3 + h, s] = diag_matrix(
                gen[3, HALF * h : HALF * h + HALF, 256 * s : 256 * s + 256]
            )

    PAIRS = (((0, 1), (2, 3)), ((0, 2), (1, 3)))

    def pair_of(ref, a, b):
        return jnp.concatenate([ref[a], ref[b]], axis=1)

    for c in geny_in:
        c.wait_recv()
    for k in range(2):
        for i, (a, b) in enumerate(PAIRS[k]):
            mats_y[k, i] = pair_matrix(gy[a, k], gy[b, k])

    for c in cot_in:
        c.wait_recv()

    def pairs_backward(values, mats, save, out):
        for k in (1, 0):
            new = [None] * 4
            for i, (a, b) in enumerate(PAIRS[k]):
                v = jnp.concatenate([values[a], values[b]], axis=1)
                v = v + dot_nt(v.astype(BF16), mats[k, i])
                new[a], new[b] = v[:, :LANES], v[:, LANES:]
            values = new
            target = save if k == 1 else out
            for m in range(4):
                target[m] = values[m].astype(BF16)

    def pairs_forward(values, mats, save, out):
        for k in (0, 1):
            new = [None] * 4
            for i, (a, b) in enumerate(PAIRS[k]):
                v = jnp.concatenate([values[a], values[b]], axis=1)
                v = v + dot(v.astype(BF16), mats[k, i])
                new[a], new[b] = v[:, :LANES], v[:, LANES:]
            values = new
            target = save if k == 0 else out
            for m in range(4):
                target[m] = values[m].astype(BF16)

    def cross(src, dst, first, own_slot, dev_of, src_of):
        sent = []
        for d in range(4):
            c = copy(src.at[src_of(d)], dst.at[own_slot], first + d, dev_of(d), first + own_slot)
            if d == 0:
                keep = pltpu.make_async_copy(
                    src.at[src_of(0)], dst.at[own_slot], recv_sem.at[first + own_slot]
                )
                remote, local = dev_of(0) != me, dev_of(0) == me
                pl.when(remote)(lambda c=c: c.start())
                pl.when(local)(lambda keep=keep: keep.start())
            else:
                c.start()
            sent.append(c)

        def arrive():
            for m in range(4):
                pltpu.make_async_copy(src.at[m], dst.at[m], recv_sem.at[first + m]).wait()

        def finish():
            pl.when(dev_of(0) != me)(lambda: sent[0].wait_send())
            for c in sent[1:]:
                c.wait_send()

        return arrive, finish

    pairs_backward([gyb[m].astype(F32) for m in range(4)], mats_y, gsave_y, gsend_t)
    z_of = lax.rem(y + z, SIDE)
    bwd_arrive, bwd_finish = cross(
        gsend_t, gzb, BWD_T, z,
        lambda d: wrap(y + d, SIDE) * SIDE + z_of,
        lambda d: wrap(y + d, SIDE),
    )

    w_copy.wait()
    base[...] = dot(hid[...], w_rows(0, 0))
    ag_forward(0)
    accumulate(1, 0)
    accumulate(3, 0)

    for c in genz_in:
        c.wait_recv()
    for k in range(2):
        for i, (a, b) in enumerate(PAIRS[k]):
            mats_z[k, i] = pair_matrix(gz[a, k], gz[b, k])

    ag_z[0].wait_recv()
    ag_z.append(send(hbuf.at[0, 1, upper], hbuf.at[0, 2, upper], AG_Z + 2, at(0, 1)))
    ag_spread(1)
    ag_z[1].wait_recv()
    ag_z.append(send(hbuf.at[0, 3, lower], hbuf.at[0, 2, lower], AG_Z + 3, at(0, 3)))
    ag_spread(3)
    accumulate(0, 1)
    accumulate(0, 3)

    bwd_arrive()
    pairs_backward([gzb[m].astype(F32) for m in range(4)], mats_z, gsave_z, gsend_z)
    back_in = []
    for d in range(1, 4):
        back_in.append(
            send(gsend_z.at[wrap(z + d, SIDE)], ghome.at[z], BWD_Z + d, at(0, d))
        )
    ghome[z] = gsend_z[z]

    for c in ag_y[0][2:]:
        c.wait_recv()
    accumulate(2, 0)
    ag_z[2].wait_recv()
    ag_z[3].wait_recv()
    ag_spread(2)
    accumulate(0, 2)
    ag_forward(1)
    accumulate(1, 1)
    accumulate(3, 1)

    for c in back_in:
        c.wait_recv()
    ga = jnp.concatenate([ghome[0], ghome[1]], axis=1)
    gbb = jnp.concatenate([ghome[2], ghome[3]], axis=1)
    glocal[3, 0] = ga
    glocal[3, 1] = gbb
    fa = ga.astype(F32) + dot_nt(ga, mats_loc[3, 0]) + dot_nt(gbb, mats_loc[3, 1])
    fb = gbb.astype(F32) + dot_nt(ga, mats_loc[4, 0]) + dot_nt(gbb, mats_loc[4, 1])
    for k in (2, 1, 0):
        glocal[k, 0] = fa.astype(BF16)
        glocal[k, 1] = fb.astype(BF16)
        fa = fa + dot_nt(glocal[k, 0], mats_loc[k, 0])
        fb = fb + dot_nt(glocal[k, 1], mats_loc[k, 1])
    gb[:, :256] = fa.astype(BF16)
    gb[:, 256:] = fb.astype(BF16)

    ag_forward(3)
    accumulate(1, 3)
    accumulate(3, 3)
    ag_forward(2)
    accumulate(1, 2)
    accumulate(3, 2)

    def part(dy, dz):
        return dot_nt(gb[...], w_rows(dy, dz))

    rs = {}
    ORDER = (2, 1, 3, 0)

    def rs_far(dz):
        rs_s2[dz] = part(2, dz).astype(BF16)
        rs[dz] = [
            send(rs_s2.at[dz, upper], rs_r2.at[dz, 0], RS_Y[dz] + 0, at(1, 0)),
            send(rs_s2.at[dz, lower], rs_r2.at[dz, 1], RS_Y[dz] + 1, at(3, 0)),
        ]

    def rs_near(dz):
        p = part(1, dz)
        rs[dz][0].wait_recv()
        rs_s1[dz, upper] = (p[:half] + rs_r2[dz, 0].astype(F32)).astype(BF16)
        rs_s1[dz, lower] = p[half:].astype(BF16)
        rs[dz].append(send(rs_s1.at[dz], rs_r1.at[dz], RS_Y[dz] + 2, at(1, 0)))
        p = part(3, dz)
        rs[dz][1].wait_recv()
        rs_s3[dz, upper] = p[:half].astype(BF16)
        rs_s3[dz, lower] = (p[half:] + rs_r2[dz, 1].astype(F32)).astype(BF16)
        rs[dz].append(send(rs_s3.at[dz], rs_r3.at[dz], RS_Y[dz] + 3, at(3, 0)))

    def rs_sum(dz):
        p = part(0, dz)
        rs[dz][2].wait_recv()
        rs[dz][3].wait_recv()
        return p + rs_r1[dz].astype(F32) + rs_r3[dz].astype(F32)

    for dz in ORDER:
        rs_far(dz)

    for dz in (1, 3, 2):
        for c in ag_y[dz][2:]:
            c.wait_recv()
        accumulate(2, dz)
    fa, fb = base[:, :256], base[:, 256:]
    for k in range(3):
        slocal[k, 0] = fa.astype(BF16)
        slocal[k, 1] = fb.astype(BF16)
        fa = fa + dot(slocal[k, 0], mats_loc[k, 0])
        fb = fb + dot(slocal[k, 1], mats_loc[k, 1])
    ba, bb = fa.astype(BF16), fb.astype(BF16)
    slocal[3, 0] = ba
    slocal[3, 1] = bb
    fa = fa + dot(ba, mats_loc[3, 0]) + dot(bb, mats_loc[4, 0])
    fb = fb + dot(ba, mats_loc[3, 1]) + dot(bb, mats_loc[4, 1])
    for c in range(4):
        side = fa if c < 2 else fb
        ssend[c] = side[:, (c % 2) * LANES : (c % 2) * LANES + LANES].astype(BF16)
    fwd_in = []
    for d in range(1, 4):
        fwd_in.append(send(ssend.at[wrap(z + d, SIDE)], szb.at[z], FWD_Z + d, at(0, d)))
    szb[z] = ssend[z]

    rs_near(2)
    rs_near(1)

    def put_local(k, s, value):
        for j in range(2):
            gp[(k // 2) * 4 + 2 * s + j, (k % 2) * 64 : (k % 2) * 64 + 64] = value[
                :, j * LANES : (j + 1) * LANES
            ]

    for k in range(3):
        for s in range(2):
            put_local(k, s, near_extract(dot_tn(slocal[k, s], glocal[k, s]), k))
    for s in range(2):
        put_local(
            3, s,
            jnp.concatenate(
                [diag_extract(dot_tn(slocal[3, h], glocal[3, s])) for h in range(2)], axis=0
            ),
        )

    for c in fwd_in:
        c.wait_recv()
    pairs_forward([szb[m].astype(F32) for m in range(4)], mats_z, s5b, zsend)
    fwd_arrive, fwd_finish = cross(
        zsend, syb, FWD_T, y,
        lambda d: ((SIDE - d) % SIDE) * SIDE + wrap(z + d, SIDE),
        lambda d: wrap(z + d, SIDE),
    )

    rs_near(3)
    rs_near(0)

    def pair_grads(states, grads, dst):
        for k in range(2):
            for i, (a, b) in enumerate(PAIRS[k]):
                value = pair_extract(dot_tn(pair_of(states[k], a, b), pair_of(grads[k], a, b)))
                dst[a, k * 64 : k * 64 + 64] = value[:, :LANES]
                dst[b, k * 64 : k * 64 + 64] = value[:, LANES:]

    pair_grads((szb, s5b), (gsave_z, gzb), gp_z)
    outz_in = []
    for d in range(1, 4):
        outz_in.append(send(gp_z.at[wrap(z + d, SIDE)], gp.at[8 + z], OUT_Z + d, at(0, d)))
    gp[8 + z] = gp_z[z]

    fwd_arrive()
    pairs_forward([syb[m].astype(F32) for m in range(4)], mats_y, s7b, qsend)
    query_in = []
    for d in range(1, 4):
        query_in.append(send(qsend.at[wrap(y + d, SIDE)], qb.at[z_of], FWD_Y + d, at(d, 0)))
    qb[z_of] = qsend[y]

    pair_grads((syb, s7b), (gsave_y, gyb), gp_y)
    outy_in = []
    for d in range(1, 4):
        outy_in.append(send(gp_y.at[wrap(y + d, SIDE)], gp.at[12 + z_of], OUT_Y + d, at(d, 0)))
    gp[12 + z_of] = gp_y[y]

    q_s2[...] = rs_sum(2).astype(BF16)
    rz = [
        send(q_s2.at[upper], q_r2.at[0], RS_Z + 0, at(0, 1)),
        send(q_s2.at[lower], q_r2.at[1], RS_Z + 1, at(0, 3)),
    ]
    q = rs_sum(1)
    rz[0].wait_recv()
    q_s1[upper] = (q[:half] + q_r2[0].astype(F32)).astype(BF16)
    q_s1[lower] = q[half:].astype(BF16)
    rz.append(send(q_s1, q_r1, RS_Z + 2, at(0, 1)))
    q = rs_sum(3)
    rz[1].wait_recv()
    q_s3[upper] = q[:half].astype(BF16)
    q_s3[lower] = (q[half:] + q_r2[1].astype(F32)).astype(BF16)
    rz.append(send(q_s3, q_r3, RS_Z + 3, at(0, 3)))
    q = rs_sum(0)

    for c in query_in + outz_in + outy_in:
        c.wait_recv()
    for c in range(4):
        query[:, c * LANES : (c + 1) * LANES] = qb[c]
    ggrad[...] = gp[...]
    rz[2].wait_recv()
    rz[3].wait_recv()
    igrad[...] = (q + q_r1[...].astype(F32) + q_r3[...].astype(F32)).astype(BF16)

    for c in pending:
        c.wait_send()
    bwd_finish()
    fwd_finish()


def main_call(hidden, weight, generators, cotangent):
    tokens = hidden.shape[0]
    half = tokens // 2
    vm = lambda *shape, dtype=BF16: pltpu.VMEM(shape, dtype)
    chunks = vm(4, tokens, LANES)
    block = vm(tokens, 512)
    blocks = vm(4, tokens, 512)
    flops = 4 * tokens * 8192 * 512
    return pl.pallas_call(
        main_kernel,
        out_shape=(
            jax.ShapeDtypeStruct((tokens, 512), BF16),
            jax.ShapeDtypeStruct((tokens, 512), BF16),
            jax.ShapeDtypeStruct((16, 128, 128), F32),
        ),
        in_specs=[
            pl.BlockSpec(memory_space=pltpu.VMEM),
            pl.BlockSpec(memory_space=pl.ANY),
            pl.BlockSpec(memory_space=pltpu.VMEM),
            pl.BlockSpec(memory_space=pltpu.VMEM),
        ],
        out_specs=[pl.BlockSpec(memory_space=pltpu.VMEM)] * 3,
        scratch_shapes=[
            vm(8192, 512),
            vm(4, 4, tokens, 512),
            vm(tokens, 512, dtype=F32),
            vm(4, 2, 64, LANES, dtype=F32),
            vm(4, 2, 64, LANES, dtype=F32),
            chunks, chunks, chunks, chunks, chunks,
            vm(4, 2, tokens, 256),
            vm(4, 2, tokens, 256),
            chunks, chunks, chunks, chunks, chunks,
            chunks, chunks, chunks, chunks, chunks,
            block,
            blocks, vm(4, 2, half, 512), blocks, blocks, blocks, blocks,
            block, vm(2, half, 512), block, block, block, block,
            vm(16, 128, 128, dtype=F32),
            vm(4, 128, 128, dtype=F32),
            vm(4, 128, 128, dtype=F32),
            vm(5, 2, 256, 256),
            vm(2, 2, 256, 256),
            vm(2, 2, 256, 256),
            pltpu.SemaphoreType.DMA((N_SEMS,)),
            pltpu.SemaphoreType.DMA((N_SEMS,)),
            pltpu.SemaphoreType.DMA,
            pltpu.SemaphoreType.DMA,
        ],
        compiler_params=pltpu.CompilerParams(
            collective_id=0, has_side_effects=True, vmem_limit_bytes=VMEM_BYTES
        ),
        cost_estimate=pl.CostEstimate(
            flops=flops, bytes_accessed=12 * 1024 * 1024, transcendentals=0
        ),
        name="adapt",
    )(hidden, weight, generators, cotangent)


def reduce_kernel(scale, n, parts, out, rbuf, sbuf, obuf, abuf, s1, r1, s2, r2):
    me = lax.axis_index("dp")
    barrier = pltpu.get_barrier_semaphore()
    for d in range(1, n):
        pl.semaphore_signal(
            barrier, inc=1, device_id={"dp": lax.rem(me + d, n)}, device_id_type=MESH
        )
    sbuf[...] = parts[...].astype(BF16)
    pl.semaphore_wait(barrier, n - 1)
    first = []
    for d in range(1, n):
        dev = lax.rem(me + d, n)
        c = pltpu.make_async_remote_copy(
            src_ref=sbuf.at[dev], dst_ref=rbuf.at[d], send_sem=s1.at[d], recv_sem=r1.at[d],
            device_id={"dp": dev}, device_id_type=MESH,
        )
        c.start()
        first.append(c)
    total = parts[me]
    for c, d in zip(first, range(1, n)):
        c.wait_recv()
        total = total + rbuf[d].astype(F32)
    obuf[...] = total * scale
    second = []
    for d in range(1, n):
        c = pltpu.make_async_remote_copy(
            src_ref=obuf, dst_ref=abuf.at[me], send_sem=s2.at[d], recv_sem=r2.at[d],
            device_id={"dp": lax.rem(me + d, n)}, device_id_type=MESH,
        )
        c.start()
        second.append(c)
    abuf[me] = obuf[...]
    for c in second:
        c.wait_recv()
    for pair in range(4):
        for c in range(4):
            for j in range(2):
                out[2 * pair + j, :, c * LANES : (c + 1) * LANES] = abuf[
                    pair * 4 + c, j * 64 : (j + 1) * 64
                ]
    for c in first + second:
        c.wait_send()


def reduce_call(parts, scale, n):
    return pl.pallas_call(
        functools.partial(reduce_kernel, scale, n),
        out_shape=jax.ShapeDtypeStruct((8, 64, 512), F32),
        in_specs=[pl.BlockSpec(memory_space=pltpu.VMEM)],
        out_specs=pl.BlockSpec(memory_space=pltpu.VMEM),
        scratch_shapes=[
            pltpu.VMEM((n, 128, 128), BF16),
            pltpu.VMEM((16, 128, 128), BF16),
            pltpu.VMEM((128, 128), F32),
            pltpu.VMEM((16, 128, 128), F32),
            pltpu.SemaphoreType.DMA((n,)),
            pltpu.SemaphoreType.DMA((n,)),
            pltpu.SemaphoreType.DMA((n,)),
            pltpu.SemaphoreType.DMA((n,)),
        ],
        compiler_params=pltpu.CompilerParams(
            collective_id=1, has_side_effects=True, vmem_limit_bytes=16 * 1024 * 1024
        ),
        name="dp_sum",
    )(parts)


def on_device(hidden, base_weight, generators, cotangent):
    n = lax.axis_size("dp")
    query, input_grad, parts = main_call(hidden, base_weight, generators, cotangent)
    scale = 1.0 / math.sqrt(hidden.shape[0] * n)
    return query, input_grad, reduce_call(parts, scale, n)


def solution(mesh):
    placed = (P("dp", "tensor"), P(None, "tensor"), P(None, None, "tensor"), P("dp", "tensor"))
    return jax.shard_map(
        on_device,
        mesh=mesh,
        in_specs=placed,
        out_specs=(P("dp", "tensor"), P("dp", "tensor"), P(None, None, "tensor")),
        check_vma=False,
    )
```

```python
import functools
import math

import jax
import jax.numpy as jnp
from jax import lax
from jax.experimental import pallas as pl
from jax.experimental.pallas import tpu as pltpu
from jax.sharding import PartitionSpec as P

MESH = pl.DeviceIdType.MESH
F32 = jnp.float32
BF16 = jnp.bfloat16
SIDE = 4
LANES = 128
HALF = 32
VMEM_BYTES = 60 * 1024 * 1024


def wrap(value, n):
    return lax.rem(value + n, n)


def dot(a, b):
    return jnp.dot(a, b, preferred_element_type=F32)


def dot_nt(a, b):
    return lax.dot_general(a, b, (((1,), (1,)), ((), ())), preferred_element_type=F32)


def dot_tn(a, b):
    return lax.dot_general(a, b, (((0,), (0,)), ((), ())), preferred_element_type=F32)


def split(value):
    high = value.astype(BF16)
    return high, (value - high.astype(F32)).astype(BF16)


def put_split(ref, index, value):
    ref[(*index, 0)], ref[(*index, 1)] = split(value)


def mix(product, value, ref, index):
    top, rest = ref[(*index, 0)], ref[(*index, 1)]
    if value.dtype == BF16:
        return product(value, top) + product(value, rest)
    high, low = split(value)
    return product(high, top) + product(low, top) + product(high, rest)


def groups_of(shape):
    rows = lax.broadcasted_iota(jnp.int32, shape, 0) >> 5
    cols = lax.broadcasted_iota(jnp.int32, shape, 1) >> 5
    return rows, cols


def spread(block, mask, copies):
    return jnp.where(mask, jnp.concatenate([block] * copies, axis=0), 0.0)


def pair_matrix(gen_a, gen_b):
    both = jnp.concatenate([gen_a, gen_b], axis=1)
    rows, cols = groups_of((LANES, 2 * LANES))
    mask = rows == (cols & 3)
    return jnp.concatenate([spread(both[:HALF], mask, 4), spread(both[HALF:], mask, 4)], axis=0)


def pair_extract(grad):
    cols = (lax.broadcasted_iota(jnp.int32, (HALF, 2 * LANES), 1) >> 5) & 3
    parts = []
    for h in range(2):
        total = jnp.zeros((HALF, 2 * LANES), F32)
        for g in range(4):
            start = h * LANES + g * HALF
            total = total + jnp.where(cols == g, grad[start : start + HALF], 0.0)
        parts.append(total)
    return jnp.concatenate(parts, axis=0)


def near_matrix(gen, k):
    rows, cols = groups_of((256, 256))
    low = cols & ~(1 << k)
    return spread(gen[:HALF], rows == low, 8) + spread(gen[HALF:], rows == (low | (1 << k)), 8)


def near_extract(grad, k):
    cols = lax.broadcasted_iota(jnp.int32, (HALF, 256), 1) >> 5
    low = cols & ~(1 << k)
    parts = []
    for want in (low, low | (1 << k)):
        total = jnp.zeros((HALF, 256), F32)
        for g in range(8):
            total = total + jnp.where(want == g, grad[g * HALF : (g + 1) * HALF], 0.0)
        parts.append(total)
    return jnp.concatenate(parts, axis=0)


def diag_matrix(block):
    rows, cols = groups_of((256, 256))
    return spread(block, rows == cols, 8)


def diag_extract(grad):
    cols = lax.broadcasted_iota(jnp.int32, (HALF, 256), 1) >> 5
    total = jnp.zeros((HALF, 256), F32)
    for g in range(8):
        total = total + jnp.where(cols == g, grad[g * HALF : (g + 1) * HALF], 0.0)
    return total


PAIRS = (((0, 1), (2, 3)), ((0, 2), (1, 3)))
N_SEMS = 224
SPLIT_GATHER = 320
SPLIT_SUM = 320
STOP = None


class Stop(Exception):
    pass


class Sent:
    def __init__(self, copy):
        self.copy, self.received = copy, False

    def arrive(self):
        if not self.received:
            self.copy.wait_recv()
            self.received = True


def main_kernel(n_dp, scale, *refs):
    pending, endings = [], []
    try:
        main_body(n_dp, scale, pending, endings, *refs)
    except Stop:
        pass
    for c in pending:
        c.arrive()
        c.copy.wait_send()
    for end in endings:
        end()


def main_body(
    n_dp, scale, pending, endings,
    hid, wt, gen, cot, query, igrad, ggrad,
    w_v, hbuf, base, pb, gz, gy, gyb, gzb, ghome, gsave_y, gsave_z, glocal, slocal,
    szb, ssend, syb, qsend, qb, s5b, s7b, zsend, gsend_t, gsend_z, gb,
    rs_s2, rs_r2, rs_s1, rs_s3, rs_r1, rs_r3, q_s2, q_r2, q_s1, q_s3, q_r1, q_r3,
    gp, gp_z, gp_y, gpb, sums_a, sums_b, slab_a, slab_b, gout, mats_loc, mats_z, mats_y,
    send_sem, recv_sem, w_sem,
):
    tokens = hid.shape[0]
    me = lax.axis_index("tensor")
    my_dp = lax.axis_index("dp")
    y, z = me // SIDE, lax.rem(me, SIDE)
    z_of = lax.rem(y + z, SIDE)
    counter = [0]

    def mark(name):
        if STOP == name:
            raise Stop

    def at(dy, dz):
        return wrap(y + dy, SIDE) * SIDE + wrap(z + dz, SIDE)

    def toward(axis, step):
        return at(step, 0) if axis == "y" else at(0, step)

    def place(axis, step, fixed):
        return (step, fixed) if axis == "y" else (fixed, step)

    def ids(n=1):
        first = counter[0]
        counter[0] += n
        return first

    def copy(src, dst, send_index, recv_index, device):
        return pltpu.make_async_remote_copy(
            src_ref=src,
            dst_ref=dst,
            send_sem=send_sem.at[send_index],
            recv_sem=recv_sem.at[recv_index],
            device_id=device,
            device_id_type=MESH,
        )

    def send(src, dst, dev, axis="tensor"):
        index = ids()
        c = copy(src, dst, index, index, {axis: dev})
        c.start()
        c = Sent(c)
        pending.append(c)
        return c

    def w_rows(dy, dz):
        return w_v[pl.ds(pl.multiple_of(at(dy, dz) * 512, 512), 512), :]

    def chunk_at(index):
        return pl.ds(pl.multiple_of(index * LANES, LANES), LANES)

    w_copy = pltpu.make_async_copy(wt, w_v, w_sem)
    w_copy.start()

    barrier = pltpu.get_barrier_semaphore()
    for d in range(1, 16):
        pl.semaphore_signal(
            barrier, inc=1, device_id={"tensor": lax.rem(me + d, 16)}, device_id_type=MESH
        )
    for d in range(1, n_dp):
        pl.semaphore_signal(
            barrier, inc=1, device_id={"dp": lax.rem(my_dp + d, n_dp)}, device_id_type=MESH
        )
    pl.semaphore_wait(barrier, 15 + n_dp - 1)

    cot_in, genz_in, geny_in = [], [], []
    for d in range(1, 4):
        cols = chunk_at(lax.rem(y + d + z, SIDE))
        cot_in.append(send(cot.at[:, cols], gyb.at[y], at(d, 0)))
        geny_in.append(send(gen.at[pl.ds(6, 2), :, cols], gy.at[y], at(d, 0)))

    def held(dy, dz, lo, hi):
        ref = hid if (dy, dz) == (0, 0) else hbuf.at[dy, dz]
        return ref.at[pl.ds(lo, hi - lo)]

    arrivals = {(dy, dz): [] for dy in range(4) for dz in range(4)}

    def hop(axis, fixed, step, sign, lo, hi):
        target = place(axis, step + sign & 3, fixed)
        c = send(
            held(*place(axis, step, fixed), lo, hi),
            hbuf.at[(*target, pl.ds(lo, hi - lo))],
            toward(axis, sign),
        )
        arrivals[target].append(c)
        return c

    def ring_start(axis, fixed, lo, hi):
        return [hop(axis, fixed, 0, 1, lo, hi), hop(axis, fixed, 0, -1, lo, hi)]

    def ring_forward(axis, fixed, lo, hi, copies):
        middle = (lo + hi) // 2
        copies[0].arrive()
        copies.append(hop(axis, fixed, 1, 1, lo, middle))
        copies[1].arrive()
        copies.append(hop(axis, fixed, 3, -1, middle, hi))

    cut = SPLIT_GATHER * tokens // 384 // 32 * 32
    routes = [("z", "y", 0, cut)]
    if cut < tokens:
        routes.append(("y", "z", cut, tokens))
    first = [ring_start(a, 0, lo, hi) for a, _, lo, hi in routes]
    second = [{0: ring_start(b, 0, lo, hi)} for _, b, lo, hi in routes]
    for d in range(1, 4):
        cols = chunk_at(wrap(z + d, SIDE))
        genz_in.append(send(gen.at[pl.ds(4, 2), :, cols], gz.at[z], at(0, d)))

    def gather_second(step):
        for (_, b, lo, hi), copies in zip(routes, second):
            ring_forward(b, step, lo, hi, copies[step])

    def gather_first():
        for (a, b, lo, hi), ring, copies in zip(routes, first, second):
            middle = (lo + hi) // 2
            ring[0].arrive()
            ring.append(hop(a, 0, 1, 1, lo, middle))
            copies[1] = ring_start(b, 1, lo, hi)
            ring[1].arrive()
            ring.append(hop(a, 0, 3, -1, middle, hi))
            copies[3] = ring_start(b, 3, lo, hi)

    def gather_far():
        for (_, b, lo, hi), ring, copies in zip(routes, first, second):
            ring[2].arrive()
            ring[3].arrive()
            copies[2] = ring_start(b, 2, lo, hi)

    def accumulate(*blocks):
        for dy, dz in blocks:
            for c in arrivals[dy, dz]:
                c.arrive()
            base[...] += dot(hbuf[dy, dz], w_rows(-dy, -dz))

    gyb[y] = cot[:, chunk_at(z_of)]
    gy[y] = gen[6:8, :, chunk_at(z_of)]
    gz[z] = gen[4:6, :, chunk_at(z)]

    for k in range(3):
        for s in range(2):
            put_split(mats_loc, (k, s), near_matrix(gen[k, :, 256 * s : 256 * s + 256], k))
    for s in range(2):
        for h in range(2):
            block = gen[3, HALF * h : HALF * h + HALF, 256 * s : 256 * s + 256]
            put_split(mats_loc, (3 + h, s), diag_matrix(block))

    def pair_of(ref, a, b):
        return jnp.concatenate([ref[a], ref[b]], axis=1)

    def fill_pairs(mats, gens):
        for k in range(2):
            for i, (a, b) in enumerate(PAIRS[k]):
                put_split(mats, (k, i), pair_matrix(gens[a, k], gens[b, k]))

    def pairs_apply(product, order, source, mats, save, out):
        values = None
        for k, target in zip(order, (save, out)):
            new = [None] * 4
            for i, (a, b) in enumerate(PAIRS[k]):
                if values is None:
                    v = pair_of(source, a, b)
                else:
                    v = jnp.concatenate([values[a], values[b]], axis=1)
                v = v.astype(F32) + mix(product, v, mats, (k, i))
                new[a], new[b] = v[:, :LANES], v[:, LANES:]
            values = new
            for m in range(4):
                target[m] = values[m].astype(BF16)

    def cross(src, dst, own_slot, dev_of, src_of):
        index = ids(4)
        sent = []
        for d in range(4):
            c = copy(
                src.at[src_of(d)], dst.at[own_slot], index + d, index + own_slot,
                {"tensor": dev_of(d)},
            )
            if d == 0:
                keep = pltpu.make_async_copy(
                    src.at[src_of(0)], dst.at[own_slot], recv_sem.at[index + own_slot]
                )
                pl.when(dev_of(0) != me)(lambda c=c: c.start())
                pl.when(dev_of(0) == me)(lambda keep=keep: keep.start())
            else:
                c.start()
            sent.append(c)
        done = []

        def arrive():
            if not done:
                done.append(True)
                for m in range(4):
                    pltpu.make_async_copy(src.at[m], dst.at[m], recv_sem.at[index + m]).wait()

        def finish():
            arrive()
            pl.when(dev_of(0) != me)(lambda: sent[0].wait_send())
            for c in sent[1:]:
                c.wait_send()

        endings.append(finish)
        return arrive

    for c in geny_in:
        c.arrive()
    fill_pairs(mats_y, gy)
    for c in cot_in:
        c.arrive()
    pairs_apply(dot_nt, (1, 0), gyb, mats_y, gsave_y, gsend_t)
    bwd_arrive = cross(
        gsend_t, gzb, z,
        lambda d: wrap(y + d, SIDE) * SIDE + z_of,
        lambda d: wrap(y + d, SIDE),
    )
    mark("bwd_y")

    w_copy.wait()
    base[...] = dot(hid[...], w_rows(0, 0))
    gather_second(0)
    for c in genz_in:
        c.arrive()
    fill_pairs(mats_z, gz)
    mark("ag0")

    gather_first()
    accumulate((1, 0), (3, 0), (0, 1), (0, 3))
    mark("ag1")

    bwd_arrive()
    pairs_apply(dot_nt, (1, 0), gzb, mats_z, gsave_z, gsend_z)
    back_in = []
    for d in range(1, 4):
        back_in.append(send(gsend_z.at[wrap(z + d, SIDE)], ghome.at[z], at(0, d)))
    ghome[z] = gsend_z[z]
    mark("bwd_z")

    gather_far()
    accumulate((2, 0), (0, 2))
    gather_second(1)
    accumulate((1, 1), (3, 1))
    mark("ag2")

    for c in back_in:
        c.arrive()
    ga = pair_of(ghome, 0, 1)
    gc = pair_of(ghome, 2, 3)
    glocal[3, 0], glocal[3, 1] = ga, gc
    fa = ga.astype(F32) + mix(dot_nt, ga, mats_loc, (3, 0)) + mix(dot_nt, gc, mats_loc, (3, 1))
    fb = gc.astype(F32) + mix(dot_nt, ga, mats_loc, (4, 0)) + mix(dot_nt, gc, mats_loc, (4, 1))
    for k in (2, 1, 0):
        glocal[k, 0], glocal[k, 1] = fa.astype(BF16), fb.astype(BF16)
        fa = fa + mix(dot_nt, fa, mats_loc, (k, 0))
        fb = fb + mix(dot_nt, fb, mats_loc, (k, 1))
    gb[:, :256] = fa.astype(BF16)
    gb[:, 256:] = fb.astype(BF16)
    mark("bwd_local")

    gather_second(3)
    accumulate((1, 3), (3, 3))
    gather_second(2)
    accumulate((1, 2), (3, 2))
    mark("ag3")

    computed = set()

    def partial(dy, dz, lo, hi):
        if (dy, dz) not in computed:
            computed.add((dy, dz))
            pb[dy, dz] = dot_nt(gb[...], w_rows(dy, dz))
        return pb[dy, dz, lo:hi]

    class Sum:
        def __init__(self, a, b, lo, hi):
            self.a, self.b, self.lo, self.hi, self.middle = a, b, lo, hi, (lo + hi) // 2
            self.copies, self.last = {}, []
            self.rows = pl.ds(lo, hi - lo)
            self.top, self.low = pl.ds(lo, self.middle - lo), pl.ds(self.middle, hi - self.middle)

        def far(self, fixed):
            block = partial(*place(self.a, 2, fixed), self.lo, self.hi)
            rs_s2[fixed, self.rows] = block.astype(BF16)
            self.copies[fixed] = [
                send(rs_s2.at[fixed, self.top], rs_r2.at[fixed, self.top], toward(self.a, 1)),
                send(rs_s2.at[fixed, self.low], rs_r2.at[fixed, self.low], toward(self.a, -1)),
            ]

        def near(self, fixed):
            cs, size = self.copies[fixed], self.middle - self.lo
            p = partial(*place(self.a, 1, fixed), self.lo, self.hi)
            cs[0].arrive()
            rs_s1[fixed, self.top] = (p[:size] + rs_r2[fixed, self.top].astype(F32)).astype(BF16)
            rs_s1[fixed, self.low] = p[size:].astype(BF16)
            cs.append(
                send(rs_s1.at[fixed, self.rows], rs_r1.at[fixed, self.rows], toward(self.a, 1))
            )
            p = partial(*place(self.a, 3, fixed), self.lo, self.hi)
            cs[1].arrive()
            rs_s3[fixed, self.top] = p[:size].astype(BF16)
            rs_s3[fixed, self.low] = (p[size:] + rs_r2[fixed, self.low].astype(F32)).astype(BF16)
            cs.append(
                send(rs_s3.at[fixed, self.rows], rs_r3.at[fixed, self.rows], toward(self.a, -1))
            )

        def whole(self, fixed):
            p = partial(*place(self.a, 0, fixed), self.lo, self.hi)
            for c in self.copies[fixed][2:]:
                c.arrive()
            return p + rs_r1[fixed, self.rows].astype(F32) + rs_r3[fixed, self.rows].astype(F32)

        def last_far(self):
            q_s2[self.rows] = self.whole(2).astype(BF16)
            self.last = [
                send(q_s2.at[self.top], q_r2.at[self.top], toward(self.b, 1)),
                send(q_s2.at[self.low], q_r2.at[self.low], toward(self.b, -1)),
            ]

        def last_near(self):
            size = self.middle - self.lo
            q = self.whole(1)
            self.last[0].arrive()
            q_s1[self.top] = (q[:size] + q_r2[self.top].astype(F32)).astype(BF16)
            q_s1[self.low] = q[size:].astype(BF16)
            self.last.append(send(q_s1.at[self.rows], q_r1.at[self.rows], toward(self.b, 1)))
            q = self.whole(3)
            self.last[1].arrive()
            q_s3[self.top] = q[:size].astype(BF16)
            q_s3[self.low] = (q[size:] + q_r2[self.low].astype(F32)).astype(BF16)
            self.last.append(send(q_s3.at[self.rows], q_r3.at[self.rows], toward(self.b, -1)))

        def end(self):
            q = self.whole(0)
            for c in self.last[2:]:
                c.arrive()
            q = q + q_r1[self.rows].astype(F32) + q_r3[self.rows].astype(F32)
            igrad[self.rows] = q.astype(BF16)

    cut = SPLIT_SUM * tokens // 384 // 32 * 32
    sums = [Sum("y", "z", 0, cut)]
    if cut < tokens:
        sums.append(Sum("z", "y", cut, tokens))
    for fixed in (2, 1, 3, 0):
        for s in sums:
            s.far(fixed)
    mark("rs_far")

    accumulate((2, 1), (2, 3), (2, 2))
    mark("base")
    fa, fb = base[:, :256], base[:, 256:]
    for k in range(3):
        slocal[k, 0], slocal[k, 1] = fa.astype(BF16), fb.astype(BF16)
        fa = fa + mix(dot, fa, mats_loc, (k, 0))
        fb = fb + mix(dot, fb, mats_loc, (k, 1))
    slocal[3, 0], slocal[3, 1] = fa.astype(BF16), fb.astype(BF16)
    fc = fa + mix(dot, fa, mats_loc, (3, 0)) + mix(dot, fb, mats_loc, (4, 0))
    fd = fb + mix(dot, fa, mats_loc, (3, 1)) + mix(dot, fb, mats_loc, (4, 1))
    for c in range(4):
        side = fc if c < 2 else fd
        ssend[c] = side[:, (c % 2) * LANES : (c % 2) * LANES + LANES].astype(BF16)
    fwd_in = []
    for d in range(1, 4):
        fwd_in.append(send(ssend.at[wrap(z + d, SIDE)], szb.at[z], at(0, d)))
    szb[z] = ssend[z]
    mark("fwd_local")

    for fixed in (2, 1):
        for s in sums:
            s.near(fixed)
    mark("near1")

    def put_local(k, s, value):
        for j in range(2):
            gp[pl.ds(((k // 2) * 4 + 2 * s + j) * 128 + (k % 2) * 64, 64)] = value[
                :, j * LANES : (j + 1) * LANES
            ]

    for k in range(3):
        for s in range(2):
            put_local(k, s, near_extract(dot_tn(slocal[k, s], glocal[k, s]), k))
    for s in range(2):
        put_local(
            3, s,
            jnp.concatenate(
                [diag_extract(dot_tn(slocal[3, h], glocal[3, s])) for h in range(2)], axis=0
            ),
        )

    for c in fwd_in:
        c.arrive()
    pairs_apply(dot, (0, 1), szb, mats_z, s5b, zsend)
    fwd_arrive = cross(
        zsend, syb, y,
        lambda d: ((SIDE - d) % SIDE) * SIDE + wrap(z + d, SIDE),
        lambda d: wrap(z + d, SIDE),
    )
    mark("fwd_z")

    def pair_grads(states, grads, dst):
        for k in range(2):
            for i, (a, b) in enumerate(PAIRS[k]):
                value = pair_extract(dot_tn(pair_of(states[k], a, b), pair_of(grads[k], a, b)))
                dst[a, k * 64 : k * 64 + 64] = value[:, :LANES]
                dst[b, k * 64 : k * 64 + 64] = value[:, LANES:]

    def piece(index):
        return pl.ds(pl.multiple_of(index * 128, 128), 128)

    pair_grads((szb, s5b), (gsave_z, gzb), gp_z)
    outz_in = []
    for d in range(1, 4):
        outz_in.append(send(gp_z.at[wrap(z + d, SIDE)], gp.at[piece(8 + z)], at(0, d)))
    gp[piece(8 + z)] = gp_z[z]

    for fixed in (3, 0):
        for s in sums:
            s.near(fixed)
    mark("near2")

    fwd_arrive()
    pairs_apply(dot, (0, 1), syb, mats_y, s7b, qsend)
    query_in = []
    for d in range(1, 4):
        query_in.append(send(qsend.at[wrap(y + d, SIDE)], qb.at[z_of], at(d, 0)))
    qb[z_of] = qsend[y]
    mark("fwd_y")

    pair_grads((syb, s7b), (gsave_y, gyb), gp_y)
    outy_in = []
    for d in range(1, 4):
        outy_in.append(send(gp_y.at[wrap(y + d, SIDE)], gp.at[piece(12 + z_of)], at(d, 0)))
    gp[piece(12 + z_of)] = gp_y[y]
    mark("grads")

    class Slabs:
        def __init__(self, start, size, sums_ref, slab_ref):
            self.start, self.size = start, size
            self.sums_ref, self.slab_ref = sums_ref, slab_ref
            self.ins, self.outs = [], []

        def rows(self, dev):
            return pl.ds(pl.multiple_of(self.start + dev * self.size, 32), self.size)

        def scatter(self):
            all_rows = pl.ds(self.start, 16 * self.size)
            gpb[all_rows] = gp[all_rows].astype(BF16)
            for d in range(1, n_dp):
                dev = lax.rem(my_dp + d, n_dp)
                self.ins.append(send(gpb.at[self.rows(dev)], self.sums_ref.at[d], dev, "dp"))

        def gather(self):
            total = gp[self.rows(my_dp)]
            for d, c in zip(range(1, n_dp), self.ins):
                c.arrive()
                total = total + self.sums_ref[d].astype(F32)
            self.slab_ref[...] = total * scale
            for d in range(1, n_dp):
                dev = lax.rem(my_dp + d, n_dp)
                self.outs.append(send(self.slab_ref, gout.at[self.rows(my_dp)], dev, "dp"))
            gout[self.rows(my_dp)] = self.slab_ref[...]

        def finish(self):
            for c in self.outs:
                c.arrive()

    early, late = Slabs(0, 96, sums_a, slab_a), Slabs(1536, 32, sums_b, slab_b)
    for c in outz_in:
        c.arrive()
    if n_dp > 1:
        early.scatter()

    for s in sums:
        s.last_far()
    mark("last_far")
    for c in outy_in:
        c.arrive()
    if n_dp > 1:
        late.scatter()
        early.gather()
    for s in sums:
        s.last_near()
    mark("last_near")
    if n_dp > 1:
        late.gather()

    for c in query_in:
        c.arrive()
    for c in range(4):
        query[:, c * LANES : (c + 1) * LANES] = qb[c]
    mark("query")
    for s in sums:
        s.end()
    mark("igrad")
    if n_dp > 1:
        early.finish()
        late.finish()
    final = gout if n_dp > 1 else gp
    for pair in range(4):
        for c in range(4):
            for j in range(2):
                ggrad[2 * pair + j, :, c * LANES : (c + 1) * LANES] = final[
                    pl.ds((pair * 4 + c) * 128 + j * 64, 64)
                ]


def main_call(hidden, weight, generators, cotangent, n_dp=1, scale=1.0):
    tokens = hidden.shape[0]
    vm = lambda *shape, dtype=BF16: pltpu.VMEM(shape, dtype)
    chunks = vm(4, tokens, LANES)
    block = vm(tokens, 512)
    blocks = vm(4, tokens, 512)
    flops = 4 * tokens * 8192 * 512
    return pl.pallas_call(
        functools.partial(main_kernel, n_dp, scale),
        out_shape=(
            jax.ShapeDtypeStruct((tokens, 512), BF16),
            jax.ShapeDtypeStruct((tokens, 512), BF16),
            jax.ShapeDtypeStruct((8, 64, 512), F32),
        ),
        in_specs=[
            pl.BlockSpec(memory_space=pltpu.VMEM),
            pl.BlockSpec(memory_space=pl.ANY),
            pl.BlockSpec(memory_space=pltpu.VMEM),
            pl.BlockSpec(memory_space=pltpu.VMEM),
        ],
        out_specs=[pl.BlockSpec(memory_space=pltpu.VMEM)] * 3,
        scratch_shapes=[
            vm(8192, 512),
            vm(4, 4, tokens, 512),
            vm(tokens, 512, dtype=F32),
            vm(4, 4, tokens, 512, dtype=F32),
            vm(4, 2, 64, LANES, dtype=F32),
            vm(4, 2, 64, LANES, dtype=F32),
            chunks, chunks, chunks, chunks, chunks,
            vm(4, 2, tokens, 256),
            vm(4, 2, tokens, 256),
            chunks, chunks, chunks, chunks, chunks,
            chunks, chunks, chunks, chunks, chunks,
            block,
            blocks, blocks, blocks, blocks, blocks, blocks,
            block, block, block, block, block, block,
            vm(2048, 128, dtype=F32),
            vm(4, 128, 128, dtype=F32),
            vm(4, 128, 128, dtype=F32),
            vm(2048, 128),
            vm(16, 96, 128),
            vm(16, 32, 128),
            vm(96, 128, dtype=F32),
            vm(32, 128, dtype=F32),
            vm(2048, 128, dtype=F32),
            vm(5, 2, 2, 256, 256),
            vm(2, 2, 2, 256, 256),
            vm(2, 2, 2, 256, 256),
            pltpu.SemaphoreType.DMA((N_SEMS,)),
            pltpu.SemaphoreType.DMA((N_SEMS,)),
            pltpu.SemaphoreType.DMA,
        ],
        compiler_params=pltpu.CompilerParams(
            collective_id=0, has_side_effects=True, vmem_limit_bytes=VMEM_BYTES
        ),
        cost_estimate=pl.CostEstimate(
            flops=flops, bytes_accessed=12 * 1024 * 1024, transcendentals=0
        ),
        name="adapt",
    )(hidden, weight, generators, cotangent)


def copy_kernel(*refs):
    count = len(refs) // 2
    sems = refs[-1]
    copies = [
        pltpu.make_async_copy(refs[i], refs[count + i], sems.at[i]) for i in range(count)
    ]
    for c in copies:
        c.start()
    for c in copies:
        c.wait()


def copy_call(*arrays):
    anywhere = pl.BlockSpec(memory_space=pl.ANY)
    return pl.pallas_call(
        copy_kernel,
        out_shape=tuple(jax.ShapeDtypeStruct(a.shape, a.dtype) for a in arrays),
        in_specs=[anywhere] * len(arrays),
        out_specs=[anywhere] * len(arrays),
        scratch_shapes=[pltpu.SemaphoreType.DMA((len(arrays),))],
        name="results",
    )(*arrays)


def on_device(hidden, base_weight, generators, cotangent):
    n = lax.axis_size("dp")
    scale = 1.0 / math.sqrt(hidden.shape[0] * n)
    return copy_call(*main_call(hidden, base_weight, generators, cotangent, n, scale))


def solution(mesh):
    placed = (P("dp", "tensor"), P(None, "tensor"), P(None, None, "tensor"), P("dp", "tensor"))
    return jax.shard_map(
        on_device,
        mesh=mesh,
        in_specs=placed,
        out_specs=(P("dp", "tensor"), P("dp", "tensor"), P(None, None, "tensor")),
        check_vma=False,
    )
```

```python
import functools
import math

import jax
import jax.numpy as jnp
from jax import lax
from jax.experimental import pallas as pl
from jax.experimental.pallas import tpu as pltpu
from jax.sharding import PartitionSpec as P

MESH = pl.DeviceIdType.MESH
F32 = jnp.float32
BF16 = jnp.bfloat16
SIDE = 4
LANES = 128
HALF = 32
VMEM_BYTES = 60 * 1024 * 1024


def wrap(value, n):
    return lax.rem(value + n, n)


def dot(a, b):
    return jnp.dot(a, b, preferred_element_type=F32)


def dot_nt(a, b):
    return lax.dot_general(a, b, (((1,), (1,)), ((), ())), preferred_element_type=F32)


def dot_tn(a, b):
    return lax.dot_general(a, b, (((0,), (0,)), ((), ())), preferred_element_type=F32)


def split(value):
    high = value.astype(BF16)
    return high, (value - high.astype(F32)).astype(BF16)


def put_split(ref, index, value):
    ref[(*index, 0)], ref[(*index, 1)] = split(value)


def mix(product, value, ref, index):
    top, rest = ref[(*index, 0)], ref[(*index, 1)]
    if value.dtype == BF16:
        return product(value, top) + product(value, rest)
    high, low = split(value)
    return product(high, top) + product(low, top) + product(high, rest)


def groups_of(shape):
    rows = lax.broadcasted_iota(jnp.int32, shape, 0) >> 5
    cols = lax.broadcasted_iota(jnp.int32, shape, 1) >> 5
    return rows, cols


def spread(block, mask, copies):
    return jnp.where(mask, jnp.concatenate([block] * copies, axis=0), 0.0)


def pair_matrix(gen_a, gen_b):
    both = jnp.concatenate([gen_a, gen_b], axis=1)
    rows, cols = groups_of((LANES, 2 * LANES))
    mask = rows == (cols & 3)
    return jnp.concatenate([spread(both[:HALF], mask, 4), spread(both[HALF:], mask, 4)], axis=0)


def pair_extract(grad):
    cols = (lax.broadcasted_iota(jnp.int32, (HALF, 2 * LANES), 1) >> 5) & 3
    parts = []
    for h in range(2):
        total = jnp.zeros((HALF, 2 * LANES), F32)
        for g in range(4):
            start = h * LANES + g * HALF
            total = total + jnp.where(cols == g, grad[start : start + HALF], 0.0)
        parts.append(total)
    return jnp.concatenate(parts, axis=0)


def near_matrix(gen, k):
    rows, cols = groups_of((256, 256))
    low = cols & ~(1 << k)
    return spread(gen[:HALF], rows == low, 8) + spread(gen[HALF:], rows == (low | (1 << k)), 8)


def near_extract(grad, k):
    cols = lax.broadcasted_iota(jnp.int32, (HALF, 256), 1) >> 5
    low = cols & ~(1 << k)
    parts = []
    for want in (low, low | (1 << k)):
        total = jnp.zeros((HALF, 256), F32)
        for g in range(8):
            total = total + jnp.where(want == g, grad[g * HALF : (g + 1) * HALF], 0.0)
        parts.append(total)
    return jnp.concatenate(parts, axis=0)


def diag_matrix(block):
    rows, cols = groups_of((256, 256))
    return spread(block, rows == cols, 8)


def diag_extract(grad):
    cols = lax.broadcasted_iota(jnp.int32, (HALF, 256), 1) >> 5
    total = jnp.zeros((HALF, 256), F32)
    for g in range(8):
        total = total + jnp.where(cols == g, grad[g * HALF : (g + 1) * HALF], 0.0)
    return total


PAIRS = (((0, 1), (2, 3)), ((0, 2), (1, 3)))
N_SEMS = 224
SPLIT_GATHER = 320
SPLIT_SUM = 320
STOP = None


class Stop(Exception):
    pass


class Sent:
    def __init__(self, copy):
        self.copy, self.received = copy, False

    def arrive(self):
        if not self.received:
            self.copy.wait_recv()
            self.received = True


def main_kernel(n_dp, scale, *refs):
    pending, endings = [], []
    try:
        main_body(n_dp, scale, pending, endings, *refs)
    except Stop:
        pass
    for c in pending:
        c.arrive()
        c.copy.wait_send()
    for end in endings:
        end()


def main_body(
    n_dp, scale, pending, endings,
    hid, wt, gen, cot, query, igrad, ggrad,
    w_v, hbuf, base, pb, gz, gy, gyb, gzb, ghome, gsave_y, gsave_z, gmid, glocal, slocal,
    szb, ssend, syb, qsend, qb, s5b, s7b, zsend, gsend_t, gsend_z, gb,
    rs_s2, rs_r2, rs_s1, rs_s3, rs_r1, rs_r3, q_s2, q_r2, q_s1, q_s3, q_r1, q_r3,
    gp, gp_z, gp_y, gpb, sums_a, sums_b, slab_a, slab_b, gout, mats_loc, mats_z, mats_y,
    send_sem, recv_sem, w_sem,
):
    tokens = hid.shape[0]
    me = lax.axis_index("tensor")
    my_dp = lax.axis_index("dp")
    y, z = me // SIDE, lax.rem(me, SIDE)
    z_of = lax.rem(y + z, SIDE)
    counter = [0]

    def mark(name):
        if STOP == name:
            if name == "bwd_y":
                w_copy.wait()
            raise Stop

    def at(dy, dz):
        return wrap(y + dy, SIDE) * SIDE + wrap(z + dz, SIDE)

    def toward(axis, step):
        return at(step, 0) if axis == "y" else at(0, step)

    def place(axis, step, fixed):
        return (step, fixed) if axis == "y" else (fixed, step)

    def ids(n=1):
        first = counter[0]
        counter[0] += n
        return first

    def copy(src, dst, send_index, recv_index, device):
        return pltpu.make_async_remote_copy(
            src_ref=src,
            dst_ref=dst,
            send_sem=send_sem.at[send_index],
            recv_sem=recv_sem.at[recv_index],
            device_id=device,
            device_id_type=MESH,
        )

    def send(src, dst, dev, axis="tensor"):
        index = ids()
        c = copy(src, dst, index, index, {axis: dev})
        c.start()
        c = Sent(c)
        pending.append(c)
        return c

    def w_rows(dy, dz):
        return w_v[pl.ds(pl.multiple_of(at(dy, dz) * 512, 512), 512), :]

    def chunk_at(index):
        return pl.ds(pl.multiple_of(index * LANES, LANES), LANES)

    w_copy = pltpu.make_async_copy(wt, w_v, w_sem)
    w_copy.start()

    barrier = pltpu.get_barrier_semaphore()
    for d in range(1, 16):
        pl.semaphore_signal(
            barrier, inc=1, device_id={"tensor": lax.rem(me + d, 16)}, device_id_type=MESH
        )
    for d in range(1, n_dp):
        pl.semaphore_signal(
            barrier, inc=1, device_id={"dp": lax.rem(my_dp + d, n_dp)}, device_id_type=MESH
        )
    pl.semaphore_wait(barrier, 15 + n_dp - 1)

    cot_in, genz_in, geny_in = [], [], []
    for d in range(1, 4):
        cols = chunk_at(lax.rem(y + d + z, SIDE))
        cot_in.append(send(cot.at[:, cols], gyb.at[y], at(d, 0)))
        geny_in.append(send(gen.at[pl.ds(6, 2), :, cols], gy.at[y], at(d, 0)))

    def held(dy, dz, lo, hi):
        ref = hid if (dy, dz) == (0, 0) else hbuf.at[dy, dz]
        return ref.at[pl.ds(lo, hi - lo)]

    arrivals = {(dy, dz): [] for dy in range(4) for dz in range(4)}

    def hop(axis, fixed, step, sign, lo, hi):
        target = place(axis, step + sign & 3, fixed)
        c = send(
            held(*place(axis, step, fixed), lo, hi),
            hbuf.at[(*target, pl.ds(lo, hi - lo))],
            toward(axis, sign),
        )
        arrivals[target].append(c)
        return c

    def ring_start(axis, fixed, lo, hi):
        return [hop(axis, fixed, 0, 1, lo, hi), hop(axis, fixed, 0, -1, lo, hi)]

    def ring_forward(axis, fixed, lo, hi, copies):
        middle = (lo + hi) // 2
        copies[0].arrive()
        copies.append(hop(axis, fixed, 1, 1, lo, middle))
        copies[1].arrive()
        copies.append(hop(axis, fixed, 3, -1, middle, hi))

    cut = SPLIT_GATHER * tokens // 384 // 32 * 32
    routes = [("z", "y", 0, cut)]
    if cut < tokens:
        routes.append(("y", "z", cut, tokens))
    first = [ring_start(a, 0, lo, hi) for a, _, lo, hi in routes]
    second = [{0: ring_start(b, 0, lo, hi)} for _, b, lo, hi in routes]
    for d in range(1, 4):
        cols = chunk_at(wrap(z + d, SIDE))
        genz_in.append(send(gen.at[pl.ds(4, 2), :, cols], gz.at[z], at(0, d)))

    def gather_second(step):
        for (_, b, lo, hi), copies in zip(routes, second):
            ring_forward(b, step, lo, hi, copies[step])

    def gather_first():
        for (a, b, lo, hi), ring, copies in zip(routes, first, second):
            middle = (lo + hi) // 2
            ring[0].arrive()
            ring.append(hop(a, 0, 1, 1, lo, middle))
            copies[1] = ring_start(b, 1, lo, hi)
            ring[1].arrive()
            ring.append(hop(a, 0, 3, -1, middle, hi))
            copies[3] = ring_start(b, 3, lo, hi)

    def gather_far():
        for (_, b, lo, hi), ring, copies in zip(routes, first, second):
            ring[2].arrive()
            ring[3].arrive()
            copies[2] = ring_start(b, 2, lo, hi)

    def accumulate(*blocks):
        for dy, dz in blocks:
            for c in arrivals[dy, dz]:
                c.arrive()
            base[...] += dot(hbuf[dy, dz], w_rows(-dy, -dz))

    gyb[y] = cot[:, chunk_at(z_of)]
    gy[y] = gen[6:8, :, chunk_at(z_of)]
    gz[z] = gen[4:6, :, chunk_at(z)]

    for k in range(3):
        for s in range(2):
            put_split(mats_loc, (k, s), near_matrix(gen[k, :, 256 * s : 256 * s + 256], k))
    for s in range(2):
        for h in range(2):
            block = gen[3, HALF * h : HALF * h + HALF, 256 * s : 256 * s + 256]
            put_split(mats_loc, (3 + h, s), diag_matrix(block))

    def pair_of(ref, a, b):
        return jnp.concatenate([ref[a], ref[b]], axis=1)

    def fill_pairs(mats, gens):
        for k in range(2):
            for i, (a, b) in enumerate(PAIRS[k]):
                put_split(mats, (k, i), pair_matrix(gens[a, k], gens[b, k]))

    def pairs_apply(product, order, source, mats, save, out):
        values = None
        for k, target in zip(order, (save, out)):
            new = [None] * 4
            for i, (a, b) in enumerate(PAIRS[k]):
                if values is None:
                    v = pair_of(source, a, b)
                else:
                    v = jnp.concatenate([values[a], values[b]], axis=1)
                v = v.astype(F32) + mix(product, v, mats, (k, i))
                new[a], new[b] = v[:, :LANES], v[:, LANES:]
            values = new
            for m in range(4):
                target[m] = values[m].astype(BF16)

    def cross(src, dst, own_slot, dev_of, src_of):
        index = ids(4)
        sent = []
        for d in range(4):
            c = copy(
                src.at[src_of(d)], dst.at[own_slot], index + d, index + own_slot,
                {"tensor": dev_of(d)},
            )
            if d == 0:
                keep = pltpu.make_async_copy(
                    src.at[src_of(0)], dst.at[own_slot], recv_sem.at[index + own_slot]
                )
                pl.when(dev_of(0) != me)(lambda c=c: c.start())
                pl.when(dev_of(0) == me)(lambda keep=keep: keep.start())
            else:
                c.start()
            sent.append(c)
        done = []

        def arrive():
            if not done:
                done.append(True)
                for m in range(4):
                    pltpu.make_async_copy(src.at[m], dst.at[m], recv_sem.at[index + m]).wait()

        def finish():
            arrive()
            pl.when(dev_of(0) != me)(lambda: sent[0].wait_send())
            for c in sent[1:]:
                c.wait_send()

        endings.append(finish)
        return arrive

    for c in geny_in:
        c.arrive()
    fill_pairs(mats_y, gy)
    for c in cot_in:
        c.arrive()
    pairs_apply(dot_nt, (1, 0), gyb, mats_y, gsave_y, gsend_t)
    step_in = []
    for d in range(1, 4):
        step_in.append(send(gsend_t.at[wrap(y + d, SIDE)], gmid.at[z_of], at(d, 0)))
    gmid[z_of] = gsend_t[y]
    mark("bwd_y")

    gather_second(0)
    for c in genz_in:
        c.arrive()
    fill_pairs(mats_z, gz)
    for c in step_in:
        c.arrive()
    step_in = []
    for d in range(1, 4):
        step_in.append(send(gmid.at[wrap(z + d, SIDE)], gzb.at[z], at(0, d)))
    gzb[z] = gmid[z]
    w_copy.wait()
    base[...] = dot(hid[...], w_rows(0, 0))
    mark("ag0")

    gather_first()
    accumulate((1, 0), (3, 0), (0, 1), (0, 3))
    mark("ag1")
    gather_far()
    accumulate((2, 0), (0, 2))

    for c in step_in:
        c.arrive()
    pairs_apply(dot_nt, (1, 0), gzb, mats_z, gsave_z, gsend_z)
    back_in = []
    for d in range(1, 4):
        back_in.append(send(gsend_z.at[wrap(z + d, SIDE)], ghome.at[z], at(0, d)))
    ghome[z] = gsend_z[z]
    mark("bwd_z")

    gather_second(1)
    accumulate((1, 1), (3, 1))
    gather_second(3)
    accumulate((1, 3), (3, 3))
    mark("ag2")

    for c in back_in:
        c.arrive()
    ga = pair_of(ghome, 0, 1)
    gc = pair_of(ghome, 2, 3)
    glocal[3, 0], glocal[3, 1] = ga, gc
    fa = ga.astype(F32) + mix(dot_nt, ga, mats_loc, (3, 0)) + mix(dot_nt, gc, mats_loc, (3, 1))
    fb = gc.astype(F32) + mix(dot_nt, ga, mats_loc, (4, 0)) + mix(dot_nt, gc, mats_loc, (4, 1))
    for k in (2, 1, 0):
        glocal[k, 0], glocal[k, 1] = fa.astype(BF16), fb.astype(BF16)
        fa = fa + mix(dot_nt, fa, mats_loc, (k, 0))
        fb = fb + mix(dot_nt, fb, mats_loc, (k, 1))
    gb[:, :256] = fa.astype(BF16)
    gb[:, 256:] = fb.astype(BF16)
    mark("bwd_local")

    gather_second(2)
    accumulate((1, 2), (3, 2))
    mark("ag3")

    computed = set()

    def partial(dy, dz, lo, hi):
        if (dy, dz) not in computed:
            computed.add((dy, dz))
            pb[dy, dz] = dot_nt(gb[...], w_rows(dy, dz))
        return pb[dy, dz, lo:hi]

    class Sum:
        def __init__(self, a, b, lo, hi):
            self.a, self.b, self.lo, self.hi, self.middle = a, b, lo, hi, (lo + hi) // 2
            self.copies, self.last = {}, []
            self.rows = pl.ds(lo, hi - lo)
            self.top, self.low = pl.ds(lo, self.middle - lo), pl.ds(self.middle, hi - self.middle)

        def far(self, fixed):
            block = partial(*place(self.a, 2, fixed), self.lo, self.hi)
            rs_s2[fixed, self.rows] = block.astype(BF16)
            self.copies[fixed] = [
                send(rs_s2.at[fixed, self.top], rs_r2.at[fixed, self.top], toward(self.a, 1)),
                send(rs_s2.at[fixed, self.low], rs_r2.at[fixed, self.low], toward(self.a, -1)),
            ]

        def near(self, fixed):
            cs, size = self.copies[fixed], self.middle - self.lo
            p = partial(*place(self.a, 1, fixed), self.lo, self.hi)
            cs[0].arrive()
            rs_s1[fixed, self.top] = (p[:size] + rs_r2[fixed, self.top].astype(F32)).astype(BF16)
            rs_s1[fixed, self.low] = p[size:].astype(BF16)
            cs.append(
                send(rs_s1.at[fixed, self.rows], rs_r1.at[fixed, self.rows], toward(self.a, 1))
            )
            p = partial(*place(self.a, 3, fixed), self.lo, self.hi)
            cs[1].arrive()
            rs_s3[fixed, self.top] = p[:size].astype(BF16)
            rs_s3[fixed, self.low] = (p[size:] + rs_r2[fixed, self.low].astype(F32)).astype(BF16)
            cs.append(
                send(rs_s3.at[fixed, self.rows], rs_r3.at[fixed, self.rows], toward(self.a, -1))
            )

        def whole(self, fixed):
            p = partial(*place(self.a, 0, fixed), self.lo, self.hi)
            for c in self.copies[fixed][2:]:
                c.arrive()
            return p + rs_r1[fixed, self.rows].astype(F32) + rs_r3[fixed, self.rows].astype(F32)

        def last_far(self):
            q_s2[self.rows] = self.whole(2).astype(BF16)
            self.last = [
                send(q_s2.at[self.top], q_r2.at[self.top], toward(self.b, 1)),
                send(q_s2.at[self.low], q_r2.at[self.low], toward(self.b, -1)),
            ]

        def last_near(self):
            size = self.middle - self.lo
            q = self.whole(1)
            self.last[0].arrive()
            q_s1[self.top] = (q[:size] + q_r2[self.top].astype(F32)).astype(BF16)
            q_s1[self.low] = q[size:].astype(BF16)
            self.last.append(send(q_s1.at[self.rows], q_r1.at[self.rows], toward(self.b, 1)))
            q = self.whole(3)
            self.last[1].arrive()
            q_s3[self.top] = q[:size].astype(BF16)
            q_s3[self.low] = (q[size:] + q_r2[self.low].astype(F32)).astype(BF16)
            self.last.append(send(q_s3.at[self.rows], q_r3.at[self.rows], toward(self.b, -1)))

        def end(self):
            q = self.whole(0)
            for c in self.last[2:]:
                c.arrive()
            q = q + q_r1[self.rows].astype(F32) + q_r3[self.rows].astype(F32)
            igrad[self.rows] = q.astype(BF16)

    cut = SPLIT_SUM * tokens // 384 // 32 * 32
    sums = [Sum("y", "z", 0, cut)]
    if cut < tokens:
        sums.append(Sum("z", "y", cut, tokens))
    for fixed in (2, 1, 3, 0):
        for s in sums:
            s.far(fixed)
    mark("rs_far")

    accumulate((2, 1), (2, 3), (2, 2))
    mark("base")
    fa, fb = base[:, :256], base[:, 256:]
    for k in range(3):
        slocal[k, 0], slocal[k, 1] = fa.astype(BF16), fb.astype(BF16)
        fa = fa + mix(dot, fa, mats_loc, (k, 0))
        fb = fb + mix(dot, fb, mats_loc, (k, 1))
    slocal[3, 0], slocal[3, 1] = fa.astype(BF16), fb.astype(BF16)
    fc = fa + mix(dot, fa, mats_loc, (3, 0)) + mix(dot, fb, mats_loc, (4, 0))
    fd = fb + mix(dot, fa, mats_loc, (3, 1)) + mix(dot, fb, mats_loc, (4, 1))
    for c in range(4):
        side = fc if c < 2 else fd
        ssend[c] = side[:, (c % 2) * LANES : (c % 2) * LANES + LANES].astype(BF16)
    fwd_in = []
    for d in range(1, 4):
        fwd_in.append(send(ssend.at[wrap(z + d, SIDE)], szb.at[z], at(0, d)))
    szb[z] = ssend[z]
    mark("fwd_local")

    for fixed in (2, 1):
        for s in sums:
            s.near(fixed)
    mark("near1")

    def put_local(k, s, value):
        for j in range(2):
            gp[pl.ds(((k // 2) * 4 + 2 * s + j) * 128 + (k % 2) * 64, 64)] = value[
                :, j * LANES : (j + 1) * LANES
            ]

    for k in range(3):
        for s in range(2):
            put_local(k, s, near_extract(dot_tn(slocal[k, s], glocal[k, s]), k))
    for s in range(2):
        put_local(
            3, s,
            jnp.concatenate(
                [diag_extract(dot_tn(slocal[3, h], glocal[3, s])) for h in range(2)], axis=0
            ),
        )

    for c in fwd_in:
        c.arrive()
    pairs_apply(dot, (0, 1), szb, mats_z, s5b, zsend)
    fwd_arrive = cross(
        zsend, syb, y,
        lambda d: ((SIDE - d) % SIDE) * SIDE + wrap(z + d, SIDE),
        lambda d: wrap(z + d, SIDE),
    )
    mark("fwd_z")
    for fixed in (3, 0):
        for s in sums:
            s.near(fixed)
    for s in sums:
        s.last_far()
    mark("near2")

    def pair_grads(states, grads, dst):
        for k in range(2):
            for i, (a, b) in enumerate(PAIRS[k]):
                value = pair_extract(dot_tn(pair_of(states[k], a, b), pair_of(grads[k], a, b)))
                dst[a, k * 64 : k * 64 + 64] = value[:, :LANES]
                dst[b, k * 64 : k * 64 + 64] = value[:, LANES:]

    def piece(index):
        return pl.ds(pl.multiple_of(index * 128, 128), 128)

    pair_grads((szb, s5b), (gsave_z, gzb), gp_z)
    outz_in = []
    for d in range(1, 4):
        outz_in.append(send(gp_z.at[wrap(z + d, SIDE)], gp.at[piece(8 + z)], at(0, d)))
    gp[piece(8 + z)] = gp_z[z]

    fwd_arrive()
    pairs_apply(dot, (0, 1), syb, mats_y, s7b, qsend)
    query_in = []
    for d in range(1, 4):
        query_in.append(send(qsend.at[wrap(y + d, SIDE)], qb.at[z_of], at(d, 0)))
    qb[z_of] = qsend[y]
    mark("fwd_y")

    pair_grads((syb, s7b), (gsave_y, gyb), gp_y)
    outy_in = []
    for d in range(1, 4):
        outy_in.append(send(gp_y.at[wrap(y + d, SIDE)], gp.at[piece(12 + z_of)], at(d, 0)))
    gp[piece(12 + z_of)] = gp_y[y]
    mark("grads")

    class Slabs:
        def __init__(self, start, size, sums_ref, slab_ref):
            self.start, self.size = start, size
            self.sums_ref, self.slab_ref = sums_ref, slab_ref
            self.ins, self.outs = [], []

        def rows(self, dev):
            return pl.ds(pl.multiple_of(self.start + dev * self.size, 32), self.size)

        def scatter(self):
            all_rows = pl.ds(self.start, 16 * self.size)
            gpb[all_rows] = gp[all_rows].astype(BF16)
            for d in range(1, n_dp):
                dev = lax.rem(my_dp + d, n_dp)
                self.ins.append(send(gpb.at[self.rows(dev)], self.sums_ref.at[d], dev, "dp"))

        def gather(self):
            total = gp[self.rows(my_dp)]
            for d, c in zip(range(1, n_dp), self.ins):
                c.arrive()
                total = total + self.sums_ref[d].astype(F32)
            self.slab_ref[...] = total * scale
            for d in range(1, n_dp):
                dev = lax.rem(my_dp + d, n_dp)
                self.outs.append(send(self.slab_ref, gout.at[self.rows(my_dp)], dev, "dp"))
            gout[self.rows(my_dp)] = self.slab_ref[...]

        def finish(self):
            for c in self.outs:
                c.arrive()

    for s in sums:
        s.last_near()
    mark("last_near")
    early, late = Slabs(0, 96, sums_a, slab_a), Slabs(1536, 32, sums_b, slab_b)
    for c in outz_in:
        c.arrive()
    if n_dp > 1:
        early.scatter()

    for c in outy_in:
        c.arrive()
    if n_dp > 1:
        late.scatter()
        early.gather()
    if n_dp > 1:
        late.gather()
    mark("dp")

    for c in query_in:
        c.arrive()
    for c in range(4):
        query[:, c * LANES : (c + 1) * LANES] = qb[c]
    mark("query")
    for s in sums:
        s.end()
    mark("igrad")
    if n_dp > 1:
        early.finish()
        late.finish()
    final = gout if n_dp > 1 else gp
    for pair in range(4):
        for c in range(4):
            for j in range(2):
                ggrad[2 * pair + j, :, c * LANES : (c + 1) * LANES] = final[
                    pl.ds((pair * 4 + c) * 128 + j * 64, 64)
                ]


def main_call(hidden, weight, generators, cotangent, n_dp=1, scale=1.0):
    tokens = hidden.shape[0]
    vm = lambda *shape, dtype=BF16: pltpu.VMEM(shape, dtype)
    chunks = vm(4, tokens, LANES)
    block = vm(tokens, 512)
    blocks = vm(4, tokens, 512)
    flops = 4 * tokens * 8192 * 512
    return pl.pallas_call(
        functools.partial(main_kernel, n_dp, scale),
        out_shape=(
            jax.ShapeDtypeStruct((tokens, 512), BF16),
            jax.ShapeDtypeStruct((tokens, 512), BF16),
            jax.ShapeDtypeStruct((8, 64, 512), F32),
        ),
        in_specs=[
            pl.BlockSpec(memory_space=pltpu.VMEM),
            pl.BlockSpec(memory_space=pl.ANY),
            pl.BlockSpec(memory_space=pltpu.VMEM),
            pl.BlockSpec(memory_space=pltpu.VMEM),
        ],
        out_specs=[pl.BlockSpec(memory_space=pltpu.VMEM)] * 3,
        scratch_shapes=[
            vm(8192, 512),
            vm(4, 4, tokens, 512),
            vm(tokens, 512, dtype=F32),
            vm(4, 4, tokens, 512, dtype=F32),
            vm(4, 2, 64, LANES, dtype=F32),
            vm(4, 2, 64, LANES, dtype=F32),
            chunks, chunks, chunks, chunks, chunks, chunks,
            vm(4, 2, tokens, 256),
            vm(4, 2, tokens, 256),
            chunks, chunks, chunks, chunks, chunks,
            chunks, chunks, chunks, chunks, chunks,
            block,
            blocks, blocks, blocks, blocks, blocks, blocks,
            block, block, block, block, block, block,
            vm(2048, 128, dtype=F32),
            vm(4, 128, 128, dtype=F32),
            vm(4, 128, 128, dtype=F32),
            vm(2048, 128),
            vm(16, 96, 128),
            vm(16, 32, 128),
            vm(96, 128, dtype=F32),
            vm(32, 128, dtype=F32),
            vm(2048, 128, dtype=F32),
            vm(5, 2, 2, 256, 256),
            vm(2, 2, 2, 256, 256),
            vm(2, 2, 2, 256, 256),
            pltpu.SemaphoreType.DMA((N_SEMS,)),
            pltpu.SemaphoreType.DMA((N_SEMS,)),
            pltpu.SemaphoreType.DMA,
        ],
        compiler_params=pltpu.CompilerParams(
            collective_id=0, has_side_effects=True, vmem_limit_bytes=VMEM_BYTES
        ),
        cost_estimate=pl.CostEstimate(
            flops=flops, bytes_accessed=12 * 1024 * 1024, transcendentals=0
        ),
        name="adapt",
    )(hidden, weight, generators, cotangent)


def copy_kernel(*refs):
    count = len(refs) // 2
    for source, target in zip(refs[:count], refs[count:]):
        target[...] = source[...]


def copy_call(*arrays):
    whole = pl.BlockSpec(memory_space=pltpu.VMEM)
    return pl.pallas_call(
        copy_kernel,
        out_shape=tuple(jax.ShapeDtypeStruct(a.shape, a.dtype) for a in arrays),
        in_specs=[whole] * len(arrays),
        out_specs=[whole] * len(arrays),
        name="results",
    )(*arrays)


def on_device(hidden, base_weight, generators, cotangent):
    n = lax.axis_size("dp")
    scale = 1.0 / math.sqrt(hidden.shape[0] * n)
    return copy_call(*main_call(hidden, base_weight, generators, cotangent, n, scale))


def solution(mesh):
    placed = (P("dp", "tensor"), P(None, "tensor"), P(None, None, "tensor"), P("dp", "tensor"))
    return jax.shard_map(
        on_device,
        mesh=mesh,
        in_specs=placed,
        out_specs=(P("dp", "tensor"), P("dp", "tensor"), P(None, None, "tensor")),
        check_vma=False,
    )
```

```python
import functools
import math

import jax
import jax.numpy as jnp
from jax import lax
from jax.experimental import pallas as pl
from jax.experimental.pallas import tpu as pltpu
from jax.sharding import PartitionSpec as P

MESH = pl.DeviceIdType.MESH
F32 = jnp.float32
BF16 = jnp.bfloat16
SIDE = 4
LANES = 128
HALF = 32
VMEM_BYTES = 60 * 1024 * 1024


def wrap(value, n):
    return lax.rem(value + n, n)


def dot(a, b):
    return jnp.dot(a, b, preferred_element_type=F32)


def dot_nt(a, b):
    return lax.dot_general(a, b, (((1,), (1,)), ((), ())), preferred_element_type=F32)


def dot_tn(a, b):
    return lax.dot_general(a, b, (((0,), (0,)), ((), ())), preferred_element_type=F32)


def split(value):
    high = value.astype(BF16)
    return high, (value - high.astype(F32)).astype(BF16)


def put_split(ref, index, value):
    ref[(*index, 0)], ref[(*index, 1)] = split(value)


def mix(product, value, ref, index):
    top, rest = ref[(*index, 0)], ref[(*index, 1)]
    if value.dtype == BF16:
        return product(value, top) + product(value, rest)
    high, low = split(value)
    return product(high, top) + product(low, top) + product(high, rest)


def groups_of(shape):
    rows = lax.broadcasted_iota(jnp.int32, shape, 0) >> 5
    cols = lax.broadcasted_iota(jnp.int32, shape, 1) >> 5
    return rows, cols


def spread(block, mask, copies):
    return jnp.where(mask, jnp.concatenate([block] * copies, axis=0), 0.0)


def pair_matrix(gen_a, gen_b):
    both = jnp.concatenate([gen_a, gen_b], axis=1)
    rows, cols = groups_of((LANES, 2 * LANES))
    mask = rows == (cols & 3)
    return jnp.concatenate([spread(both[:HALF], mask, 4), spread(both[HALF:], mask, 4)], axis=0)


def pair_extract(grad):
    cols = (lax.broadcasted_iota(jnp.int32, (HALF, 2 * LANES), 1) >> 5) & 3
    parts = []
    for h in range(2):
        total = jnp.zeros((HALF, 2 * LANES), F32)
        for g in range(4):
            start = h * LANES + g * HALF
            total = total + jnp.where(cols == g, grad[start : start + HALF], 0.0)
        parts.append(total)
    return jnp.concatenate(parts, axis=0)


def near_matrix(gen, k):
    rows, cols = groups_of((256, 256))
    low = cols & ~(1 << k)
    return spread(gen[:HALF], rows == low, 8) + spread(gen[HALF:], rows == (low | (1 << k)), 8)


def near_extract(grad, k):
    cols = lax.broadcasted_iota(jnp.int32, (HALF, 256), 1) >> 5
    low = cols & ~(1 << k)
    parts = []
    for want in (low, low | (1 << k)):
        total = jnp.zeros((HALF, 256), F32)
        for g in range(8):
            total = total + jnp.where(want == g, grad[g * HALF : (g + 1) * HALF], 0.0)
        parts.append(total)
    return jnp.concatenate(parts, axis=0)


def diag_matrix(block):
    rows, cols = groups_of((256, 256))
    return spread(block, rows == cols, 8)


def diag_extract(grad):
    cols = lax.broadcasted_iota(jnp.int32, (HALF, 256), 1) >> 5
    total = jnp.zeros((HALF, 256), F32)
    for g in range(8):
        total = total + jnp.where(cols == g, grad[g * HALF : (g + 1) * HALF], 0.0)
    return total


PAIRS = (((0, 1), (2, 3)), ((0, 2), (1, 3)))
N_SEMS = 224
SPLIT_GATHER = 352
SPLIT_SUM = 352
STOP = None


class Stop(Exception):
    pass


class Sent:
    def __init__(self, copy):
        self.copy, self.received = copy, False

    def arrive(self):
        if not self.received:
            self.copy.wait_recv()
            self.received = True


def main_kernel(n_dp, scale, *refs):
    pending, endings = [], []
    try:
        main_body(n_dp, scale, pending, endings, *refs)
    except Stop:
        pass
    for c in pending:
        c.arrive()
        c.copy.wait_send()
    for end in endings:
        end()


def main_body(
    n_dp, scale, pending, endings,
    hid, wt, gen, cot, query, igrad, ggrad,
    w_v, hbuf, base, pb, gz, gy, gyb, gzb, ghome, gsave_y, gsave_z, qmid, glocal, slocal,
    szb, ssend, syb, qsend, qb, s5b, s7b, zsend, gsend_t, gsend_z, gb,
    rs_s2, rs_r2, rs_s1, rs_s3, rs_r1, rs_r3, q_s2, q_r2, q_s1, q_s3, q_r1, q_r3,
    gp, gp_z, gp_y, gp_mid, gpf, gpb, sums_a, sums_b, slab_a, slab_b, gout, mats_loc, mats_z, mats_y,
    send_sem, recv_sem, w_sem,
):
    tokens = hid.shape[0]
    me = lax.axis_index("tensor")
    my_dp = lax.axis_index("dp")
    y, z = me // SIDE, lax.rem(me, SIDE)
    counter = [0]

    def mark(name):
        if STOP == name:
            if name == "bwd_y":
                w_copy.wait()
            raise Stop

    def at(dy, dz):
        return wrap(y + dy, SIDE) * SIDE + wrap(z + dz, SIDE)

    def toward(axis, step):
        return at(step, 0) if axis == "y" else at(0, step)

    def place(axis, step, fixed):
        return (step, fixed) if axis == "y" else (fixed, step)

    def ids(n=1):
        first = counter[0]
        counter[0] += n
        return first

    def copy(src, dst, send_index, recv_index, device):
        return pltpu.make_async_remote_copy(
            src_ref=src,
            dst_ref=dst,
            send_sem=send_sem.at[send_index],
            recv_sem=recv_sem.at[recv_index],
            device_id=device,
            device_id_type=MESH,
        )

    def send(src, dst, dev, axis="tensor"):
        index = ids()
        c = copy(src, dst, index, index, {axis: dev})
        c.start()
        c = Sent(c)
        pending.append(c)
        return c

    def w_rows(dy, dz):
        return w_v[pl.ds(pl.multiple_of(at(dy, dz) * 512, 512), 512), :]

    def chunk_at(index):
        return pl.ds(pl.multiple_of(index * LANES, LANES), LANES)

    w_copy = pltpu.make_async_copy(wt, w_v, w_sem)
    w_copy.start()

    barrier = pltpu.get_barrier_semaphore()
    for d in range(1, 16):
        pl.semaphore_signal(
            barrier, inc=1, device_id={"tensor": lax.rem(me + d, 16)}, device_id_type=MESH
        )
    for d in range(1, n_dp):
        pl.semaphore_signal(
            barrier, inc=1, device_id={"dp": lax.rem(my_dp + d, n_dp)}, device_id_type=MESH
        )
    pl.semaphore_wait(barrier, 15 + n_dp - 1)

    def cross(src_of, dst, own_slot, dev_of, always_remote):
        index = ids(4)
        sent = []
        for d in range(4):
            c = copy(
                src_of(d), dst.at[own_slot], index + d, index + own_slot, {"tensor": dev_of(d)}
            )
            if d == 0:
                keep = pltpu.make_async_copy(
                    src_of(0), dst.at[own_slot], recv_sem.at[index + own_slot]
                )
                pl.when(always_remote)(lambda c=c: c.start())
                pl.when(jnp.logical_not(always_remote))(lambda keep=keep: keep.start())
            else:
                c.start()
            sent.append(c)
        done = []

        def arrive():
            if not done:
                done.append(True)
                for m in range(4):
                    pltpu.make_async_copy(dst.at[m], dst.at[m], recv_sem.at[index + m]).wait()

        def finish():
            arrive()
            pl.when(always_remote)(lambda: sent[0].wait_send())
            for c in sent[1:]:
                c.wait_send()

        endings.append(finish)
        return arrive

    def along_y(src, dst):
        copies = [send(src.at[wrap(y + d, SIDE)], dst.at[y], at(d, 0)) for d in range(1, 4)]
        dst[y] = src[y]
        return copies

    def along_z(src, dst, first=0):
        copies = [
            send(src.at[wrap(z + d, SIDE)], dst.at[first + z], at(0, d)) for d in range(1, 4)
        ]
        dst[first + z] = src[z]
        return copies

    def arrive_all(copies):
        for c in copies:
            c.arrive()

    def turned(d):
        return z * SIDE + wrap(z + d, SIDE)

    cot_arrive = cross(
        lambda d: cot.at[:, chunk_at(wrap(z + d, SIDE))], gyb, y, turned, y != z
    )
    geny_arrive = cross(
        lambda d: gen.at[pl.ds(6, 2), :, chunk_at(wrap(z + d, SIDE))], gy, y, turned, y != z
    )

    def held(dy, dz, lo, hi):
        ref = hid if (dy, dz) == (0, 0) else hbuf.at[dy, dz]
        return ref.at[pl.ds(lo, hi - lo)]

    arrivals = {(dy, dz): [] for dy in range(4) for dz in range(4)}

    def hop(axis, fixed, step, sign, lo, hi):
        target = place(axis, step + sign & 3, fixed)
        c = send(
            held(*place(axis, step, fixed), lo, hi),
            hbuf.at[(*target, pl.ds(lo, hi - lo))],
            toward(axis, sign),
        )
        arrivals[target].append(c)
        return c

    def ring_start(axis, fixed, lo, hi):
        return [hop(axis, fixed, 0, 1, lo, hi), hop(axis, fixed, 0, -1, lo, hi)]

    def ring_forward(axis, fixed, lo, hi, copies):
        middle = (lo + hi) // 2
        copies[0].arrive()
        copies.append(hop(axis, fixed, 1, 1, lo, middle))
        copies[1].arrive()
        copies.append(hop(axis, fixed, 3, -1, middle, hi))

    cut = SPLIT_GATHER * tokens // 384 // 32 * 32
    routes = [("z", "y", 0, cut)]
    if cut < tokens:
        routes.append(("y", "z", cut, tokens))
    first = [ring_start(a, 0, lo, hi) for a, _, lo, hi in routes]
    second = [{0: ring_start(b, 0, lo, hi)} for _, b, lo, hi in routes]
    genz_in = []
    for d in range(1, 4):
        cols = chunk_at(wrap(z + d, SIDE))
        genz_in.append(send(gen.at[pl.ds(4, 2), :, cols], gz.at[z], at(0, d)))

    def gather_second(step):
        for (_, b, lo, hi), copies in zip(routes, second):
            ring_forward(b, step, lo, hi, copies[step])

    def gather_first():
        for (a, b, lo, hi), ring, copies in zip(routes, first, second):
            middle = (lo + hi) // 2
            ring[0].arrive()
            ring.append(hop(a, 0, 1, 1, lo, middle))
            copies[1] = ring_start(b, 1, lo, hi)
            ring[1].arrive()
            ring.append(hop(a, 0, 3, -1, middle, hi))
            copies[3] = ring_start(b, 3, lo, hi)

    def gather_far():
        for (_, b, lo, hi), ring, copies in zip(routes, first, second):
            ring[2].arrive()
            ring[3].arrive()
            copies[2] = ring_start(b, 2, lo, hi)

    def accumulate(*blocks):
        for dy, dz in blocks:
            for c in arrivals[dy, dz]:
                c.arrive()
            base[...] += dot(hbuf[dy, dz], w_rows(-dy, -dz))

    gz[z] = gen[4:6, :, chunk_at(z)]

    for k in range(3):
        for s in range(2):
            put_split(mats_loc, (k, s), near_matrix(gen[k, :, 256 * s : 256 * s + 256], k))
    for s in range(2):
        for h in range(2):
            block = gen[3, HALF * h : HALF * h + HALF, 256 * s : 256 * s + 256]
            put_split(mats_loc, (3 + h, s), diag_matrix(block))

    def pair_of(ref, a, b):
        return jnp.concatenate([ref[a], ref[b]], axis=1)

    def fill_pairs(mats, gens):
        for k in range(2):
            for i, (a, b) in enumerate(PAIRS[k]):
                put_split(mats, (k, i), pair_matrix(gens[a, k], gens[b, k]))

    def pairs_apply(product, order, source, mats, save, out):
        values = None
        for k, target in zip(order, (save, out)):
            new = [None] * 4
            for i, (a, b) in enumerate(PAIRS[k]):
                if values is None:
                    v = pair_of(source, a, b)
                else:
                    v = jnp.concatenate([values[a], values[b]], axis=1)
                v = v.astype(F32) + mix(product, v, mats, (k, i))
                new[a], new[b] = v[:, :LANES], v[:, LANES:]
            values = new
            for m in range(4):
                target[m] = values[m].astype(BF16)

    geny_arrive()
    fill_pairs(mats_y, gy)
    cot_arrive()
    pairs_apply(dot_nt, (1, 0), gyb, mats_y, gsave_y, gsend_t)
    step_in = along_y(gsend_t, gzb)
    mark("bwd_y")

    gather_second(0)
    arrive_all(genz_in)
    fill_pairs(mats_z, gz)
    w_copy.wait()
    base[...] = dot(hid[...], w_rows(0, 0))
    mark("ag0")

    gather_first()
    mark("ag1")
    arrive_all(step_in)
    pairs_apply(dot_nt, (1, 0), gzb, mats_z, gsave_z, gsend_z)
    back_in = along_z(gsend_z, ghome)
    mark("bwd_z")
    accumulate((1, 0), (3, 0), (0, 1), (0, 3))

    gather_far()
    accumulate((2, 0), (0, 2))
    gather_second(1)
    accumulate((1, 1), (3, 1))
    gather_second(3)
    accumulate((1, 3), (3, 3))
    mark("ag2")

    arrive_all(back_in)
    ga = pair_of(ghome, 0, 1)
    gc = pair_of(ghome, 2, 3)
    glocal[3, 0], glocal[3, 1] = ga, gc
    fa = ga.astype(F32) + mix(dot_nt, ga, mats_loc, (3, 0)) + mix(dot_nt, gc, mats_loc, (3, 1))
    fb = gc.astype(F32) + mix(dot_nt, ga, mats_loc, (4, 0)) + mix(dot_nt, gc, mats_loc, (4, 1))
    for k in (2, 1, 0):
        glocal[k, 0], glocal[k, 1] = fa.astype(BF16), fb.astype(BF16)
        fa = fa + mix(dot_nt, fa, mats_loc, (k, 0))
        fb = fb + mix(dot_nt, fb, mats_loc, (k, 1))
    gb[:, :256] = fa.astype(BF16)
    gb[:, 256:] = fb.astype(BF16)
    mark("bwd_local")

    gather_second(2)
    accumulate((1, 2), (3, 2))
    mark("ag3")

    computed = set()

    def partial(dy, dz, lo, hi):
        if (dy, dz) not in computed:
            computed.add((dy, dz))
            pb[dy, dz] = dot_nt(gb[...], w_rows(dy, dz))
        return pb[dy, dz, lo:hi]

    class Sum:
        def __init__(self, a, b, lo, hi):
            self.a, self.b, self.lo, self.hi, self.middle = a, b, lo, hi, (lo + hi) // 2
            self.copies, self.last = {}, []
            self.rows = pl.ds(lo, hi - lo)
            self.top, self.low = pl.ds(lo, self.middle - lo), pl.ds(self.middle, hi - self.middle)

        def far(self, fixed):
            block = partial(*place(self.a, 2, fixed), self.lo, self.hi)
            rs_s2[fixed, self.rows] = block.astype(BF16)
            self.copies[fixed] = [
                send(rs_s2.at[fixed, self.top], rs_r2.at[fixed, self.top], toward(self.a, 1)),
                send(rs_s2.at[fixed, self.low], rs_r2.at[fixed, self.low], toward(self.a, -1)),
            ]

        def near(self, fixed):
            cs, size = self.copies[fixed], self.middle - self.lo
            p = partial(*place(self.a, 1, fixed), self.lo, self.hi)
            cs[0].arrive()
            rs_s1[fixed, self.top] = (p[:size] + rs_r2[fixed, self.top].astype(F32)).astype(BF16)
            rs_s1[fixed, self.low] = p[size:].astype(BF16)
            cs.append(
                send(rs_s1.at[fixed, self.rows], rs_r1.at[fixed, self.rows], toward(self.a, 1))
            )
            p = partial(*place(self.a, 3, fixed), self.lo, self.hi)
            cs[1].arrive()
            rs_s3[fixed, self.top] = p[:size].astype(BF16)
            rs_s3[fixed, self.low] = (p[size:] + rs_r2[fixed, self.low].astype(F32)).astype(BF16)
            cs.append(
                send(rs_s3.at[fixed, self.rows], rs_r3.at[fixed, self.rows], toward(self.a, -1))
            )

        def whole(self, fixed):
            p = partial(*place(self.a, 0, fixed), self.lo, self.hi)
            for c in self.copies[fixed][2:]:
                c.arrive()
            return p + rs_r1[fixed, self.rows].astype(F32) + rs_r3[fixed, self.rows].astype(F32)

        def last_far(self):
            q_s2[self.rows] = self.whole(2).astype(BF16)
            self.last = [
                send(q_s2.at[self.top], q_r2.at[self.top], toward(self.b, 1)),
                send(q_s2.at[self.low], q_r2.at[self.low], toward(self.b, -1)),
            ]

        def last_near(self):
            size = self.middle - self.lo
            q = self.whole(1)
            self.last[0].arrive()
            q_s1[self.top] = (q[:size] + q_r2[self.top].astype(F32)).astype(BF16)
            q_s1[self.low] = q[size:].astype(BF16)
            self.last.append(send(q_s1.at[self.rows], q_r1.at[self.rows], toward(self.b, 1)))
            q = self.whole(3)
            self.last[1].arrive()
            q_s3[self.top] = q[:size].astype(BF16)
            q_s3[self.low] = (q[size:] + q_r2[self.low].astype(F32)).astype(BF16)
            self.last.append(send(q_s3.at[self.rows], q_r3.at[self.rows], toward(self.b, -1)))

        def end(self):
            q = self.whole(0)
            for c in self.last[2:]:
                c.arrive()
            q = q + q_r1[self.rows].astype(F32) + q_r3[self.rows].astype(F32)
            igrad[self.rows] = q.astype(BF16)

    cut = SPLIT_SUM * tokens // 384 // 32 * 32
    sums = [Sum("y", "z", 0, cut)]
    if cut < tokens:
        sums.append(Sum("z", "y", cut, tokens))
    for fixed in (2, 1, 3, 0):
        for s in sums:
            s.far(fixed)
    mark("rs_far")

    accumulate((2, 1), (2, 3), (2, 2))
    mark("base")
    fa, fb = base[:, :256], base[:, 256:]
    for k in range(3):
        slocal[k, 0], slocal[k, 1] = fa.astype(BF16), fb.astype(BF16)
        fa = fa + mix(dot, fa, mats_loc, (k, 0))
        fb = fb + mix(dot, fb, mats_loc, (k, 1))
    slocal[3, 0], slocal[3, 1] = fa.astype(BF16), fb.astype(BF16)
    fc = fa + mix(dot, fa, mats_loc, (3, 0)) + mix(dot, fb, mats_loc, (4, 0))
    fd = fb + mix(dot, fa, mats_loc, (3, 1)) + mix(dot, fb, mats_loc, (4, 1))
    for c in range(4):
        side = fc if c < 2 else fd
        ssend[c] = side[:, (c % 2) * LANES : (c % 2) * LANES + LANES].astype(BF16)
    fwd_in = along_z(ssend, szb)
    mark("fwd_local")

    def near(*blocks):
        for fixed in blocks:
            for s in sums:
                s.near(fixed)

    near(2)
    mark("near1")

    def put_local(k, s, value):
        for j in range(2):
            gp[(k // 2) * 4 + 2 * s + j, (k % 2) * 64 : (k % 2) * 64 + 64] = value[
                :, j * LANES : (j + 1) * LANES
            ]

    for k in range(3):
        for s in range(2):
            put_local(k, s, near_extract(dot_tn(slocal[k, s], glocal[k, s]), k))
    for s in range(2):
        put_local(
            3, s,
            jnp.concatenate(
                [diag_extract(dot_tn(slocal[3, h], glocal[3, s])) for h in range(2)], axis=0
            ),
        )

    arrive_all(fwd_in)
    pairs_apply(dot, (0, 1), szb, mats_z, s5b, zsend)
    fwd_in = along_y(zsend, syb)
    mark("fwd_z")

    def pair_grads(states, grads, dst):
        for k in range(2):
            for i, (a, b) in enumerate(PAIRS[k]):
                value = pair_extract(dot_tn(pair_of(states[k], a, b), pair_of(grads[k], a, b)))
                dst[a, k * 64 : k * 64 + 64] = value[:, :LANES]
                dst[b, k * 64 : k * 64 + 64] = value[:, LANES:]

    pair_grads((szb, s5b), (gsave_z, gzb), gp_z)
    outz_in = along_z(gp_z, gp, 8)
    near(1)

    arrive_all(fwd_in)
    pairs_apply(dot, (0, 1), syb, mats_y, s7b, qsend)
    query_in = along_y(qsend, qmid)
    mark("fwd_y")
    pair_grads((syb, s7b), (gsave_y, gyb), gp_y)
    outy_in = along_y(gp_y, gp_mid)
    mark("grads")

    near(3)
    class Slabs:
        def __init__(self, start, size, sums_ref, slab_ref):
            self.start, self.size = start, size
            self.sums_ref, self.slab_ref = sums_ref, slab_ref
            self.ins, self.outs = [], []

        def rows(self, dev):
            return pl.ds(pl.multiple_of(self.start + dev * self.size, 32), self.size)

        def scatter(self):
            first, count = self.start // 128, 16 * self.size // 128
            for i in range(first, first + count):
                gpf[pl.ds(i * 128, 128)] = gp[i]
                gpb[pl.ds(i * 128, 128)] = gp[i].astype(BF16)
            for d in range(1, n_dp):
                dev = lax.rem(my_dp + d, n_dp)
                self.ins.append(send(gpb.at[self.rows(dev)], self.sums_ref.at[d], dev, "dp"))

        def gather(self):
            total = gpf[self.rows(my_dp)]
            for d, c in zip(range(1, n_dp), self.ins):
                c.arrive()
                total = total + self.sums_ref[d].astype(F32)
            self.slab_ref[...] = total * scale
            for d in range(1, n_dp):
                dev = lax.rem(my_dp + d, n_dp)
                self.outs.append(send(self.slab_ref, gout.at[self.rows(my_dp)], dev, "dp"))
            gout[self.rows(my_dp)] = self.slab_ref[...]

        def finish(self):
            for c in self.outs:
                c.arrive()

    early, late = Slabs(0, 96, sums_a, slab_a), Slabs(1536, 32, sums_b, slab_b)
    arrive_all(outy_in)
    outy_in = along_z(gp_mid, gp, 12)
    arrive_all(query_in)
    query_in = along_z(qmid, qb)
    arrive_all(outz_in)
    if n_dp > 1:
        early.scatter()
    near(0)
    for s in sums:
        s.last_far()
    mark("near2")
    arrive_all(outy_in)
    if n_dp > 1:
        late.scatter()
        early.gather()
    for s in sums:
        s.last_near()
    mark("last_near")
    if n_dp > 1:
        late.gather()
    mark("dp")

    arrive_all(query_in)
    for c in range(4):
        query[:, c * LANES : (c + 1) * LANES] = qb[c]
    mark("query")
    for s in sums:
        s.end()
    mark("igrad")
    if n_dp > 1:
        early.finish()
        late.finish()
    for pair in range(4):
        for c in range(4):
            i = pair * 4 + c
            value = gout[pl.ds(i * 128, 128)] if n_dp > 1 else gp[i]
            for j in range(2):
                ggrad[2 * pair + j, :, c * LANES : (c + 1) * LANES] = value[j * 64 : j * 64 + 64]


def main_call(hidden, weight, generators, cotangent, n_dp=1, scale=1.0):
    tokens = hidden.shape[0]
    vm = lambda *shape, dtype=BF16: pltpu.VMEM(shape, dtype)
    chunks = vm(4, tokens, LANES)
    block = vm(tokens, 512)
    blocks = vm(4, tokens, 512)
    flops = 4 * tokens * 8192 * 512
    return pl.pallas_call(
        functools.partial(main_kernel, n_dp, scale),
        out_shape=(
            jax.ShapeDtypeStruct((tokens, 512), BF16),
            jax.ShapeDtypeStruct((tokens, 512), BF16),
            jax.ShapeDtypeStruct((8, 64, 512), F32),
        ),
        in_specs=[
            pl.BlockSpec(memory_space=pltpu.VMEM),
            pl.BlockSpec(memory_space=pl.ANY),
            pl.BlockSpec(memory_space=pltpu.VMEM),
            pl.BlockSpec(memory_space=pltpu.VMEM),
        ],
        out_specs=[pl.BlockSpec(memory_space=pltpu.VMEM)] * 3,
        scratch_shapes=[
            vm(8192, 512),
            vm(4, 4, tokens, 512),
            vm(tokens, 512, dtype=F32),
            vm(4, 4, tokens, 512, dtype=F32),
            vm(4, 2, 64, LANES, dtype=F32),
            vm(4, 2, 64, LANES, dtype=F32),
            chunks, chunks, chunks, chunks, chunks, chunks,
            vm(4, 2, tokens, 256),
            vm(4, 2, tokens, 256),
            chunks, chunks, chunks, chunks, chunks,
            chunks, chunks, chunks, chunks, chunks,
            block,
            blocks, blocks, blocks, blocks, blocks, blocks,
            block, block, block, block, block, block,
            vm(16, 128, 128, dtype=F32),
            vm(4, 128, 128, dtype=F32),
            vm(4, 128, 128, dtype=F32),
            vm(4, 128, 128, dtype=F32),
            vm(2048, 128, dtype=F32),
            vm(2048, 128),
            vm(16, 96, 128),
            vm(16, 32, 128),
            vm(96, 128, dtype=F32),
            vm(32, 128, dtype=F32),
            vm(2048, 128, dtype=F32),
            vm(5, 2, 2, 256, 256),
            vm(2, 2, 2, 256, 256),
            vm(2, 2, 2, 256, 256),
            pltpu.SemaphoreType.DMA((N_SEMS,)),
            pltpu.SemaphoreType.DMA((N_SEMS,)),
            pltpu.SemaphoreType.DMA,
        ],
        compiler_params=pltpu.CompilerParams(
            collective_id=0, has_side_effects=True, vmem_limit_bytes=VMEM_BYTES
        ),
        cost_estimate=pl.CostEstimate(
            flops=flops, bytes_accessed=12 * 1024 * 1024, transcendentals=0
        ),
        name="adapt",
    )(hidden, weight, generators, cotangent)


def copy_kernel(*refs):
    count = len(refs) // 2
    for source, target in zip(refs[:count], refs[count:]):
        target[...] = source[...]


def copy_call(*arrays):
    whole = pl.BlockSpec(memory_space=pltpu.VMEM)
    return pl.pallas_call(
        copy_kernel,
        out_shape=tuple(jax.ShapeDtypeStruct(a.shape, a.dtype) for a in arrays),
        in_specs=[whole] * len(arrays),
        out_specs=[whole] * len(arrays),
        name="results",
    )(*arrays)


def on_device(hidden, base_weight, generators, cotangent):
    n = lax.axis_size("dp")
    scale = 1.0 / math.sqrt(hidden.shape[0] * n)
    return copy_call(*main_call(hidden, base_weight, generators, cotangent, n, scale))


def solution(mesh):
    placed = (P("dp", "tensor"), P(None, "tensor"), P(None, None, "tensor"), P("dp", "tensor"))
    return jax.shard_map(
        on_device,
        mesh=mesh,
        in_specs=placed,
        out_specs=(P("dp", "tensor"), P("dp", "tensor"), P(None, None, "tensor")),
        check_vma=False,
    )
```

```python
import functools
import math

import jax
import jax.numpy as jnp
from jax import lax
from jax.experimental import pallas as pl
from jax.experimental.pallas import tpu as pltpu
from jax.sharding import PartitionSpec as P

MESH = pl.DeviceIdType.MESH
F32 = jnp.float32
BF16 = jnp.bfloat16
SIDE = 4
LANES = 128
HALF = 32
VMEM_BYTES = 60 * 1024 * 1024


def wrap(value, n):
    return lax.rem(value + n, n)


def dot(a, b):
    return jnp.dot(a, b, preferred_element_type=F32)


def dot_nt(a, b):
    return lax.dot_general(a, b, (((1,), (1,)), ((), ())), preferred_element_type=F32)


def dot_tn(a, b):
    return lax.dot_general(a, b, (((0,), (0,)), ((), ())), preferred_element_type=F32)


def split(value):
    high = value.astype(BF16)
    return high, (value - high.astype(F32)).astype(BF16)


def put_split(ref, index, value):
    ref[(*index, 0)], ref[(*index, 1)] = split(value)


def mix(product, value, ref, index):
    top, rest = ref[(*index, 0)], ref[(*index, 1)]
    if value.dtype == BF16:
        return product(value, top) + product(value, rest)
    high, low = split(value)
    return product(high, top) + product(low, top) + product(high, rest)


def groups_of(shape):
    rows = lax.broadcasted_iota(jnp.int32, shape, 0) >> 5
    cols = lax.broadcasted_iota(jnp.int32, shape, 1) >> 5
    return rows, cols


def spread(block, mask, copies):
    return jnp.where(mask, jnp.concatenate([block] * copies, axis=0), 0.0)


def pair_matrix(gen_a, gen_b):
    both = jnp.concatenate([gen_a, gen_b], axis=1)
    rows, cols = groups_of((LANES, 2 * LANES))
    mask = rows == (cols & 3)
    return jnp.concatenate([spread(both[:HALF], mask, 4), spread(both[HALF:], mask, 4)], axis=0)


def pair_extract(grad):
    cols = (lax.broadcasted_iota(jnp.int32, (HALF, 2 * LANES), 1) >> 5) & 3
    parts = []
    for h in range(2):
        total = jnp.zeros((HALF, 2 * LANES), F32)
        for g in range(4):
            start = h * LANES + g * HALF
            total = total + jnp.where(cols == g, grad[start : start + HALF], 0.0)
        parts.append(total)
    return jnp.concatenate(parts, axis=0)


def near_matrix(gen, k):
    rows, cols = groups_of((256, 256))
    low = cols & ~(1 << k)
    return spread(gen[:HALF], rows == low, 8) + spread(gen[HALF:], rows == (low | (1 << k)), 8)


def near_extract(grad, k):
    cols = lax.broadcasted_iota(jnp.int32, (HALF, 256), 1) >> 5
    low = cols & ~(1 << k)
    parts = []
    for want in (low, low | (1 << k)):
        total = jnp.zeros((HALF, 256), F32)
        for g in range(8):
            total = total + jnp.where(want == g, grad[g * HALF : (g + 1) * HALF], 0.0)
        parts.append(total)
    return jnp.concatenate(parts, axis=0)


def diag_matrix(block):
    rows, cols = groups_of((256, 256))
    return spread(block, rows == cols, 8)


def diag_extract(grad):
    cols = lax.broadcasted_iota(jnp.int32, (HALF, 256), 1) >> 5
    total = jnp.zeros((HALF, 256), F32)
    for g in range(8):
        total = total + jnp.where(cols == g, grad[g * HALF : (g + 1) * HALF], 0.0)
    return total


PAIRS = (((0, 1), (2, 3)), ((0, 2), (1, 3)))
N_SEMS = 320
GATHER = (("z", "y", 0, 160), ("z", "y", 160, 320), ("y", "z", 320, 384))
SUM = (("y", "z", 0, 160), ("y", "z", 160, 320), ("z", "y", 320, 384))
STOP = None


def parts_of(table, tokens):
    scaled = [(a, b, lo * tokens // 384 // 32 * 32, hi * tokens // 384 // 32 * 32) for a, b, lo, hi in table]
    return [part for part in scaled if part[2] < part[3]]


class Stop(Exception):
    pass


class Sent:
    def __init__(self, copy):
        self.copy, self.received = copy, False

    def arrive(self):
        if not self.received:
            self.copy.wait_recv()
            self.received = True


def main_kernel(n_dp, scale, *refs):
    pending, endings = [], []
    try:
        main_body(n_dp, scale, pending, endings, *refs)
    except Stop:
        pass
    for c in pending:
        c.arrive()
        c.copy.wait_send()
    for end in endings:
        end()


def main_body(
    n_dp, scale, pending, endings,
    hid, wt, gen, cot, query, igrad, ggrad,
    w_v, hbuf, base, pb, gz, gy, gyb, gzb, ghome, gsave_y, gsave_z, gmid, cotc, genc, glocal, slocal,
    szb, ssend, syb, qsend, qb, s5b, s7b, zsend, gsend_t, gsend_z, gb,
    rs_s2, rs_r2, rs_s1, rs_s3, rs_r1, rs_r3, q_s2, q_r2, q_s1, q_s3, q_r1, q_r3,
    gp, gp_z, gp_y, gpb, sums_a, sums_b, slab_a, slab_b, gout, mats_loc, mats_z, mats_y,
    send_sem, recv_sem, w_sem,
):
    tokens = hid.shape[0]
    me = lax.axis_index("tensor")
    my_dp = lax.axis_index("dp")
    y, z = me // SIDE, lax.rem(me, SIDE)
    z_of = lax.rem(y + z, SIDE)
    counter = [0]

    def mark(name):
        if STOP == name:
            if name == "bwd_y":
                w_copy.wait()
            raise Stop

    def at(dy, dz):
        return wrap(y + dy, SIDE) * SIDE + wrap(z + dz, SIDE)

    def toward(axis, step):
        return at(step, 0) if axis == "y" else at(0, step)

    def place(axis, step, fixed):
        return (step, fixed) if axis == "y" else (fixed, step)

    def ids(n=1):
        first = counter[0]
        counter[0] += n
        return first

    def copy(src, dst, send_index, recv_index, device):
        return pltpu.make_async_remote_copy(
            src_ref=src,
            dst_ref=dst,
            send_sem=send_sem.at[send_index],
            recv_sem=recv_sem.at[recv_index],
            device_id=device,
            device_id_type=MESH,
        )

    def send(src, dst, dev, axis="tensor"):
        index = ids()
        c = copy(src, dst, index, index, {axis: dev})
        c.start()
        c = Sent(c)
        pending.append(c)
        return c

    def w_rows(dy, dz):
        return w_v[pl.ds(pl.multiple_of(at(dy, dz) * 512, 512), 512), :]

    w_copy = pltpu.make_async_copy(wt, w_v, w_sem)
    for c in range(4):
        cols = slice(c * LANES, (c + 1) * LANES)
        cotc[c] = cot[:, cols]
        genc[c] = gen[4:8, :, cols]

    barrier = pltpu.get_barrier_semaphore()
    for d in range(1, 16):
        pl.semaphore_signal(
            barrier, inc=1, device_id={"tensor": lax.rem(me + d, 16)}, device_id_type=MESH
        )
    for d in range(1, n_dp):
        pl.semaphore_signal(
            barrier, inc=1, device_id={"dp": lax.rem(my_dp + d, n_dp)}, device_id_type=MESH
        )
    pl.semaphore_wait(barrier, 15 + n_dp - 1)

    cot_in, genz_in, geny_in = [], [], []
    for d in range(1, 4):
        c = lax.rem(y + d + z, SIDE)
        cot_in.append(send(cotc.at[c], gyb.at[y], at(d, 0)))
        geny_in.append(send(genc.at[c, pl.ds(2, 2)], gy.at[y], at(d, 0)))

    def held(dy, dz, lo, hi):
        ref = hid if (dy, dz) == (0, 0) else hbuf.at[dy, dz]
        return ref.at[pl.ds(lo, hi - lo)]

    arrivals = {(dy, dz): [] for dy in range(4) for dz in range(4)}

    def hop(axis, fixed, step, sign, lo, hi):
        target = place(axis, step + sign & 3, fixed)
        c = send(
            held(*place(axis, step, fixed), lo, hi),
            hbuf.at[(*target, pl.ds(lo, hi - lo))],
            toward(axis, sign),
        )
        arrivals[target].append(c)
        return c

    def ring_start(axis, fixed, lo, hi):
        return [hop(axis, fixed, 0, 1, lo, hi), hop(axis, fixed, 0, -1, lo, hi)]

    def ring_forward(axis, fixed, lo, hi, copies):
        middle = (lo + hi) // 2
        copies[0].arrive()
        copies.append(hop(axis, fixed, 1, 1, lo, middle))
        copies[1].arrive()
        copies.append(hop(axis, fixed, 3, -1, middle, hi))

    routes = parts_of(GATHER, tokens)
    first = [ring_start(a, 0, lo, hi) for a, _, lo, hi in routes]
    second = [{0: ring_start(b, 0, lo, hi)} for _, b, lo, hi in routes]
    for d in range(1, 4):
        genz_in.append(send(genc.at[wrap(z + d, SIDE), pl.ds(0, 2)], gz.at[z], at(0, d)))

    w_copy.start()

    def gather_second(step):
        for (_, b, lo, hi), copies in zip(routes, second):
            ring_forward(b, step, lo, hi, copies[step])

    def gather_first():
        for (a, b, lo, hi), ring, copies in zip(routes, first, second):
            middle = (lo + hi) // 2
            ring[0].arrive()
            ring.append(hop(a, 0, 1, 1, lo, middle))
            copies[1] = ring_start(b, 1, lo, hi)
            ring[1].arrive()
            ring.append(hop(a, 0, 3, -1, middle, hi))
            copies[3] = ring_start(b, 3, lo, hi)

    def gather_far():
        for (_, b, lo, hi), ring, copies in zip(routes, first, second):
            ring[2].arrive()
            ring[3].arrive()
            copies[2] = ring_start(b, 2, lo, hi)

    def accumulate(*blocks):
        for dy, dz in blocks:
            for c in arrivals[dy, dz]:
                c.arrive()
            base[...] += dot(hbuf[dy, dz], w_rows(-dy, -dz))

    gyb[y] = cotc[z_of]
    gy[y] = genc[z_of, 2:4]
    gz[z] = genc[z, 0:2]

    for k in range(3):
        for s in range(2):
            put_split(mats_loc, (k, s), near_matrix(gen[k, :, 256 * s : 256 * s + 256], k))
    for s in range(2):
        for h in range(2):
            block = gen[3, HALF * h : HALF * h + HALF, 256 * s : 256 * s + 256]
            put_split(mats_loc, (3 + h, s), diag_matrix(block))

    def pair_of(ref, a, b):
        return jnp.concatenate([ref[a], ref[b]], axis=1)

    def fill_pairs(mats, gens):
        for k in range(2):
            for i, (a, b) in enumerate(PAIRS[k]):
                put_split(mats, (k, i), pair_matrix(gens[a, k], gens[b, k]))

    def pairs_apply(product, order, source, mats, save, out):
        values = None
        for k, target in zip(order, (save, out)):
            new = [None] * 4
            for i, (a, b) in enumerate(PAIRS[k]):
                if values is None:
                    v = pair_of(source, a, b)
                else:
                    v = jnp.concatenate([values[a], values[b]], axis=1)
                v = v.astype(F32) + mix(product, v, mats, (k, i))
                new[a], new[b] = v[:, :LANES], v[:, LANES:]
            values = new
            for m in range(4):
                target[m] = values[m].astype(BF16)

    def cross(src, dst, own_slot, dev_of, src_of):
        index = ids(4)
        sent = []
        for d in range(4):
            c = copy(
                src.at[src_of(d)], dst.at[own_slot], index + d, index + own_slot,
                {"tensor": dev_of(d)},
            )
            if d == 0:
                keep = pltpu.make_async_copy(
                    src.at[src_of(0)], dst.at[own_slot], recv_sem.at[index + own_slot]
                )
                pl.when(dev_of(0) != me)(lambda c=c: c.start())
                pl.when(dev_of(0) == me)(lambda keep=keep: keep.start())
            else:
                c.start()
            sent.append(c)
        done = []

        def arrive():
            if not done:
                done.append(True)
                for m in range(4):
                    pltpu.make_async_copy(src.at[m], dst.at[m], recv_sem.at[index + m]).wait()

        def finish():
            arrive()
            pl.when(dev_of(0) != me)(lambda: sent[0].wait_send())
            for c in sent[1:]:
                c.wait_send()

        endings.append(finish)
        return arrive

    for c in geny_in:
        c.arrive()
    fill_pairs(mats_y, gy)
    for c in cot_in:
        c.arrive()
    pairs_apply(dot_nt, (1, 0), gyb, mats_y, gsave_y, gsend_t)
    step_in = []
    for d in range(1, 4):
        step_in.append(send(gsend_t.at[wrap(y + d, SIDE)], gmid.at[z_of], at(d, 0)))
    gmid[z_of] = gsend_t[y]
    mark("bwd_y")

    gather_second(0)
    for c in genz_in:
        c.arrive()
    fill_pairs(mats_z, gz)
    for c in step_in:
        c.arrive()
    step_in = []
    for d in range(1, 4):
        step_in.append(send(gmid.at[wrap(z + d, SIDE)], gzb.at[z], at(0, d)))
    gzb[z] = gmid[z]
    w_copy.wait()
    base[...] = dot(hid[...], w_rows(0, 0))
    mark("ag0")

    gather_first()
    mark("ag1")
    for c in step_in:
        c.arrive()
    pairs_apply(dot_nt, (1, 0), gzb, mats_z, gsave_z, gsend_z)
    back_in = []
    for d in range(1, 4):
        back_in.append(send(gsend_z.at[wrap(z + d, SIDE)], ghome.at[z], at(0, d)))
    ghome[z] = gsend_z[z]
    mark("bwd_z")

    gather_far()
    accumulate((1, 0), (3, 0), (0, 1), (0, 3))
    gather_second(1)
    gather_second(3)
    accumulate((2, 0), (0, 2), (1, 1), (3, 1))
    mark("ag2")

    for c in back_in:
        c.arrive()
    ga = pair_of(ghome, 0, 1)
    gc = pair_of(ghome, 2, 3)
    glocal[3, 0], glocal[3, 1] = ga, gc
    fa = ga.astype(F32) + mix(dot_nt, ga, mats_loc, (3, 0)) + mix(dot_nt, gc, mats_loc, (3, 1))
    fb = gc.astype(F32) + mix(dot_nt, ga, mats_loc, (4, 0)) + mix(dot_nt, gc, mats_loc, (4, 1))
    for k in (2, 1, 0):
        glocal[k, 0], glocal[k, 1] = fa.astype(BF16), fb.astype(BF16)
        fa = fa + mix(dot_nt, fa, mats_loc, (k, 0))
        fb = fb + mix(dot_nt, fb, mats_loc, (k, 1))
    gb[:, :256] = fa.astype(BF16)
    gb[:, 256:] = fb.astype(BF16)
    mark("bwd_local")

    gather_second(2)
    mark("ag3")

    computed = set()

    def partial(dy, dz, lo, hi):
        if (dy, dz) not in computed:
            computed.add((dy, dz))
            pb[dy, dz] = dot_nt(gb[...], w_rows(dy, dz))
        return pb[dy, dz, lo:hi]

    class Sum:
        def __init__(self, a, b, lo, hi):
            self.a, self.b, self.lo, self.hi, self.middle = a, b, lo, hi, (lo + hi) // 2
            self.copies, self.last = {}, []
            self.rows = pl.ds(lo, hi - lo)
            self.top, self.low = pl.ds(lo, self.middle - lo), pl.ds(self.middle, hi - self.middle)

        def far(self, fixed):
            block = partial(*place(self.a, 2, fixed), self.lo, self.hi)
            rs_s2[fixed, self.rows] = block.astype(BF16)
            self.copies[fixed] = [
                send(rs_s2.at[fixed, self.top], rs_r2.at[fixed, self.top], toward(self.a, 1)),
                send(rs_s2.at[fixed, self.low], rs_r2.at[fixed, self.low], toward(self.a, -1)),
            ]

        def near(self, fixed):
            cs, size = self.copies[fixed], self.middle - self.lo
            p = partial(*place(self.a, 1, fixed), self.lo, self.hi)
            cs[0].arrive()
            rs_s1[fixed, self.top] = (p[:size] + rs_r2[fixed, self.top].astype(F32)).astype(BF16)
            rs_s1[fixed, self.low] = p[size:].astype(BF16)
            cs.append(
                send(rs_s1.at[fixed, self.rows], rs_r1.at[fixed, self.rows], toward(self.a, 1))
            )
            p = partial(*place(self.a, 3, fixed), self.lo, self.hi)
            cs[1].arrive()
            rs_s3[fixed, self.top] = p[:size].astype(BF16)
            rs_s3[fixed, self.low] = (p[size:] + rs_r2[fixed, self.low].astype(F32)).astype(BF16)
            cs.append(
                send(rs_s3.at[fixed, self.rows], rs_r3.at[fixed, self.rows], toward(self.a, -1))
            )

        def whole(self, fixed):
            p = partial(*place(self.a, 0, fixed), self.lo, self.hi)
            for c in self.copies[fixed][2:]:
                c.arrive()
            return p + rs_r1[fixed, self.rows].astype(F32) + rs_r3[fixed, self.rows].astype(F32)

        def last_far(self):
            q_s2[self.rows] = self.whole(2).astype(BF16)
            self.last = [
                send(q_s2.at[self.top], q_r2.at[self.top], toward(self.b, 1)),
                send(q_s2.at[self.low], q_r2.at[self.low], toward(self.b, -1)),
            ]

        def last_near(self):
            size = self.middle - self.lo
            q = self.whole(1)
            self.last[0].arrive()
            q_s1[self.top] = (q[:size] + q_r2[self.top].astype(F32)).astype(BF16)
            q_s1[self.low] = q[size:].astype(BF16)
            self.last.append(send(q_s1.at[self.rows], q_r1.at[self.rows], toward(self.b, 1)))
            q = self.whole(3)
            self.last[1].arrive()
            q_s3[self.top] = q[:size].astype(BF16)
            q_s3[self.low] = (q[size:] + q_r2[self.low].astype(F32)).astype(BF16)
            self.last.append(send(q_s3.at[self.rows], q_r3.at[self.rows], toward(self.b, -1)))

        def end(self):
            q = self.whole(0)
            for c in self.last[2:]:
                c.arrive()
            q = q + q_r1[self.rows].astype(F32) + q_r3[self.rows].astype(F32)
            igrad[self.rows] = q.astype(BF16)

    sums = [Sum(*part) for part in parts_of(SUM, tokens)]
    def far(group, *blocks):
        for fixed in blocks:
            for s in group:
                s.far(fixed)

    def near(group, *blocks):
        for fixed in blocks:
            for s in group:
                s.near(fixed)

    far(sums, 2, 1, 3, 0)
    mark("rs_far")
    accumulate((1, 3), (3, 3), (1, 2), (3, 2))

    accumulate((2, 1), (2, 3), (2, 2))
    mark("base")
    fa, fb = base[:, :256], base[:, 256:]
    for k in range(3):
        slocal[k, 0], slocal[k, 1] = fa.astype(BF16), fb.astype(BF16)
        fa = fa + mix(dot, fa, mats_loc, (k, 0))
        fb = fb + mix(dot, fb, mats_loc, (k, 1))
    slocal[3, 0], slocal[3, 1] = fa.astype(BF16), fb.astype(BF16)
    fc = fa + mix(dot, fa, mats_loc, (3, 0)) + mix(dot, fb, mats_loc, (4, 0))
    fd = fb + mix(dot, fa, mats_loc, (3, 1)) + mix(dot, fb, mats_loc, (4, 1))
    for c in range(4):
        side = fc if c < 2 else fd
        ssend[c] = side[:, (c % 2) * LANES : (c % 2) * LANES + LANES].astype(BF16)
    fwd_in = []
    for d in range(1, 4):
        fwd_in.append(send(ssend.at[wrap(z + d, SIDE)], szb.at[z], at(0, d)))
    szb[z] = ssend[z]
    mark("fwd_local")

    near(sums, 2, 1)
    mark("near1")

    def put_local(k, s, value):
        for j in range(2):
            gp[pl.ds(((k // 2) * 4 + 2 * s + j) * 128 + (k % 2) * 64, 64)] = value[
                :, j * LANES : (j + 1) * LANES
            ]

    for k in range(3):
        for s in range(2):
            put_local(k, s, near_extract(dot_tn(slocal[k, s], glocal[k, s]), k))
    for s in range(2):
        put_local(
            3, s,
            jnp.concatenate(
                [diag_extract(dot_tn(slocal[3, h], glocal[3, s])) for h in range(2)], axis=0
            ),
        )

    for c in fwd_in:
        c.arrive()
    pairs_apply(dot, (0, 1), szb, mats_z, s5b, zsend)
    fwd_arrive = cross(
        zsend, syb, y,
        lambda d: ((SIDE - d) % SIDE) * SIDE + wrap(z + d, SIDE),
        lambda d: wrap(z + d, SIDE),
    )
    mark("fwd_z")
    near(sums, 3, 0)
    for s in sums:
        s.last_far()
    mark("near2")

    def pair_grads(states, grads, dst):
        for k in range(2):
            for i, (a, b) in enumerate(PAIRS[k]):
                value = pair_extract(dot_tn(pair_of(states[k], a, b), pair_of(grads[k], a, b)))
                dst[a, k * 64 : k * 64 + 64] = value[:, :LANES]
                dst[b, k * 64 : k * 64 + 64] = value[:, LANES:]

    def piece(index):
        return pl.ds(pl.multiple_of(index * 128, 128), 128)

    pair_grads((szb, s5b), (gsave_z, gzb), gp_z)
    outz_in = []
    for d in range(1, 4):
        outz_in.append(send(gp_z.at[wrap(z + d, SIDE)], gp.at[piece(8 + z)], at(0, d)))
    gp[piece(8 + z)] = gp_z[z]

    fwd_arrive()
    pairs_apply(dot, (0, 1), syb, mats_y, s7b, qsend)
    query_in = []
    for d in range(1, 4):
        query_in.append(send(qsend.at[wrap(y + d, SIDE)], qb.at[z_of], at(d, 0)))
    qb[z_of] = qsend[y]
    mark("fwd_y")

    pair_grads((syb, s7b), (gsave_y, gyb), gp_y)
    outy_in = []
    for d in range(1, 4):
        outy_in.append(send(gp_y.at[wrap(y + d, SIDE)], gp.at[piece(12 + z_of)], at(d, 0)))
    gp[piece(12 + z_of)] = gp_y[y]
    mark("grads")

    class Slabs:
        def __init__(self, start, size, sums_ref, slab_ref):
            self.start, self.size = start, size
            self.sums_ref, self.slab_ref = sums_ref, slab_ref
            self.ins, self.outs = [], []

        def rows(self, dev):
            return pl.ds(pl.multiple_of(self.start + dev * self.size, 32), self.size)

        def scatter(self):
            all_rows = pl.ds(self.start, 16 * self.size)
            gpb[all_rows] = gp[all_rows].astype(BF16)
            for d in range(1, n_dp):
                dev = lax.rem(my_dp + d, n_dp)
                self.ins.append(send(gpb.at[self.rows(dev)], self.sums_ref.at[d], dev, "dp"))

        def gather(self):
            total = gp[self.rows(my_dp)]
            for d, c in zip(range(1, n_dp), self.ins):
                c.arrive()
                total = total + self.sums_ref[d].astype(F32)
            self.slab_ref[...] = (total * scale).astype(BF16)
            for d in range(1, n_dp):
                dev = lax.rem(my_dp + d, n_dp)
                self.outs.append(send(self.slab_ref, gout.at[self.rows(my_dp)], dev, "dp"))
            gout[self.rows(my_dp)] = self.slab_ref[...]

        def finish(self):
            for c in self.outs:
                c.arrive()

    early, late = Slabs(0, 96, sums_a, slab_a), Slabs(1536, 32, sums_b, slab_b)
    for c in outz_in:
        c.arrive()
    if n_dp > 1:
        early.scatter()
    for s in sums:
        s.last_near()
    mark("last_near")
    for c in outy_in:
        c.arrive()
    if n_dp > 1:
        late.scatter()
        early.gather()
        late.gather()
    mark("dp")

    for c in query_in:
        c.arrive()
    for c in range(4):
        query[:, c * LANES : (c + 1) * LANES] = qb[c]
    mark("query")
    for s in sums:
        s.end()
    mark("igrad")
    if n_dp > 1:
        early.finish()
        late.finish()
    final = gout if n_dp > 1 else gp
    for pair in range(4):
        for c in range(4):
            value = final[pl.ds((pair * 4 + c) * 128, 128)].astype(F32)
            for j in range(2):
                ggrad[2 * pair + j, :, c * LANES : (c + 1) * LANES] = value[j * 64 : j * 64 + 64]


def main_call(hidden, weight, generators, cotangent, n_dp=1, scale=1.0):
    tokens = hidden.shape[0]
    vm = lambda *shape, dtype=BF16: pltpu.VMEM(shape, dtype)
    chunks = vm(4, tokens, LANES)
    block = vm(tokens, 512)
    blocks = vm(4, tokens, 512)
    flops = 4 * tokens * 8192 * 512
    return pl.pallas_call(
        functools.partial(main_kernel, n_dp, scale),
        out_shape=(
            jax.ShapeDtypeStruct((tokens, 512), BF16),
            jax.ShapeDtypeStruct((tokens, 512), BF16),
            jax.ShapeDtypeStruct((8, 64, 512), F32),
        ),
        in_specs=[
            pl.BlockSpec(memory_space=pltpu.VMEM),
            pl.BlockSpec(memory_space=pl.ANY),
            pl.BlockSpec(memory_space=pltpu.VMEM),
            pl.BlockSpec(memory_space=pltpu.VMEM),
        ],
        out_specs=[pl.BlockSpec(memory_space=pltpu.VMEM)] * 3,
        scratch_shapes=[
            vm(8192, 512),
            vm(4, 4, tokens, 512),
            vm(tokens, 512, dtype=F32),
            vm(4, 4, tokens, 512, dtype=F32),
            vm(4, 2, 64, LANES, dtype=F32),
            vm(4, 2, 64, LANES, dtype=F32),
            chunks, chunks, chunks, chunks, chunks, chunks,
            chunks, vm(4, 4, 64, LANES, dtype=F32),
            vm(4, 2, tokens, 256),
            vm(4, 2, tokens, 256),
            chunks, chunks, chunks, chunks, chunks,
            chunks, chunks, chunks, chunks, chunks,
            block,
            blocks, blocks, blocks, blocks, blocks, blocks,
            block, block, block, block, block, block,
            vm(2048, 128, dtype=F32),
            vm(4, 128, 128, dtype=F32),
            vm(4, 128, 128, dtype=F32),
            vm(2048, 128),
            vm(16, 96, 128),
            vm(16, 32, 128),
            vm(96, 128),
            vm(32, 128),
            vm(2048, 128),
            vm(5, 2, 2, 256, 256),
            vm(2, 2, 2, 256, 256),
            vm(2, 2, 2, 256, 256),
            pltpu.SemaphoreType.DMA((N_SEMS,)),
            pltpu.SemaphoreType.DMA((N_SEMS,)),
            pltpu.SemaphoreType.DMA,
        ],
        compiler_params=pltpu.CompilerParams(
            collective_id=0, has_side_effects=True, vmem_limit_bytes=VMEM_BYTES
        ),
        cost_estimate=pl.CostEstimate(
            flops=flops, bytes_accessed=12 * 1024 * 1024, transcendentals=0
        ),
        name="adapt",
    )(hidden, weight, generators, cotangent)


def copy_kernel(*refs):
    count = len(refs) // 2
    for source, target in zip(refs[:count], refs[count:]):
        target[...] = source[...]


def copy_call(*arrays):
    whole = pl.BlockSpec(memory_space=pltpu.VMEM)
    return pl.pallas_call(
        copy_kernel,
        out_shape=tuple(jax.ShapeDtypeStruct(a.shape, a.dtype) for a in arrays),
        in_specs=[whole] * len(arrays),
        out_specs=[whole] * len(arrays),
        name="results",
    )(*arrays)


def on_device(hidden, base_weight, generators, cotangent):
    n = lax.axis_size("dp")
    scale = 1.0 / math.sqrt(hidden.shape[0] * n)
    return copy_call(*main_call(hidden, base_weight, generators, cotangent, n, scale))


def solution(mesh):
    placed = (P("dp", "tensor"), P(None, "tensor"), P(None, None, "tensor"), P("dp", "tensor"))
    return jax.shard_map(
        on_device,
        mesh=mesh,
        in_specs=placed,
        out_specs=(P("dp", "tensor"), P("dp", "tensor"), P(None, None, "tensor")),
        check_vma=False,
    )
```

```python
import functools
import math

import jax
import jax.numpy as jnp
from jax import lax
from jax.experimental import pallas as pl
from jax.experimental.pallas import tpu as pltpu
from jax.sharding import PartitionSpec as P

MESH = pl.DeviceIdType.MESH
F32 = jnp.float32
BF16 = jnp.bfloat16
SIDE = 4
LANES = 128
HALF = 32
VMEM_BYTES = 60 * 1024 * 1024


def wrap(value, n):
    return lax.rem(value + n, n)


def dot(a, b):
    return jnp.dot(a, b, preferred_element_type=F32)


def dot_nt(a, b):
    return lax.dot_general(a, b, (((1,), (1,)), ((), ())), preferred_element_type=F32)


def dot_tn(a, b):
    return lax.dot_general(a, b, (((0,), (0,)), ((), ())), preferred_element_type=F32)


def split(value):
    high = value.astype(BF16)
    return high, (value - high.astype(F32)).astype(BF16)


def put_split(ref, index, value):
    ref[(*index, 0)], ref[(*index, 1)] = split(value)


def mix(product, value, ref, index):
    top, rest = ref[(*index, 0)], ref[(*index, 1)]
    if value.dtype == BF16:
        return product(value, top) + product(value, rest)
    high, low = split(value)
    return product(high, top) + product(low, top) + product(high, rest)


def groups_of(shape):
    rows = lax.broadcasted_iota(jnp.int32, shape, 0) >> 5
    cols = lax.broadcasted_iota(jnp.int32, shape, 1) >> 5
    return rows, cols


def spread(block, mask, copies):
    return jnp.where(mask, jnp.concatenate([block] * copies, axis=0), 0.0)


def pair_matrix(gen_a, gen_b):
    both = jnp.concatenate([gen_a, gen_b], axis=1)
    rows, cols = groups_of((LANES, 2 * LANES))
    mask = rows == (cols & 3)
    return jnp.concatenate([spread(both[:HALF], mask, 4), spread(both[HALF:], mask, 4)], axis=0)


def pair_extract(grad):
    cols = (lax.broadcasted_iota(jnp.int32, (HALF, 2 * LANES), 1) >> 5) & 3
    parts = []
    for h in range(2):
        total = jnp.zeros((HALF, 2 * LANES), F32)
        for g in range(4):
            start = h * LANES + g * HALF
            total = total + jnp.where(cols == g, grad[start : start + HALF], 0.0)
        parts.append(total)
    return jnp.concatenate(parts, axis=0)


def near_matrix(gen, k):
    rows, cols = groups_of((256, 256))
    low = cols & ~(1 << k)
    return spread(gen[:HALF], rows == low, 8) + spread(gen[HALF:], rows == (low | (1 << k)), 8)


def near_extract(grad, k):
    cols = lax.broadcasted_iota(jnp.int32, (HALF, 256), 1) >> 5
    low = cols & ~(1 << k)
    parts = []
    for want in (low, low | (1 << k)):
        total = jnp.zeros((HALF, 256), F32)
        for g in range(8):
            total = total + jnp.where(want == g, grad[g * HALF : (g + 1) * HALF], 0.0)
        parts.append(total)
    return jnp.concatenate(parts, axis=0)


def diag_matrix(block):
    rows, cols = groups_of((256, 256))
    return spread(block, rows == cols, 8)


def diag_extract(grad):
    cols = lax.broadcasted_iota(jnp.int32, (HALF, 256), 1) >> 5
    total = jnp.zeros((HALF, 256), F32)
    for g in range(8):
        total = total + jnp.where(cols == g, grad[g * HALF : (g + 1) * HALF], 0.0)
    return total


PAIRS = (((0, 1), (2, 3)), ((0, 2), (1, 3)))
N_SEMS = 320
GATHER = (("z", "y", 0, 160), ("z", "y", 160, 352), ("y", "z", 352, 384))
SUM = (("y", "z", 0, 160), ("y", "z", 160, 352), ("z", "y", 352, 384))
STOP = None


def parts_of(table, tokens):
    scaled = [(a, b, lo * tokens // 384 // 32 * 32, hi * tokens // 384 // 32 * 32) for a, b, lo, hi in table]
    return [part for part in scaled if part[2] < part[3]]


class Stop(Exception):
    pass


class Sent:
    def __init__(self, copy):
        self.copy, self.received = copy, False

    def arrive(self):
        if not self.received:
            self.copy.wait_recv()
            self.received = True


def main_kernel(n_dp, scale, *refs):
    pending, endings = [], []
    try:
        main_body(n_dp, scale, pending, endings, *refs)
    except Stop:
        pass
    for c in pending:
        c.arrive()
        c.copy.wait_send()
    for end in endings:
        end()


def main_body(
    n_dp, scale, pending, endings,
    hid, wt, gen, cot, query, igrad, ggrad,
    w_v, hbuf, base, pb, gz, gy, gyb, gzb, ghome, gsave_y, gsave_z, gmid, cotc, genc, glocal, slocal,
    szb, ssend, syb, qsend, qb, s5b, s7b, zsend, gsend_t, gsend_z, gb,
    rs_s2, rs_r2, rs_s1, rs_s3, rs_r1, rs_r3, q_s2, q_r2, q_s1, q_s3, q_r1, q_r3,
    gp, gp_z, gp_y, gpb, sums_a, sums_b, slab_a, slab_b, gout, mats_loc, mats_z, mats_y,
    send_sem, recv_sem, w_sem,
):
    tokens = hid.shape[0]
    me = lax.axis_index("tensor")
    my_dp = lax.axis_index("dp")
    y, z = me // SIDE, lax.rem(me, SIDE)
    z_of = lax.rem(y + z, SIDE)
    counter = [0]

    def mark(name):
        if STOP == name:
            if name == "bwd_y":
                w_copy.wait()
            raise Stop

    def at(dy, dz):
        return wrap(y + dy, SIDE) * SIDE + wrap(z + dz, SIDE)

    def toward(axis, step):
        return at(step, 0) if axis == "y" else at(0, step)

    def place(axis, step, fixed):
        return (step, fixed) if axis == "y" else (fixed, step)

    def ids(n=1):
        first = counter[0]
        counter[0] += n
        return first

    def copy(src, dst, send_index, recv_index, device):
        return pltpu.make_async_remote_copy(
            src_ref=src,
            dst_ref=dst,
            send_sem=send_sem.at[send_index],
            recv_sem=recv_sem.at[recv_index],
            device_id=device,
            device_id_type=MESH,
        )

    def send(src, dst, dev, axis="tensor"):
        index = ids()
        c = copy(src, dst, index, index, {axis: dev})
        c.start()
        c = Sent(c)
        pending.append(c)
        return c

    def w_rows(dy, dz):
        return w_v[pl.ds(pl.multiple_of(at(dy, dz) * 512, 512), 512), :]

    w_copy = pltpu.make_async_copy(wt, w_v, w_sem)
    for c in range(4):
        cols = slice(c * LANES, (c + 1) * LANES)
        cotc[c] = cot[:, cols]
        genc[c] = gen[4:8, :, cols]

    barrier = pltpu.get_barrier_semaphore()
    for d in range(1, 16):
        pl.semaphore_signal(
            barrier, inc=1, device_id={"tensor": lax.rem(me + d, 16)}, device_id_type=MESH
        )
    for d in range(1, n_dp):
        pl.semaphore_signal(
            barrier, inc=1, device_id={"dp": lax.rem(my_dp + d, n_dp)}, device_id_type=MESH
        )
    pl.semaphore_wait(barrier, 15 + n_dp - 1)

    cot_in, genz_in, geny_in = [], [], []
    for d in range(1, 4):
        c = lax.rem(y + d + z, SIDE)
        cot_in.append(send(cotc.at[c], gyb.at[y], at(d, 0)))
        geny_in.append(send(genc.at[c, pl.ds(2, 2)], gy.at[y], at(d, 0)))

    def held(dy, dz, lo, hi):
        ref = hid if (dy, dz) == (0, 0) else hbuf.at[dy, dz]
        return ref.at[pl.ds(lo, hi - lo)]

    arrivals = {(dy, dz): [] for dy in range(4) for dz in range(4)}

    def hop(axis, fixed, step, sign, lo, hi):
        target = place(axis, step + sign & 3, fixed)
        c = send(
            held(*place(axis, step, fixed), lo, hi),
            hbuf.at[(*target, pl.ds(lo, hi - lo))],
            toward(axis, sign),
        )
        arrivals[target].append(c)
        return c

    def ring_start(axis, fixed, lo, hi):
        return [hop(axis, fixed, 0, 1, lo, hi), hop(axis, fixed, 0, -1, lo, hi)]

    def ring_forward(axis, fixed, lo, hi, copies):
        middle = (lo + hi) // 2
        copies[0].arrive()
        copies.append(hop(axis, fixed, 1, 1, lo, middle))
        copies[1].arrive()
        copies.append(hop(axis, fixed, 3, -1, middle, hi))

    routes = parts_of(GATHER, tokens)
    first = [ring_start(a, 0, lo, hi) for a, _, lo, hi in routes]
    second = [{0: ring_start(b, 0, lo, hi)} for _, b, lo, hi in routes]
    for d in range(1, 4):
        genz_in.append(send(genc.at[wrap(z + d, SIDE), pl.ds(0, 2)], gz.at[z], at(0, d)))

    w_copy.start()

    def gather_second(step, parts):
        for i in parts:
            _, b, lo, hi = routes[i]
            ring_forward(b, step, lo, hi, second[i][step])

    def gather_first(parts):
        for i in parts:
            a, b, lo, hi = routes[i]
            ring, copies, middle = first[i], second[i], (lo + hi) // 2
            ring[0].arrive()
            ring.append(hop(a, 0, 1, 1, lo, middle))
            copies[1] = ring_start(b, 1, lo, hi)
            ring[1].arrive()
            ring.append(hop(a, 0, 3, -1, middle, hi))
            copies[3] = ring_start(b, 3, lo, hi)

    def gather_far(parts):
        for i in parts:
            _, b, lo, hi = routes[i]
            first[i][2].arrive()
            first[i][3].arrive()
            second[i][2] = ring_start(b, 2, lo, hi)

    z_parts = [i for i, part in enumerate(routes) if part[0] == "z"]
    y_parts = [i for i, part in enumerate(routes) if part[0] == "y"]

    def accumulate(*blocks):
        for dy, dz in blocks:
            for c in arrivals[dy, dz]:
                c.arrive()
            base[...] += dot(hbuf[dy, dz], w_rows(-dy, -dz))

    gyb[y] = cotc[z_of]
    gy[y] = genc[z_of, 2:4]
    gz[z] = genc[z, 0:2]

    for k in range(3):
        for s in range(2):
            put_split(mats_loc, (k, s), near_matrix(gen[k, :, 256 * s : 256 * s + 256], k))
    for s in range(2):
        for h in range(2):
            block = gen[3, HALF * h : HALF * h + HALF, 256 * s : 256 * s + 256]
            put_split(mats_loc, (3 + h, s), diag_matrix(block))

    def pair_of(ref, a, b):
        return jnp.concatenate([ref[a], ref[b]], axis=1)

    def fill_pairs(mats, gens):
        for k in range(2):
            for i, (a, b) in enumerate(PAIRS[k]):
                put_split(mats, (k, i), pair_matrix(gens[a, k], gens[b, k]))

    def pairs_apply(product, order, source, mats, save, out):
        values = None
        for k, target in zip(order, (save, out)):
            new = [None] * 4
            for i, (a, b) in enumerate(PAIRS[k]):
                if values is None:
                    v = pair_of(source, a, b)
                else:
                    v = jnp.concatenate([values[a], values[b]], axis=1)
                v = v.astype(F32) + mix(product, v, mats, (k, i))
                new[a], new[b] = v[:, :LANES], v[:, LANES:]
            values = new
            for m in range(4):
                target[m] = values[m].astype(BF16)

    def cross(src, dst, own_slot, dev_of, src_of):
        index = ids(4)
        sent = []
        for d in range(4):
            c = copy(
                src.at[src_of(d)], dst.at[own_slot], index + d, index + own_slot,
                {"tensor": dev_of(d)},
            )
            if d == 0:
                keep = pltpu.make_async_copy(
                    src.at[src_of(0)], dst.at[own_slot], recv_sem.at[index + own_slot]
                )
                pl.when(dev_of(0) != me)(lambda c=c: c.start())
                pl.when(dev_of(0) == me)(lambda keep=keep: keep.start())
            else:
                c.start()
            sent.append(c)
        done = []

        def arrive():
            if not done:
                done.append(True)
                for m in range(4):
                    pltpu.make_async_copy(src.at[m], dst.at[m], recv_sem.at[index + m]).wait()

        def finish():
            arrive()
            pl.when(dev_of(0) != me)(lambda: sent[0].wait_send())
            for c in sent[1:]:
                c.wait_send()

        endings.append(finish)
        return arrive

    for c in geny_in:
        c.arrive()
    fill_pairs(mats_y, gy)
    for c in cot_in:
        c.arrive()
    pairs_apply(dot_nt, (1, 0), gyb, mats_y, gsave_y, gsend_t)
    step_in = []
    for d in range(1, 4):
        step_in.append(send(gsend_t.at[wrap(y + d, SIDE)], gmid.at[z_of], at(d, 0)))
    gmid[z_of] = gsend_t[y]
    mark("bwd_y")

    gather_second(0, z_parts)
    for c in genz_in:
        c.arrive()
    fill_pairs(mats_z, gz)
    for c in step_in:
        c.arrive()
    step_in = []
    for d in range(1, 4):
        step_in.append(send(gmid.at[wrap(z + d, SIDE)], gzb.at[z], at(0, d)))
    gzb[z] = gmid[z]
    mark("ag0")

    gather_first(z_parts)
    gather_first(y_parts)
    gather_second(0, y_parts)
    w_copy.wait()
    base[...] = dot(hid[...], w_rows(0, 0))
    mark("ag1")
    for c in step_in:
        c.arrive()
    pairs_apply(dot_nt, (1, 0), gzb, mats_z, gsave_z, gsend_z)
    back_in = []
    for d in range(1, 4):
        back_in.append(send(gsend_z.at[wrap(z + d, SIDE)], ghome.at[z], at(0, d)))
    ghome[z] = gsend_z[z]
    mark("bwd_z")

    gather_far(z_parts)
    gather_second(1, z_parts)
    gather_second(3, z_parts)
    gather_far(y_parts)
    accumulate((1, 0), (3, 0), (0, 1), (0, 3))
    mark("ag2")

    for c in back_in:
        c.arrive()
    ga = pair_of(ghome, 0, 1)
    gc = pair_of(ghome, 2, 3)
    glocal[3, 0], glocal[3, 1] = ga, gc
    fa = ga.astype(F32) + mix(dot_nt, ga, mats_loc, (3, 0)) + mix(dot_nt, gc, mats_loc, (3, 1))
    fb = gc.astype(F32) + mix(dot_nt, ga, mats_loc, (4, 0)) + mix(dot_nt, gc, mats_loc, (4, 1))
    for k in (2, 1, 0):
        glocal[k, 0], glocal[k, 1] = fa.astype(BF16), fb.astype(BF16)
        fa = fa + mix(dot_nt, fa, mats_loc, (k, 0))
        fb = fb + mix(dot_nt, fb, mats_loc, (k, 1))
    gb[:, :256] = fa.astype(BF16)
    gb[:, 256:] = fb.astype(BF16)
    mark("bwd_local")

    gather_second(1, y_parts)
    gather_second(3, y_parts)
    gather_second(2, z_parts)
    gather_second(2, y_parts)
    mark("ag3")

    computed = set()

    def partial(dy, dz, lo, hi):
        if (dy, dz) not in computed:
            computed.add((dy, dz))
            pb[dy, dz] = dot_nt(gb[...], w_rows(dy, dz))
        return pb[dy, dz, lo:hi]

    class Sum:
        def __init__(self, a, b, lo, hi):
            self.a, self.b, self.lo, self.hi, self.middle = a, b, lo, hi, (lo + hi) // 2
            self.copies, self.last = {}, []
            self.rows = pl.ds(lo, hi - lo)
            self.top, self.low = pl.ds(lo, self.middle - lo), pl.ds(self.middle, hi - self.middle)

        def far(self, fixed):
            block = partial(*place(self.a, 2, fixed), self.lo, self.hi)
            rs_s2[fixed, self.rows] = block.astype(BF16)
            self.copies[fixed] = [
                send(rs_s2.at[fixed, self.top], rs_r2.at[fixed, self.top], toward(self.a, 1)),
                send(rs_s2.at[fixed, self.low], rs_r2.at[fixed, self.low], toward(self.a, -1)),
            ]

        def near(self, fixed):
            cs, size = self.copies[fixed], self.middle - self.lo
            p = partial(*place(self.a, 1, fixed), self.lo, self.hi)
            cs[0].arrive()
            rs_s1[fixed, self.top] = (p[:size] + rs_r2[fixed, self.top].astype(F32)).astype(BF16)
            rs_s1[fixed, self.low] = p[size:].astype(BF16)
            cs.append(
                send(rs_s1.at[fixed, self.rows], rs_r1.at[fixed, self.rows], toward(self.a, 1))
            )
            p = partial(*place(self.a, 3, fixed), self.lo, self.hi)
            cs[1].arrive()
            rs_s3[fixed, self.top] = p[:size].astype(BF16)
            rs_s3[fixed, self.low] = (p[size:] + rs_r2[fixed, self.low].astype(F32)).astype(BF16)
            cs.append(
                send(rs_s3.at[fixed, self.rows], rs_r3.at[fixed, self.rows], toward(self.a, -1))
            )

        def whole(self, fixed):
            p = partial(*place(self.a, 0, fixed), self.lo, self.hi)
            for c in self.copies[fixed][2:]:
                c.arrive()
            return p + rs_r1[fixed, self.rows].astype(F32) + rs_r3[fixed, self.rows].astype(F32)

        def last_far(self):
            q_s2[self.rows] = self.whole(2).astype(BF16)
            self.last = [
                send(q_s2.at[self.top], q_r2.at[self.top], toward(self.b, 1)),
                send(q_s2.at[self.low], q_r2.at[self.low], toward(self.b, -1)),
            ]

        def last_near(self):
            size = self.middle - self.lo
            q = self.whole(1)
            self.last[0].arrive()
            q_s1[self.top] = (q[:size] + q_r2[self.top].astype(F32)).astype(BF16)
            q_s1[self.low] = q[size:].astype(BF16)
            self.last.append(send(q_s1.at[self.rows], q_r1.at[self.rows], toward(self.b, 1)))
            q = self.whole(3)
            self.last[1].arrive()
            q_s3[self.top] = q[:size].astype(BF16)
            q_s3[self.low] = (q[size:] + q_r2[self.low].astype(F32)).astype(BF16)
            self.last.append(send(q_s3.at[self.rows], q_r3.at[self.rows], toward(self.b, -1)))

        def end(self):
            q = self.whole(0)
            for c in self.last[2:]:
                c.arrive()
            q = q + q_r1[self.rows].astype(F32) + q_r3[self.rows].astype(F32)
            igrad[self.rows] = q.astype(BF16)

    sums = [Sum(*part) for part in parts_of(SUM, tokens)]
    def far(group, *blocks):
        for fixed in blocks:
            for s in group:
                s.far(fixed)

    def near(group, *blocks):
        for fixed in blocks:
            for s in group:
                s.near(fixed)

    far(sums, 2, 1, 3, 0)
    mark("rs_far")
    accumulate((2, 0), (0, 2), (1, 1), (3, 1), (1, 3), (3, 3), (1, 2), (3, 2))

    accumulate((2, 1), (2, 3), (2, 2))
    mark("base")
    fa, fb = base[:, :256], base[:, 256:]
    for k in range(3):
        slocal[k, 0], slocal[k, 1] = fa.astype(BF16), fb.astype(BF16)
        fa = fa + mix(dot, fa, mats_loc, (k, 0))
        fb = fb + mix(dot, fb, mats_loc, (k, 1))
    slocal[3, 0], slocal[3, 1] = fa.astype(BF16), fb.astype(BF16)
    fc = fa + mix(dot, fa, mats_loc, (3, 0)) + mix(dot, fb, mats_loc, (4, 0))
    fd = fb + mix(dot, fa, mats_loc, (3, 1)) + mix(dot, fb, mats_loc, (4, 1))
    for c in range(4):
        side = fc if c < 2 else fd
        ssend[c] = side[:, (c % 2) * LANES : (c % 2) * LANES + LANES].astype(BF16)
    fwd_in = []
    for d in range(1, 4):
        fwd_in.append(send(ssend.at[wrap(z + d, SIDE)], szb.at[z], at(0, d)))
    szb[z] = ssend[z]
    mark("fwd_local")

    near(sums, 2, 1)
    mark("near1")

    def put_local(k, s, value):
        for j in range(2):
            gp[pl.ds(((k // 2) * 4 + 2 * s + j) * 128 + (k % 2) * 64, 64)] = value[
                :, j * LANES : (j + 1) * LANES
            ]

    for k in range(3):
        for s in range(2):
            put_local(k, s, near_extract(dot_tn(slocal[k, s], glocal[k, s]), k))
    for s in range(2):
        put_local(
            3, s,
            jnp.concatenate(
                [diag_extract(dot_tn(slocal[3, h], glocal[3, s])) for h in range(2)], axis=0
            ),
        )

    class Slabs:
        def __init__(self, start, size, sums_ref, slab_ref):
            self.start, self.size = start, size
            self.sums_ref, self.slab_ref = sums_ref, slab_ref
            self.ins, self.outs = [], []

        def rows(self, dev):
            return pl.ds(pl.multiple_of(self.start + dev * self.size, 32), self.size)

        def scatter(self):
            all_rows = pl.ds(self.start, 16 * self.size)
            gpb[all_rows] = gp[all_rows].astype(BF16)
            for d in range(1, n_dp):
                dev = lax.rem(my_dp + d, n_dp)
                self.ins.append(send(gpb.at[self.rows(dev)], self.sums_ref.at[d], dev, "dp"))

        def gather(self):
            total = gp[self.rows(my_dp)]
            for d, c in zip(range(1, n_dp), self.ins):
                c.arrive()
                total = total + self.sums_ref[d].astype(F32)
            self.slab_ref[...] = (total * scale).astype(BF16)
            for d in range(1, n_dp):
                dev = lax.rem(my_dp + d, n_dp)
                self.outs.append(send(self.slab_ref, gout.at[self.rows(my_dp)], dev, "dp"))
            gout[self.rows(my_dp)] = self.slab_ref[...]

        def finish(self):
            for c in self.outs:
                c.arrive()

    early, late = Slabs(0, 64, sums_a, slab_a), Slabs(1024, 64, sums_b, slab_b)

    for c in fwd_in:
        c.arrive()
    pairs_apply(dot, (0, 1), szb, mats_z, s5b, zsend)
    fwd_arrive = cross(
        zsend, syb, y,
        lambda d: ((SIDE - d) % SIDE) * SIDE + wrap(z + d, SIDE),
        lambda d: wrap(z + d, SIDE),
    )
    if n_dp > 1:
        early.scatter()
    mark("fwd_z")
    near(sums, 3)
    for s in sums:
        if s.a == "y":
            s.last_far()
    mark("near2")

    def pair_grads(states, grads, dst):
        for k in range(2):
            for i, (a, b) in enumerate(PAIRS[k]):
                value = pair_extract(dot_tn(pair_of(states[k], a, b), pair_of(grads[k], a, b)))
                dst[a, k * 64 : k * 64 + 64] = value[:, :LANES]
                dst[b, k * 64 : k * 64 + 64] = value[:, LANES:]

    def piece(index):
        return pl.ds(pl.multiple_of(index * 128, 128), 128)

    pair_grads((szb, s5b), (gsave_z, gzb), gp_z)
    outz_in = []
    for d in range(1, 4):
        outz_in.append(send(gp_z.at[wrap(z + d, SIDE)], gp.at[piece(8 + z)], at(0, d)))
    gp[piece(8 + z)] = gp_z[z]

    fwd_arrive()
    pairs_apply(dot, (0, 1), syb, mats_y, s7b, qsend)
    query_in = []
    for d in range(1, 4):
        query_in.append(send(qsend.at[wrap(y + d, SIDE)], qb.at[z_of], at(d, 0)))
    qb[z_of] = qsend[y]
    mark("fwd_y")

    pair_grads((syb, s7b), (gsave_y, gyb), gp_y)
    outy_in = []
    for d in range(1, 4):
        outy_in.append(send(gp_y.at[wrap(y + d, SIDE)], gp.at[piece(12 + z_of)], at(d, 0)))
    gp[piece(12 + z_of)] = gp_y[y]
    mark("grads")

    near(sums, 0)
    for s in sums:
        if s.a == "z":
            s.last_far()
    for s in sums:
        if s.a == "y":
            s.last_near()
    mark("last_near")
    if n_dp > 1:
        early.gather()
    for c in outz_in + outy_in:
        c.arrive()
    if n_dp > 1:
        late.scatter()
    for s in sums:
        if s.a == "z":
            s.last_near()
    if n_dp > 1:
        late.gather()
    mark("dp")

    for c in query_in:
        c.arrive()
    for c in range(4):
        query[:, c * LANES : (c + 1) * LANES] = qb[c]
    mark("query")
    for s in sums:
        s.end()
    mark("igrad")
    if n_dp > 1:
        early.finish()
        late.finish()
    final = gout if n_dp > 1 else gp
    for pair in range(4):
        for c in range(4):
            value = final[pl.ds((pair * 4 + c) * 128, 128)].astype(F32)
            for j in range(2):
                ggrad[2 * pair + j, :, c * LANES : (c + 1) * LANES] = value[j * 64 : j * 64 + 64]


def main_call(hidden, weight, generators, cotangent, n_dp=1, scale=1.0):
    tokens = hidden.shape[0]
    vm = lambda *shape, dtype=BF16: pltpu.VMEM(shape, dtype)
    chunks = vm(4, tokens, LANES)
    block = vm(tokens, 512)
    blocks = vm(4, tokens, 512)
    flops = 4 * tokens * 8192 * 512
    return pl.pallas_call(
        functools.partial(main_kernel, n_dp, scale),
        out_shape=(
            jax.ShapeDtypeStruct((tokens, 512), BF16),
            jax.ShapeDtypeStruct((tokens, 512), BF16),
            jax.ShapeDtypeStruct((8, 64, 512), F32),
        ),
        in_specs=[
            pl.BlockSpec(memory_space=pltpu.VMEM),
            pl.BlockSpec(memory_space=pl.ANY),
            pl.BlockSpec(memory_space=pltpu.VMEM),
            pl.BlockSpec(memory_space=pltpu.VMEM),
        ],
        out_specs=[pl.BlockSpec(memory_space=pltpu.VMEM)] * 3,
        scratch_shapes=[
            vm(8192, 512),
            vm(4, 4, tokens, 512),
            vm(tokens, 512, dtype=F32),
            vm(4, 4, tokens, 512, dtype=F32),
            vm(4, 2, 64, LANES, dtype=F32),
            vm(4, 2, 64, LANES, dtype=F32),
            chunks, chunks, chunks, chunks, chunks, chunks,
            chunks, vm(4, 4, 64, LANES, dtype=F32),
            vm(4, 2, tokens, 256),
            vm(4, 2, tokens, 256),
            chunks, chunks, chunks, chunks, chunks,
            chunks, chunks, chunks, chunks, chunks,
            block,
            blocks, blocks, blocks, blocks, blocks, blocks,
            block, block, block, block, block, block,
            vm(2048, 128, dtype=F32),
            vm(4, 128, 128, dtype=F32),
            vm(4, 128, 128, dtype=F32),
            vm(2048, 128),
            vm(16, 64, 128),
            vm(16, 64, 128),
            vm(64, 128),
            vm(64, 128),
            vm(2048, 128),
            vm(5, 2, 2, 256, 256),
            vm(2, 2, 2, 256, 256),
            vm(2, 2, 2, 256, 256),
            pltpu.SemaphoreType.DMA((N_SEMS,)),
            pltpu.SemaphoreType.DMA((N_SEMS,)),
            pltpu.SemaphoreType.DMA,
        ],
        compiler_params=pltpu.CompilerParams(
            collective_id=0, has_side_effects=True, vmem_limit_bytes=VMEM_BYTES
        ),
        cost_estimate=pl.CostEstimate(
            flops=flops, bytes_accessed=12 * 1024 * 1024, transcendentals=0
        ),
        name="adapt",
    )(hidden, weight, generators, cotangent)


def copy_kernel(*refs):
    count = len(refs) // 2
    for source, target in zip(refs[:count], refs[count:]):
        target[...] = source[...]


def copy_call(*arrays):
    whole = pl.BlockSpec(memory_space=pltpu.VMEM)
    return pl.pallas_call(
        copy_kernel,
        out_shape=tuple(jax.ShapeDtypeStruct(a.shape, a.dtype) for a in arrays),
        in_specs=[whole] * len(arrays),
        out_specs=[whole] * len(arrays),
        name="results",
    )(*arrays)


def on_device(hidden, base_weight, generators, cotangent):
    n = lax.axis_size("dp")
    scale = 1.0 / math.sqrt(hidden.shape[0] * n)
    return copy_call(*main_call(hidden, base_weight, generators, cotangent, n, scale))


def solution(mesh):
    placed = (P("dp", "tensor"), P(None, "tensor"), P(None, None, "tensor"), P("dp", "tensor"))
    return jax.shard_map(
        on_device,
        mesh=mesh,
        in_specs=placed,
        out_specs=(P("dp", "tensor"), P("dp", "tensor"), P(None, None, "tensor")),
        check_vma=False,
    )
```

```python
import functools
import math

import jax
import jax.numpy as jnp
from jax import lax
from jax.experimental import pallas as pl
from jax.experimental.pallas import tpu as pltpu
from jax.sharding import PartitionSpec as P

MESH = pl.DeviceIdType.MESH
F32 = jnp.float32
BF16 = jnp.bfloat16
SIDE = 4
LANES = 128
HALF = 32
VMEM_BYTES = 60 * 1024 * 1024


def wrap(value, n):
    return lax.rem(value + n, n)


def dot(a, b):
    return jnp.dot(a, b, preferred_element_type=F32)


def dot_nt(a, b):
    return lax.dot_general(a, b, (((1,), (1,)), ((), ())), preferred_element_type=F32)


def dot_tn(a, b):
    return lax.dot_general(a, b, (((0,), (0,)), ((), ())), preferred_element_type=F32)


def split(value):
    high = value.astype(BF16)
    return high, (value - high.astype(F32)).astype(BF16)


def put_split(ref, index, value):
    ref[(*index, 0)], ref[(*index, 1)] = split(value)


def mix(product, value, ref, index):
    top, rest = ref[(*index, 0)], ref[(*index, 1)]
    if value.dtype == BF16:
        return product(value, top) + product(value, rest)
    high, low = split(value)
    return product(high, top) + product(low, top) + product(high, rest)


def groups_of(shape):
    rows = lax.broadcasted_iota(jnp.int32, shape, 0) >> 5
    cols = lax.broadcasted_iota(jnp.int32, shape, 1) >> 5
    return rows, cols


def spread(block, mask, copies):
    return jnp.where(mask, jnp.concatenate([block] * copies, axis=0), 0.0)


def pair_matrix(gen_a, gen_b):
    both = jnp.concatenate([gen_a, gen_b], axis=1)
    rows, cols = groups_of((LANES, 2 * LANES))
    mask = rows == (cols & 3)
    return jnp.concatenate([spread(both[:HALF], mask, 4), spread(both[HALF:], mask, 4)], axis=0)


def pair_extract(grad):
    cols = (lax.broadcasted_iota(jnp.int32, (HALF, 2 * LANES), 1) >> 5) & 3
    parts = []
    for h in range(2):
        total = jnp.zeros((HALF, 2 * LANES), F32)
        for g in range(4):
            start = h * LANES + g * HALF
            total = total + jnp.where(cols == g, grad[start : start + HALF], 0.0)
        parts.append(total)
    return jnp.concatenate(parts, axis=0)


def near_matrix(gen, k):
    rows, cols = groups_of((256, 256))
    low = cols & ~(1 << k)
    return spread(gen[:HALF], rows == low, 8) + spread(gen[HALF:], rows == (low | (1 << k)), 8)


def near_extract(grad, k):
    cols = lax.broadcasted_iota(jnp.int32, (HALF, 256), 1) >> 5
    low = cols & ~(1 << k)
    parts = []
    for want in (low, low | (1 << k)):
        total = jnp.zeros((HALF, 256), F32)
        for g in range(8):
            total = total + jnp.where(want == g, grad[g * HALF : (g + 1) * HALF], 0.0)
        parts.append(total)
    return jnp.concatenate(parts, axis=0)


def diag_matrix(block):
    rows, cols = groups_of((256, 256))
    return spread(block, rows == cols, 8)


def diag_extract(grad):
    cols = lax.broadcasted_iota(jnp.int32, (HALF, 256), 1) >> 5
    total = jnp.zeros((HALF, 256), F32)
    for g in range(8):
        total = total + jnp.where(cols == g, grad[g * HALF : (g + 1) * HALF], 0.0)
    return total


PAIRS = (((0, 1), (2, 3)), ((0, 2), (1, 3)))
N_SEMS = 320
GATHER = (("z", "y", 0, 160), ("z", "y", 160, 352), ("y", "z", 352, 384))
SUM = (("y", "z", 0, 160), ("y", "z", 160, 352), ("z", "y", 352, 384))
STOP = None


def parts_of(table, tokens):
    scaled = [(a, b, lo * tokens // 384 // 32 * 32, hi * tokens // 384 // 32 * 32) for a, b, lo, hi in table]
    return [part for part in scaled if part[2] < part[3]]


class Stop(Exception):
    pass


class Sent:
    def __init__(self, copy):
        self.copy, self.received = copy, False

    def arrive(self):
        if not self.received:
            self.copy.wait_recv()
            self.received = True


def main_kernel(n_dp, scale, *refs):
    pending, endings = [], []
    try:
        main_body(n_dp, scale, pending, endings, *refs)
    except Stop:
        pass
    for c in pending:
        c.arrive()
        c.copy.wait_send()
    for end in endings:
        end()


def main_body(
    n_dp, scale, pending, endings,
    hid, wt, gen, cot, query, igrad, ggrad,
    w_v, hbuf, base, pb, gz, gy, gyb, gzb, ghome, gsave_y, gsave_z, gmid, cotc, genc, glocal, slocal,
    szb, ssend, syb, qsend, qb, s5b, s7b, zsend, gsend_t, gsend_z, gb,
    rs_s2, rs_r2, rs_s1, rs_s3, rs_r1, rs_r3, q_s2, q_r2, q_s1, q_s3, q_r1, q_r3,
    gp, gp_z, gp_y, gpb, sums_a, sums_b, slab_a, slab_b, gout, mats_loc, mats_z, mats_y,
    send_sem, recv_sem, w_sem,
):
    tokens = hid.shape[0]
    me = lax.axis_index("tensor")
    my_dp = lax.axis_index("dp")
    y, z = me // SIDE, lax.rem(me, SIDE)
    z_of = lax.rem(y + z, SIDE)
    counter = [0]

    def mark(name):
        if STOP == name:
            if name == "bwd_y":
                w_copy.wait()
            raise Stop

    def at(dy, dz):
        return wrap(y + dy, SIDE) * SIDE + wrap(z + dz, SIDE)

    def toward(axis, step):
        return at(step, 0) if axis == "y" else at(0, step)

    def place(axis, step, fixed):
        return (step, fixed) if axis == "y" else (fixed, step)

    def ids(n=1):
        first = counter[0]
        counter[0] += n
        return first

    def copy(src, dst, send_index, recv_index, device):
        return pltpu.make_async_remote_copy(
            src_ref=src,
            dst_ref=dst,
            send_sem=send_sem.at[send_index],
            recv_sem=recv_sem.at[recv_index],
            device_id=device,
            device_id_type=MESH,
        )

    def send(src, dst, dev, axis="tensor"):
        index = ids()
        c = copy(src, dst, index, index, {axis: dev})
        c.start()
        c = Sent(c)
        pending.append(c)
        return c

    def w_rows(dy, dz):
        return w_v[pl.ds(pl.multiple_of(at(dy, dz) * 512, 512), 512), :]

    w_copy = pltpu.make_async_copy(wt, w_v, w_sem)
    for c in range(4):
        cols = slice(c * LANES, (c + 1) * LANES)
        cotc[c] = cot[:, cols]
        genc[c] = gen[4:8, :, cols]

    barrier = pltpu.get_barrier_semaphore()
    for d in range(1, 16):
        pl.semaphore_signal(
            barrier, inc=1, device_id={"tensor": lax.rem(me + d, 16)}, device_id_type=MESH
        )
    for d in range(1, n_dp):
        pl.semaphore_signal(
            barrier, inc=1, device_id={"dp": lax.rem(my_dp + d, n_dp)}, device_id_type=MESH
        )
    pl.semaphore_wait(barrier, 15 + n_dp - 1)

    cot_in, genz_in, geny_in = [], [], []
    for d in range(1, 4):
        c = lax.rem(y + d + z, SIDE)
        cot_in.append(send(cotc.at[c], gyb.at[y], at(d, 0)))
        geny_in.append(send(genc.at[c, pl.ds(2, 2)], gy.at[y], at(d, 0)))

    def held(dy, dz, lo, hi):
        ref = hid if (dy, dz) == (0, 0) else hbuf.at[dy, dz]
        return ref.at[pl.ds(lo, hi - lo)]

    arrivals = {(dy, dz): [] for dy in range(4) for dz in range(4)}

    def hop(axis, fixed, step, sign, lo, hi):
        target = place(axis, step + sign & 3, fixed)
        c = send(
            held(*place(axis, step, fixed), lo, hi),
            hbuf.at[(*target, pl.ds(lo, hi - lo))],
            toward(axis, sign),
        )
        arrivals[target].append(c)
        return c

    def ring_start(axis, fixed, lo, hi):
        return [hop(axis, fixed, 0, 1, lo, hi), hop(axis, fixed, 0, -1, lo, hi)]

    def ring_forward(axis, fixed, lo, hi, copies):
        middle = (lo + hi) // 2
        copies[0].arrive()
        copies.append(hop(axis, fixed, 1, 1, lo, middle))
        copies[1].arrive()
        copies.append(hop(axis, fixed, 3, -1, middle, hi))

    routes = parts_of(GATHER, tokens)
    first = [ring_start(a, 0, lo, hi) for a, _, lo, hi in routes]
    second = [{0: ring_start(b, 0, lo, hi)} for _, b, lo, hi in routes]
    for d in range(1, 4):
        genz_in.append(send(genc.at[wrap(z + d, SIDE), pl.ds(0, 2)], gz.at[z], at(0, d)))

    w_copy.start()

    def gather_second(step):
        for (_, b, lo, hi), copies in zip(routes, second):
            ring_forward(b, step, lo, hi, copies[step])

    def gather_first():
        for (a, b, lo, hi), ring, copies in zip(routes, first, second):
            middle = (lo + hi) // 2
            ring[0].arrive()
            ring.append(hop(a, 0, 1, 1, lo, middle))
            copies[1] = ring_start(b, 1, lo, hi)
            ring[1].arrive()
            ring.append(hop(a, 0, 3, -1, middle, hi))
            copies[3] = ring_start(b, 3, lo, hi)

    def gather_far():
        for (_, b, lo, hi), ring, copies in zip(routes, first, second):
            ring[2].arrive()
            ring[3].arrive()
            copies[2] = ring_start(b, 2, lo, hi)

    def accumulate(*blocks):
        for dy, dz in blocks:
            for c in arrivals[dy, dz]:
                c.arrive()
            base[...] += dot(hbuf[dy, dz], w_rows(-dy, -dz))

    gyb[y] = cotc[z_of]
    gy[y] = genc[z_of, 2:4]
    gz[z] = genc[z, 0:2]

    for k in range(3):
        for s in range(2):
            put_split(mats_loc, (k, s), near_matrix(gen[k, :, 256 * s : 256 * s + 256], k))
    for s in range(2):
        for h in range(2):
            block = gen[3, HALF * h : HALF * h + HALF, 256 * s : 256 * s + 256]
            put_split(mats_loc, (3 + h, s), diag_matrix(block))

    def pair_of(ref, a, b):
        return jnp.concatenate([ref[a], ref[b]], axis=1)

    def fill_pairs(mats, gens):
        for k in range(2):
            for i, (a, b) in enumerate(PAIRS[k]):
                put_split(mats, (k, i), pair_matrix(gens[a, k], gens[b, k]))

    def pairs_apply(product, order, source, mats, save, out):
        values = None
        for k, target in zip(order, (save, out)):
            new = [None] * 4
            for i, (a, b) in enumerate(PAIRS[k]):
                if values is None:
                    v = pair_of(source, a, b)
                else:
                    v = jnp.concatenate([values[a], values[b]], axis=1)
                v = v.astype(F32) + mix(product, v, mats, (k, i))
                new[a], new[b] = v[:, :LANES], v[:, LANES:]
            values = new
            for m in range(4):
                target[m] = values[m].astype(BF16)

    def cross(src, dst, own_slot, dev_of, src_of):
        index = ids(4)
        sent = []
        for d in range(4):
            c = copy(
                src.at[src_of(d)], dst.at[own_slot], index + d, index + own_slot,
                {"tensor": dev_of(d)},
            )
            if d == 0:
                keep = pltpu.make_async_copy(
                    src.at[src_of(0)], dst.at[own_slot], recv_sem.at[index + own_slot]
                )
                pl.when(dev_of(0) != me)(lambda c=c: c.start())
                pl.when(dev_of(0) == me)(lambda keep=keep: keep.start())
            else:
                c.start()
            sent.append(c)
        done = []

        def arrive():
            if not done:
                done.append(True)
                for m in range(4):
                    pltpu.make_async_copy(src.at[m], dst.at[m], recv_sem.at[index + m]).wait()

        def finish():
            arrive()
            pl.when(dev_of(0) != me)(lambda: sent[0].wait_send())
            for c in sent[1:]:
                c.wait_send()

        endings.append(finish)
        return arrive

    for c in geny_in:
        c.arrive()
    fill_pairs(mats_y, gy)
    for c in cot_in:
        c.arrive()
    pairs_apply(dot_nt, (1, 0), gyb, mats_y, gsave_y, gsend_t)
    step_in = []
    for d in range(1, 4):
        step_in.append(send(gsend_t.at[wrap(y + d, SIDE)], gmid.at[z_of], at(d, 0)))
    gmid[z_of] = gsend_t[y]
    mark("bwd_y")

    gather_second(0)
    for c in genz_in:
        c.arrive()
    fill_pairs(mats_z, gz)
    for c in step_in:
        c.arrive()
    step_in = []
    for d in range(1, 4):
        step_in.append(send(gmid.at[wrap(z + d, SIDE)], gzb.at[z], at(0, d)))
    gzb[z] = gmid[z]
    w_copy.wait()
    base[...] = dot(hid[...], w_rows(0, 0))
    mark("ag0")

    gather_first()
    mark("ag1")
    for c in step_in:
        c.arrive()
    pairs_apply(dot_nt, (1, 0), gzb, mats_z, gsave_z, gsend_z)
    back_in = []
    for d in range(1, 4):
        back_in.append(send(gsend_z.at[wrap(z + d, SIDE)], ghome.at[z], at(0, d)))
    ghome[z] = gsend_z[z]
    mark("bwd_z")

    gather_far()
    accumulate((1, 0), (3, 0), (0, 1), (0, 3))
    gather_second(1)
    gather_second(3)
    accumulate((2, 0), (0, 2), (1, 1), (3, 1))
    mark("ag2")

    for c in back_in:
        c.arrive()
    ga = pair_of(ghome, 0, 1)
    gc = pair_of(ghome, 2, 3)
    glocal[3, 0], glocal[3, 1] = ga, gc
    fa = ga.astype(F32) + mix(dot_nt, ga, mats_loc, (3, 0)) + mix(dot_nt, gc, mats_loc, (3, 1))
    fb = gc.astype(F32) + mix(dot_nt, ga, mats_loc, (4, 0)) + mix(dot_nt, gc, mats_loc, (4, 1))
    for k in (2, 1, 0):
        glocal[k, 0], glocal[k, 1] = fa.astype(BF16), fb.astype(BF16)
        fa = fa + mix(dot_nt, fa, mats_loc, (k, 0))
        fb = fb + mix(dot_nt, fb, mats_loc, (k, 1))
    gb[:, :256] = fa.astype(BF16)
    gb[:, 256:] = fb.astype(BF16)
    mark("bwd_local")

    gather_second(2)
    mark("ag3")

    computed = set()

    def partial(dy, dz, lo, hi):
        if (dy, dz) not in computed:
            computed.add((dy, dz))
            pb[dy, dz] = dot_nt(gb[...], w_rows(dy, dz))
        return pb[dy, dz, lo:hi]

    class Sum:
        def __init__(self, a, b, lo, hi):
            self.a, self.b, self.lo, self.hi, self.middle = a, b, lo, hi, (lo + hi) // 2
            self.copies, self.last = {}, []
            self.rows = pl.ds(lo, hi - lo)
            self.top, self.low = pl.ds(lo, self.middle - lo), pl.ds(self.middle, hi - self.middle)

        def far(self, fixed):
            block = partial(*place(self.a, 2, fixed), self.lo, self.hi)
            rs_s2[fixed, self.rows] = block.astype(BF16)
            self.copies[fixed] = [
                send(rs_s2.at[fixed, self.top], rs_r2.at[fixed, self.top], toward(self.a, 1)),
                send(rs_s2.at[fixed, self.low], rs_r2.at[fixed, self.low], toward(self.a, -1)),
            ]

        def near(self, fixed):
            cs, size = self.copies[fixed], self.middle - self.lo
            p = partial(*place(self.a, 1, fixed), self.lo, self.hi)
            cs[0].arrive()
            rs_s1[fixed, self.top] = (p[:size] + rs_r2[fixed, self.top].astype(F32)).astype(BF16)
            rs_s1[fixed, self.low] = p[size:].astype(BF16)
            cs.append(
                send(rs_s1.at[fixed, self.rows], rs_r1.at[fixed, self.rows], toward(self.a, 1))
            )
            p = partial(*place(self.a, 3, fixed), self.lo, self.hi)
            cs[1].arrive()
            rs_s3[fixed, self.top] = p[:size].astype(BF16)
            rs_s3[fixed, self.low] = (p[size:] + rs_r2[fixed, self.low].astype(F32)).astype(BF16)
            cs.append(
                send(rs_s3.at[fixed, self.rows], rs_r3.at[fixed, self.rows], toward(self.a, -1))
            )

        def whole(self, fixed):
            p = partial(*place(self.a, 0, fixed), self.lo, self.hi)
            for c in self.copies[fixed][2:]:
                c.arrive()
            return p + rs_r1[fixed, self.rows].astype(F32) + rs_r3[fixed, self.rows].astype(F32)

        def last_far(self):
            q_s2[self.rows] = self.whole(2).astype(BF16)
            self.last = [
                send(q_s2.at[self.top], q_r2.at[self.top], toward(self.b, 1)),
                send(q_s2.at[self.low], q_r2.at[self.low], toward(self.b, -1)),
            ]

        def last_near(self):
            size = self.middle - self.lo
            q = self.whole(1)
            self.last[0].arrive()
            q_s1[self.top] = (q[:size] + q_r2[self.top].astype(F32)).astype(BF16)
            q_s1[self.low] = q[size:].astype(BF16)
            self.last.append(send(q_s1.at[self.rows], q_r1.at[self.rows], toward(self.b, 1)))
            q = self.whole(3)
            self.last[1].arrive()
            q_s3[self.top] = q[:size].astype(BF16)
            q_s3[self.low] = (q[size:] + q_r2[self.low].astype(F32)).astype(BF16)
            self.last.append(send(q_s3.at[self.rows], q_r3.at[self.rows], toward(self.b, -1)))

        def end(self):
            q = self.whole(0)
            for c in self.last[2:]:
                c.arrive()
            q = q + q_r1[self.rows].astype(F32) + q_r3[self.rows].astype(F32)
            igrad[self.rows] = q.astype(BF16)

    sums = [Sum(*part) for part in parts_of(SUM, tokens)]
    def far(group, *blocks):
        for fixed in blocks:
            for s in group:
                s.far(fixed)

    def near(group, *blocks):
        for fixed in blocks:
            for s in group:
                s.near(fixed)

    far(sums, 2, 1, 3, 0)
    mark("rs_far")
    accumulate((1, 3), (3, 3), (1, 2), (3, 2))

    accumulate((2, 1), (2, 3), (2, 2))
    mark("base")
    fa, fb = base[:, :256], base[:, 256:]
    for k in range(3):
        slocal[k, 0], slocal[k, 1] = fa.astype(BF16), fb.astype(BF16)
        fa = fa + mix(dot, fa, mats_loc, (k, 0))
        fb = fb + mix(dot, fb, mats_loc, (k, 1))
    slocal[3, 0], slocal[3, 1] = fa.astype(BF16), fb.astype(BF16)
    fc = fa + mix(dot, fa, mats_loc, (3, 0)) + mix(dot, fb, mats_loc, (4, 0))
    fd = fb + mix(dot, fa, mats_loc, (3, 1)) + mix(dot, fb, mats_loc, (4, 1))
    for c in range(4):
        side = fc if c < 2 else fd
        ssend[c] = side[:, (c % 2) * LANES : (c % 2) * LANES + LANES].astype(BF16)
    fwd_in = []
    for d in range(1, 4):
        fwd_in.append(send(ssend.at[wrap(z + d, SIDE)], szb.at[z], at(0, d)))
    szb[z] = ssend[z]
    mark("fwd_local")

    near(sums, 2, 1)
    mark("near1")

    def put_local(k, s, value):
        for j in range(2):
            gp[pl.ds(((k // 2) * 4 + 2 * s + j) * 128 + (k % 2) * 64, 64)] = value[
                :, j * LANES : (j + 1) * LANES
            ]

    for k in range(3):
        for s in range(2):
            put_local(k, s, near_extract(dot_tn(slocal[k, s], glocal[k, s]), k))
    for s in range(2):
        put_local(
            3, s,
            jnp.concatenate(
                [diag_extract(dot_tn(slocal[3, h], glocal[3, s])) for h in range(2)], axis=0
            ),
        )

    for c in fwd_in:
        c.arrive()
    pairs_apply(dot, (0, 1), szb, mats_z, s5b, zsend)
    fwd_arrive = cross(
        zsend, syb, y,
        lambda d: ((SIDE - d) % SIDE) * SIDE + wrap(z + d, SIDE),
        lambda d: wrap(z + d, SIDE),
    )
    mark("fwd_z")
    near(sums, 3, 0)
    for s in sums:
        s.last_far()
    mark("near2")

    def pair_grads(states, grads, dst):
        for k in range(2):
            for i, (a, b) in enumerate(PAIRS[k]):
                value = pair_extract(dot_tn(pair_of(states[k], a, b), pair_of(grads[k], a, b)))
                dst[a, k * 64 : k * 64 + 64] = value[:, :LANES]
                dst[b, k * 64 : k * 64 + 64] = value[:, LANES:]

    def piece(index):
        return pl.ds(pl.multiple_of(index * 128, 128), 128)

    pair_grads((szb, s5b), (gsave_z, gzb), gp_z)
    outz_in = []
    for d in range(1, 4):
        outz_in.append(send(gp_z.at[wrap(z + d, SIDE)], gp.at[piece(8 + z)], at(0, d)))
    gp[piece(8 + z)] = gp_z[z]

    fwd_arrive()
    pairs_apply(dot, (0, 1), syb, mats_y, s7b, qsend)
    query_in = []
    for d in range(1, 4):
        query_in.append(send(qsend.at[wrap(y + d, SIDE)], qb.at[z_of], at(d, 0)))
    qb[z_of] = qsend[y]
    mark("fwd_y")

    pair_grads((syb, s7b), (gsave_y, gyb), gp_y)
    outy_in = []
    for d in range(1, 4):
        outy_in.append(send(gp_y.at[wrap(y + d, SIDE)], gp.at[piece(12 + z_of)], at(d, 0)))
    gp[piece(12 + z_of)] = gp_y[y]
    mark("grads")

    class Slabs:
        def __init__(self, start, size, sums_ref, slab_ref):
            self.start, self.size = start, size
            self.sums_ref, self.slab_ref = sums_ref, slab_ref
            self.ins, self.outs = [], []

        def rows(self, dev):
            return pl.ds(pl.multiple_of(self.start + dev * self.size, 32), self.size)

        def scatter(self):
            all_rows = pl.ds(self.start, 16 * self.size)
            gpb[all_rows] = gp[all_rows].astype(BF16)
            for d in range(1, n_dp):
                dev = lax.rem(my_dp + d, n_dp)
                self.ins.append(send(gpb.at[self.rows(dev)], self.sums_ref.at[d], dev, "dp"))

        def gather(self):
            total = gp[self.rows(my_dp)]
            for d, c in zip(range(1, n_dp), self.ins):
                c.arrive()
                total = total + self.sums_ref[d].astype(F32)
            self.slab_ref[...] = (total * scale).astype(BF16)
            for d in range(1, n_dp):
                dev = lax.rem(my_dp + d, n_dp)
                self.outs.append(send(self.slab_ref, gout.at[self.rows(my_dp)], dev, "dp"))
            gout[self.rows(my_dp)] = self.slab_ref[...]

        def finish(self):
            for c in self.outs:
                c.arrive()

    early, late = Slabs(0, 96, sums_a, slab_a), Slabs(1536, 32, sums_b, slab_b)
    for c in outz_in:
        c.arrive()
    if n_dp > 1:
        early.scatter()
    for s in sums:
        s.last_near()
    mark("last_near")
    for c in outy_in:
        c.arrive()
    if n_dp > 1:
        late.scatter()
        early.gather()
        late.gather()
    mark("dp")

    for c in query_in:
        c.arrive()
    for c in range(4):
        query[:, c * LANES : (c + 1) * LANES] = qb[c]
    mark("query")
    for s in sums:
        s.end()
    mark("igrad")
    if n_dp > 1:
        early.finish()
        late.finish()
    final = gout if n_dp > 1 else gp
    for pair in range(4):
        for c in range(4):
            value = final[pl.ds((pair * 4 + c) * 128, 128)].astype(F32)
            for j in range(2):
                ggrad[2 * pair + j, :, c * LANES : (c + 1) * LANES] = value[j * 64 : j * 64 + 64]


def main_call(hidden, weight, generators, cotangent, n_dp=1, scale=1.0):
    tokens = hidden.shape[0]
    vm = lambda *shape, dtype=BF16: pltpu.VMEM(shape, dtype)
    chunks = vm(4, tokens, LANES)
    block = vm(tokens, 512)
    blocks = vm(4, tokens, 512)
    flops = 4 * tokens * 8192 * 512
    return pl.pallas_call(
        functools.partial(main_kernel, n_dp, scale),
        out_shape=(
            jax.ShapeDtypeStruct((tokens, 512), BF16),
            jax.ShapeDtypeStruct((tokens, 512), BF16),
            jax.ShapeDtypeStruct((8, 64, 512), F32),
        ),
        in_specs=[
            pl.BlockSpec(memory_space=pltpu.VMEM),
            pl.BlockSpec(memory_space=pl.ANY),
            pl.BlockSpec(memory_space=pltpu.VMEM),
            pl.BlockSpec(memory_space=pltpu.VMEM),
        ],
        out_specs=[pl.BlockSpec(memory_space=pltpu.VMEM)] * 3,
        scratch_shapes=[
            vm(8192, 512),
            vm(4, 4, tokens, 512),
            vm(tokens, 512, dtype=F32),
            vm(4, 4, tokens, 512, dtype=F32),
            vm(4, 2, 64, LANES, dtype=F32),
            vm(4, 2, 64, LANES, dtype=F32),
            chunks, chunks, chunks, chunks, chunks, chunks,
            chunks, vm(4, 4, 64, LANES, dtype=F32),
            vm(4, 2, tokens, 256),
            vm(4, 2, tokens, 256),
            chunks, chunks, chunks, chunks, chunks,
            chunks, chunks, chunks, chunks, chunks,
            block,
            blocks, blocks, blocks, blocks, blocks, blocks,
            block, block, block, block, block, block,
            vm(2048, 128, dtype=F32),
            vm(4, 128, 128, dtype=F32),
            vm(4, 128, 128, dtype=F32),
            vm(2048, 128),
            vm(16, 96, 128),
            vm(16, 32, 128),
            vm(96, 128),
            vm(32, 128),
            vm(2048, 128),
            vm(5, 2, 2, 256, 256),
            vm(2, 2, 2, 256, 256),
            vm(2, 2, 2, 256, 256),
            pltpu.SemaphoreType.DMA((N_SEMS,)),
            pltpu.SemaphoreType.DMA((N_SEMS,)),
            pltpu.SemaphoreType.DMA,
        ],
        compiler_params=pltpu.CompilerParams(
            collective_id=0, has_side_effects=True, vmem_limit_bytes=VMEM_BYTES
        ),
        cost_estimate=pl.CostEstimate(
            flops=flops, bytes_accessed=12 * 1024 * 1024, transcendentals=0
        ),
        name="adapt",
    )(hidden, weight, generators, cotangent)


def copy_kernel(*refs):
    count = len(refs) // 2
    for source, target in zip(refs[:count], refs[count:]):
        target[...] = source[...]


def copy_call(*arrays):
    whole = pl.BlockSpec(memory_space=pltpu.VMEM)
    return pl.pallas_call(
        copy_kernel,
        out_shape=tuple(jax.ShapeDtypeStruct(a.shape, a.dtype) for a in arrays),
        in_specs=[whole] * len(arrays),
        out_specs=[whole] * len(arrays),
        name="results",
    )(*arrays)


def on_device(hidden, base_weight, generators, cotangent):
    n = lax.axis_size("dp")
    scale = 1.0 / math.sqrt(hidden.shape[0] * n)
    return copy_call(*main_call(hidden, base_weight, generators, cotangent, n, scale))


def solution(mesh):
    placed = (P("dp", "tensor"), P(None, "tensor"), P(None, None, "tensor"), P("dp", "tensor"))
    return jax.shard_map(
        on_device,
        mesh=mesh,
        in_specs=placed,
        out_specs=(P("dp", "tensor"), P("dp", "tensor"), P(None, None, "tensor")),
        check_vma=False,
    )
```

```python
import functools
import math

import jax
import jax.numpy as jnp
from jax import lax
from jax.experimental import pallas as pl
from jax.experimental.pallas import tpu as pltpu
from jax.sharding import PartitionSpec as P

MESH = pl.DeviceIdType.MESH
F32 = jnp.float32
BF16 = jnp.bfloat16
SIDE = 4
LANES = 128
HALF = 32
VMEM_BYTES = 60 * 1024 * 1024


def wrap(value, n):
    return lax.rem(value + n, n)


def dot(a, b):
    return jnp.dot(a, b, preferred_element_type=F32)


def dot_nt(a, b):
    return lax.dot_general(a, b, (((1,), (1,)), ((), ())), preferred_element_type=F32)


def dot_tn(a, b):
    return lax.dot_general(a, b, (((0,), (0,)), ((), ())), preferred_element_type=F32)


def split(value):
    high = value.astype(BF16)
    return high, (value - high.astype(F32)).astype(BF16)


def put_split(ref, index, value):
    ref[(*index, 0)], ref[(*index, 1)] = split(value)


def mix(product, value, ref, index):
    top, rest = ref[(*index, 0)], ref[(*index, 1)]
    if value.dtype == BF16:
        return product(value, top) + product(value, rest)
    high, low = split(value)
    return product(high, top) + product(low, top) + product(high, rest)


def groups_of(shape):
    rows = lax.broadcasted_iota(jnp.int32, shape, 0) >> 5
    cols = lax.broadcasted_iota(jnp.int32, shape, 1) >> 5
    return rows, cols


def spread(block, mask, copies):
    return jnp.where(mask, jnp.concatenate([block] * copies, axis=0), 0.0)


def pair_matrix(gen_a, gen_b):
    both = jnp.concatenate([gen_a, gen_b], axis=1)
    rows, cols = groups_of((LANES, 2 * LANES))
    mask = rows == (cols & 3)
    return jnp.concatenate([spread(both[:HALF], mask, 4), spread(both[HALF:], mask, 4)], axis=0)


def pair_extract(grad):
    cols = (lax.broadcasted_iota(jnp.int32, (HALF, 2 * LANES), 1) >> 5) & 3
    parts = []
    for h in range(2):
        total = jnp.zeros((HALF, 2 * LANES), F32)
        for g in range(4):
            start = h * LANES + g * HALF
            total = total + jnp.where(cols == g, grad[start : start + HALF], 0.0)
        parts.append(total)
    return jnp.concatenate(parts, axis=0)


def near_matrix(gen, k):
    rows, cols = groups_of((256, 256))
    low = cols & ~(1 << k)
    return spread(gen[:HALF], rows == low, 8) + spread(gen[HALF:], rows == (low | (1 << k)), 8)


def near_extract(grad, k):
    cols = lax.broadcasted_iota(jnp.int32, (HALF, 256), 1) >> 5
    low = cols & ~(1 << k)
    parts = []
    for want in (low, low | (1 << k)):
        total = jnp.zeros((HALF, 256), F32)
        for g in range(8):
            total = total + jnp.where(want == g, grad[g * HALF : (g + 1) * HALF], 0.0)
        parts.append(total)
    return jnp.concatenate(parts, axis=0)


def diag_matrix(block):
    rows, cols = groups_of((256, 256))
    return spread(block, rows == cols, 8)


def diag_extract(grad):
    cols = lax.broadcasted_iota(jnp.int32, (HALF, 256), 1) >> 5
    total = jnp.zeros((HALF, 256), F32)
    for g in range(8):
        total = total + jnp.where(cols == g, grad[g * HALF : (g + 1) * HALF], 0.0)
    return total


PAIRS = (((0, 1), (2, 3)), ((0, 2), (1, 3)))
N_SEMS = 320
GATHER = (("z", "y", 0, 160), ("z", "y", 160, 352), ("y", "z", 352, 384))
SUM = (("y", "z", 0, 160), ("y", "z", 160, 352), ("z", "y", 352, 384))
STOP = None


def parts_of(table, tokens):
    scaled = [(a, b, lo * tokens // 384 // 32 * 32, hi * tokens // 384 // 32 * 32) for a, b, lo, hi in table]
    return [part for part in scaled if part[2] < part[3]]


class Stop(Exception):
    pass


class Sent:
    def __init__(self, copy):
        self.copy, self.received = copy, False

    def arrive(self):
        if not self.received:
            self.copy.wait_recv()
            self.received = True


def main_kernel(n_dp, scale, *refs):
    pending, endings = [], []
    try:
        main_body(n_dp, scale, pending, endings, *refs)
    except Stop:
        pass
    for c in pending:
        c.arrive()
        c.copy.wait_send()
    for end in endings:
        end()


def main_body(
    n_dp, scale, pending, endings,
    hid, wt, gen, cot, query, igrad, ggrad,
    w_v, hbuf, base, pb, gz, gy, gyb, gzb, ghome, gsave_y, gsave_z, gmid, cotc, genc, glocal, slocal,
    szb, ssend, syb, qsend, qb, s5b, s7b, zsend, gsend_t, gsend_z, gb,
    rs_s2, rs_r2, rs_s1, rs_s3, rs_r1, rs_r3, q_s2, q_r2, q_s1, q_s3, q_r1, q_r3,
    gp, gp_z, gp_y, gpb, sums_a, sums_b, slab_a, slab_b, gout, mats_loc, mats_z, mats_y,
    send_sem, recv_sem, w_sem,
):
    tokens = hid.shape[0]
    me = lax.axis_index("tensor")
    my_dp = lax.axis_index("dp")
    y, z = me // SIDE, lax.rem(me, SIDE)
    z_of = lax.rem(y + z, SIDE)
    counter = [0]

    def mark(name):
        if STOP == name:
            if name == "bwd_y":
                w_copy.wait()
            raise Stop

    def at(dy, dz):
        return wrap(y + dy, SIDE) * SIDE + wrap(z + dz, SIDE)

    def toward(axis, step):
        return at(step, 0) if axis == "y" else at(0, step)

    def place(axis, step, fixed):
        return (step, fixed) if axis == "y" else (fixed, step)

    def ids(n=1):
        first = counter[0]
        counter[0] += n
        return first

    def copy(src, dst, send_index, recv_index, device):
        return pltpu.make_async_remote_copy(
            src_ref=src,
            dst_ref=dst,
            send_sem=send_sem.at[send_index],
            recv_sem=recv_sem.at[recv_index],
            device_id=device,
            device_id_type=MESH,
        )

    def send(src, dst, dev, axis="tensor"):
        index = ids()
        c = copy(src, dst, index, index, {axis: dev})
        c.start()
        c = Sent(c)
        pending.append(c)
        return c

    def w_rows(dy, dz):
        return w_v[pl.ds(pl.multiple_of(at(dy, dz) * 512, 512), 512), :]

    w_copy = pltpu.make_async_copy(wt, w_v, w_sem)
    for c in range(4):
        cols = slice(c * LANES, (c + 1) * LANES)
        cotc[c] = cot[:, cols]
        genc[c] = gen[4:8, :, cols]

    barrier = pltpu.get_barrier_semaphore()
    for d in range(1, 16):
        pl.semaphore_signal(
            barrier, inc=1, device_id={"tensor": lax.rem(me + d, 16)}, device_id_type=MESH
        )
    for d in range(1, n_dp):
        pl.semaphore_signal(
            barrier, inc=1, device_id={"dp": lax.rem(my_dp + d, n_dp)}, device_id_type=MESH
        )
    pl.semaphore_wait(barrier, 15 + n_dp - 1)

    cot_in, genz_in, geny_in = [], [], []
    for d in range(1, 4):
        c = lax.rem(y + d + z, SIDE)
        cot_in.append(send(cotc.at[c], gyb.at[y], at(d, 0)))
        geny_in.append(send(genc.at[c, pl.ds(2, 2)], gy.at[y], at(d, 0)))

    def held(dy, dz, lo, hi):
        ref = hid if (dy, dz) == (0, 0) else hbuf.at[dy, dz]
        return ref.at[pl.ds(lo, hi - lo)]

    arrivals = {(dy, dz): [] for dy in range(4) for dz in range(4)}

    def hop(axis, fixed, step, sign, lo, hi):
        target = place(axis, step + sign & 3, fixed)
        c = send(
            held(*place(axis, step, fixed), lo, hi),
            hbuf.at[(*target, pl.ds(lo, hi - lo))],
            toward(axis, sign),
        )
        arrivals[target].append(c)
        return c

    def ring_start(axis, fixed, lo, hi):
        return [hop(axis, fixed, 0, 1, lo, hi), hop(axis, fixed, 0, -1, lo, hi)]

    def ring_forward(axis, fixed, lo, hi, copies):
        middle = (lo + hi) // 2
        copies[0].arrive()
        copies.append(hop(axis, fixed, 1, 1, lo, middle))
        copies[1].arrive()
        copies.append(hop(axis, fixed, 3, -1, middle, hi))

    routes = parts_of(GATHER, tokens)
    first = [ring_start(a, 0, lo, hi) for a, _, lo, hi in routes]
    second = [{0: ring_start(b, 0, lo, hi)} for _, b, lo, hi in routes]
    for d in range(1, 4):
        genz_in.append(send(genc.at[wrap(z + d, SIDE), pl.ds(0, 2)], gz.at[z], at(0, d)))

    w_copy.start()

    def gather_second(step, parts):
        for i in parts:
            _, b, lo, hi = routes[i]
            ring_forward(b, step, lo, hi, second[i][step])

    def gather_first(parts):
        for i in parts:
            a, b, lo, hi = routes[i]
            ring, copies, middle = first[i], second[i], (lo + hi) // 2
            ring[0].arrive()
            ring.append(hop(a, 0, 1, 1, lo, middle))
            copies[1] = ring_start(b, 1, lo, hi)
            ring[1].arrive()
            ring.append(hop(a, 0, 3, -1, middle, hi))
            copies[3] = ring_start(b, 3, lo, hi)

    def gather_far(parts):
        for i in parts:
            _, b, lo, hi = routes[i]
            first[i][2].arrive()
            first[i][3].arrive()
            second[i][2] = ring_start(b, 2, lo, hi)

    z_parts = [i for i, part in enumerate(routes) if part[0] == "z"]
    y_parts = [i for i, part in enumerate(routes) if part[0] == "y"]

    def accumulate(*blocks):
        for dy, dz in blocks:
            for c in arrivals[dy, dz]:
                c.arrive()
            base[...] += dot(hbuf[dy, dz], w_rows(-dy, -dz))

    gyb[y] = cotc[z_of]
    gy[y] = genc[z_of, 2:4]
    gz[z] = genc[z, 0:2]

    for k in range(3):
        for s in range(2):
            put_split(mats_loc, (k, s), near_matrix(gen[k, :, 256 * s : 256 * s + 256], k))
    for s in range(2):
        for h in range(2):
            block = gen[3, HALF * h : HALF * h + HALF, 256 * s : 256 * s + 256]
            put_split(mats_loc, (3 + h, s), diag_matrix(block))

    def pair_of(ref, a, b):
        return jnp.concatenate([ref[a], ref[b]], axis=1)

    def fill_pairs(mats, gens):
        for k in range(2):
            for i, (a, b) in enumerate(PAIRS[k]):
                put_split(mats, (k, i), pair_matrix(gens[a, k], gens[b, k]))

    def pairs_apply(product, order, source, mats, save, out):
        values = None
        for k, target in zip(order, (save, out)):
            new = [None] * 4
            for i, (a, b) in enumerate(PAIRS[k]):
                if values is None:
                    v = pair_of(source, a, b)
                else:
                    v = jnp.concatenate([values[a], values[b]], axis=1)
                v = v.astype(F32) + mix(product, v, mats, (k, i))
                new[a], new[b] = v[:, :LANES], v[:, LANES:]
            values = new
            for m in range(4):
                target[m] = values[m].astype(BF16)

    def cross(src, dst, own_slot, dev_of, src_of):
        index = ids(4)
        sent = []
        for d in range(4):
            c = copy(
                src.at[src_of(d)], dst.at[own_slot], index + d, index + own_slot,
                {"tensor": dev_of(d)},
            )
            if d == 0:
                keep = pltpu.make_async_copy(
                    src.at[src_of(0)], dst.at[own_slot], recv_sem.at[index + own_slot]
                )
                pl.when(dev_of(0) != me)(lambda c=c: c.start())
                pl.when(dev_of(0) == me)(lambda keep=keep: keep.start())
            else:
                c.start()
            sent.append(c)
        done = []

        def arrive():
            if not done:
                done.append(True)
                for m in range(4):
                    pltpu.make_async_copy(src.at[m], dst.at[m], recv_sem.at[index + m]).wait()

        def finish():
            arrive()
            pl.when(dev_of(0) != me)(lambda: sent[0].wait_send())
            for c in sent[1:]:
                c.wait_send()

        endings.append(finish)
        return arrive

    for c in geny_in:
        c.arrive()
    fill_pairs(mats_y, gy)
    for c in cot_in:
        c.arrive()
    pairs_apply(dot_nt, (1, 0), gyb, mats_y, gsave_y, gsend_t)
    step_in = []
    for d in range(1, 4):
        step_in.append(send(gsend_t.at[wrap(y + d, SIDE)], gmid.at[z_of], at(d, 0)))
    gmid[z_of] = gsend_t[y]
    mark("bwd_y")

    gather_second(0, z_parts)
    for c in genz_in:
        c.arrive()
    fill_pairs(mats_z, gz)
    for c in step_in:
        c.arrive()
    step_in = []
    for d in range(1, 4):
        step_in.append(send(gmid.at[wrap(z + d, SIDE)], gzb.at[z], at(0, d)))
    gzb[z] = gmid[z]
    mark("ag0")

    gather_first(z_parts)
    gather_first(y_parts)
    gather_second(0, y_parts)
    w_copy.wait()
    base[...] = dot(hid[...], w_rows(0, 0))
    mark("ag1")
    for c in step_in:
        c.arrive()
    pairs_apply(dot_nt, (1, 0), gzb, mats_z, gsave_z, gsend_z)
    back_in = []
    for d in range(1, 4):
        back_in.append(send(gsend_z.at[wrap(z + d, SIDE)], ghome.at[z], at(0, d)))
    ghome[z] = gsend_z[z]
    mark("bwd_z")

    gather_far(z_parts)
    gather_second(1, z_parts)
    gather_second(3, z_parts)
    gather_far(y_parts)
    accumulate((1, 0), (3, 0), (0, 1), (0, 3))
    mark("ag2")

    for c in back_in:
        c.arrive()
    ga = pair_of(ghome, 0, 1)
    gc = pair_of(ghome, 2, 3)
    glocal[3, 0], glocal[3, 1] = ga, gc
    fa = ga.astype(F32) + mix(dot_nt, ga, mats_loc, (3, 0)) + mix(dot_nt, gc, mats_loc, (3, 1))
    fb = gc.astype(F32) + mix(dot_nt, ga, mats_loc, (4, 0)) + mix(dot_nt, gc, mats_loc, (4, 1))
    for k in (2, 1, 0):
        glocal[k, 0], glocal[k, 1] = fa.astype(BF16), fb.astype(BF16)
        fa = fa + mix(dot_nt, fa, mats_loc, (k, 0))
        fb = fb + mix(dot_nt, fb, mats_loc, (k, 1))
    gb[:, :256] = fa.astype(BF16)
    gb[:, 256:] = fb.astype(BF16)
    mark("bwd_local")

    gather_second(1, y_parts)
    gather_second(3, y_parts)
    gather_second(2, z_parts)
    gather_second(2, y_parts)
    mark("ag3")

    computed = set()

    def partial(dy, dz, lo, hi):
        if (dy, dz) not in computed:
            computed.add((dy, dz))
            pb[dy, dz] = dot_nt(gb[...], w_rows(dy, dz))
        return pb[dy, dz, lo:hi]

    class Sum:
        def __init__(self, a, b, lo, hi):
            self.a, self.b, self.lo, self.hi, self.middle = a, b, lo, hi, (lo + hi) // 2
            self.copies, self.last = {}, []
            self.rows = pl.ds(lo, hi - lo)
            self.top, self.low = pl.ds(lo, self.middle - lo), pl.ds(self.middle, hi - self.middle)

        def far(self, fixed):
            block = partial(*place(self.a, 2, fixed), self.lo, self.hi)
            rs_s2[fixed, self.rows] = block.astype(BF16)
            self.copies[fixed] = [
                send(rs_s2.at[fixed, self.top], rs_r2.at[fixed, self.top], toward(self.a, 1)),
                send(rs_s2.at[fixed, self.low], rs_r2.at[fixed, self.low], toward(self.a, -1)),
            ]

        def near(self, fixed):
            cs, size = self.copies[fixed], self.middle - self.lo
            p = partial(*place(self.a, 1, fixed), self.lo, self.hi)
            cs[0].arrive()
            rs_s1[fixed, self.top] = (p[:size] + rs_r2[fixed, self.top].astype(F32)).astype(BF16)
            rs_s1[fixed, self.low] = p[size:].astype(BF16)
            cs.append(
                send(rs_s1.at[fixed, self.rows], rs_r1.at[fixed, self.rows], toward(self.a, 1))
            )
            p = partial(*place(self.a, 3, fixed), self.lo, self.hi)
            cs[1].arrive()
            rs_s3[fixed, self.top] = p[:size].astype(BF16)
            rs_s3[fixed, self.low] = (p[size:] + rs_r2[fixed, self.low].astype(F32)).astype(BF16)
            cs.append(
                send(rs_s3.at[fixed, self.rows], rs_r3.at[fixed, self.rows], toward(self.a, -1))
            )

        def whole(self, fixed):
            p = partial(*place(self.a, 0, fixed), self.lo, self.hi)
            for c in self.copies[fixed][2:]:
                c.arrive()
            return p + rs_r1[fixed, self.rows].astype(F32) + rs_r3[fixed, self.rows].astype(F32)

        def last_far(self):
            q_s2[self.rows] = self.whole(2).astype(BF16)
            self.last = [
                send(q_s2.at[self.top], q_r2.at[self.top], toward(self.b, 1)),
                send(q_s2.at[self.low], q_r2.at[self.low], toward(self.b, -1)),
            ]

        def last_near(self):
            size = self.middle - self.lo
            q = self.whole(1)
            self.last[0].arrive()
            q_s1[self.top] = (q[:size] + q_r2[self.top].astype(F32)).astype(BF16)
            q_s1[self.low] = q[size:].astype(BF16)
            self.last.append(send(q_s1.at[self.rows], q_r1.at[self.rows], toward(self.b, 1)))
            q = self.whole(3)
            self.last[1].arrive()
            q_s3[self.top] = q[:size].astype(BF16)
            q_s3[self.low] = (q[size:] + q_r2[self.low].astype(F32)).astype(BF16)
            self.last.append(send(q_s3.at[self.rows], q_r3.at[self.rows], toward(self.b, -1)))

        def end(self):
            q = self.whole(0)
            for c in self.last[2:]:
                c.arrive()
            q = q + q_r1[self.rows].astype(F32) + q_r3[self.rows].astype(F32)
            igrad[self.rows] = q.astype(BF16)

    sums = [Sum(*part) for part in parts_of(SUM, tokens)]
    def far(group, *blocks):
        for fixed in blocks:
            for s in group:
                s.far(fixed)

    def near(group, *blocks):
        for fixed in blocks:
            for s in group:
                s.near(fixed)

    far(sums, 2, 1, 3, 0)
    mark("rs_far")
    accumulate((2, 0), (0, 2), (1, 1), (3, 1), (1, 3), (3, 3), (1, 2), (3, 2))

    accumulate((2, 1), (2, 3), (2, 2))
    mark("base")
    fa, fb = base[:, :256], base[:, 256:]
    for k in range(3):
        slocal[k, 0], slocal[k, 1] = fa.astype(BF16), fb.astype(BF16)
        fa = fa + mix(dot, fa, mats_loc, (k, 0))
        fb = fb + mix(dot, fb, mats_loc, (k, 1))
    slocal[3, 0], slocal[3, 1] = fa.astype(BF16), fb.astype(BF16)
    fc = fa + mix(dot, fa, mats_loc, (3, 0)) + mix(dot, fb, mats_loc, (4, 0))
    fd = fb + mix(dot, fa, mats_loc, (3, 1)) + mix(dot, fb, mats_loc, (4, 1))
    for c in range(4):
        side = fc if c < 2 else fd
        ssend[c] = side[:, (c % 2) * LANES : (c % 2) * LANES + LANES].astype(BF16)
    fwd_in = []
    for d in range(1, 4):
        fwd_in.append(send(ssend.at[wrap(z + d, SIDE)], szb.at[z], at(0, d)))
    szb[z] = ssend[z]
    mark("fwd_local")

    near(sums, 2, 1)
    mark("near1")

    def put_local(k, s, value):
        for j in range(2):
            gp[pl.ds(((k // 2) * 4 + 2 * s + j) * 128 + (k % 2) * 64, 64)] = value[
                :, j * LANES : (j + 1) * LANES
            ]

    for k in range(3):
        for s in range(2):
            put_local(k, s, near_extract(dot_tn(slocal[k, s], glocal[k, s]), k))
    for s in range(2):
        put_local(
            3, s,
            jnp.concatenate(
                [diag_extract(dot_tn(slocal[3, h], glocal[3, s])) for h in range(2)], axis=0
            ),
        )

    for c in fwd_in:
        c.arrive()
    pairs_apply(dot, (0, 1), szb, mats_z, s5b, zsend)
    fwd_arrive = cross(
        zsend, syb, y,
        lambda d: ((SIDE - d) % SIDE) * SIDE + wrap(z + d, SIDE),
        lambda d: wrap(z + d, SIDE),
    )
    mark("fwd_z")
    near(sums, 3)
    for s in sums:
        if s.a == "y":
            s.last_far()
    mark("near2")

    def pair_grads(states, grads, dst):
        for k in range(2):
            for i, (a, b) in enumerate(PAIRS[k]):
                value = pair_extract(dot_tn(pair_of(states[k], a, b), pair_of(grads[k], a, b)))
                dst[a, k * 64 : k * 64 + 64] = value[:, :LANES]
                dst[b, k * 64 : k * 64 + 64] = value[:, LANES:]

    def piece(index):
        return pl.ds(pl.multiple_of(index * 128, 128), 128)

    pair_grads((szb, s5b), (gsave_z, gzb), gp_z)
    outz_in = []
    for d in range(1, 4):
        outz_in.append(send(gp_z.at[wrap(z + d, SIDE)], gp.at[piece(8 + z)], at(0, d)))
    gp[piece(8 + z)] = gp_z[z]

    fwd_arrive()
    pairs_apply(dot, (0, 1), syb, mats_y, s7b, qsend)
    query_in = []
    for d in range(1, 4):
        query_in.append(send(qsend.at[wrap(y + d, SIDE)], qb.at[z_of], at(d, 0)))
    qb[z_of] = qsend[y]
    mark("fwd_y")

    pair_grads((syb, s7b), (gsave_y, gyb), gp_y)
    outy_in = []
    for d in range(1, 4):
        outy_in.append(send(gp_y.at[wrap(y + d, SIDE)], gp.at[piece(12 + z_of)], at(d, 0)))
    gp[piece(12 + z_of)] = gp_y[y]
    mark("grads")

    class Slabs:
        def __init__(self, start, size, sums_ref, slab_ref):
            self.start, self.size = start, size
            self.sums_ref, self.slab_ref = sums_ref, slab_ref
            self.ins, self.outs = [], []

        def rows(self, dev):
            return pl.ds(pl.multiple_of(self.start + dev * self.size, 32), self.size)

        def scatter(self):
            all_rows = pl.ds(self.start, 16 * self.size)
            gpb[all_rows] = gp[all_rows].astype(BF16)
            for d in range(1, n_dp):
                dev = lax.rem(my_dp + d, n_dp)
                self.ins.append(send(gpb.at[self.rows(dev)], self.sums_ref.at[d], dev, "dp"))

        def gather(self):
            total = gp[self.rows(my_dp)]
            for d, c in zip(range(1, n_dp), self.ins):
                c.arrive()
                total = total + self.sums_ref[d].astype(F32)
            self.slab_ref[...] = (total * scale).astype(BF16)
            for d in range(1, n_dp):
                dev = lax.rem(my_dp + d, n_dp)
                self.outs.append(send(self.slab_ref, gout.at[self.rows(my_dp)], dev, "dp"))
            gout[self.rows(my_dp)] = self.slab_ref[...]

        def finish(self):
            for c in self.outs:
                c.arrive()

    near(sums, 0)
    for s in sums:
        if s.a == "z":
            s.last_far()
    early, late = Slabs(0, 96, sums_a, slab_a), Slabs(1536, 32, sums_b, slab_b)
    for c in outz_in:
        c.arrive()
    if n_dp > 1:
        early.scatter()
    for s in sums:
        s.last_near()
    mark("last_near")
    for c in outy_in:
        c.arrive()
    if n_dp > 1:
        late.scatter()
        early.gather()
        late.gather()
    mark("dp")

    for c in query_in:
        c.arrive()
    for c in range(4):
        query[:, c * LANES : (c + 1) * LANES] = qb[c]
    mark("query")
    for s in sums:
        s.end()
    mark("igrad")
    if n_dp > 1:
        early.finish()
        late.finish()
    final = gout if n_dp > 1 else gp
    for pair in range(4):
        for c in range(4):
            value = final[pl.ds((pair * 4 + c) * 128, 128)].astype(F32)
            for j in range(2):
                ggrad[2 * pair + j, :, c * LANES : (c + 1) * LANES] = value[j * 64 : j * 64 + 64]


def main_call(hidden, weight, generators, cotangent, n_dp=1, scale=1.0):
    tokens = hidden.shape[0]
    vm = lambda *shape, dtype=BF16: pltpu.VMEM(shape, dtype)
    chunks = vm(4, tokens, LANES)
    block = vm(tokens, 512)
    blocks = vm(4, tokens, 512)
    flops = 4 * tokens * 8192 * 512
    return pl.pallas_call(
        functools.partial(main_kernel, n_dp, scale),
        out_shape=(
            jax.ShapeDtypeStruct((tokens, 512), BF16),
            jax.ShapeDtypeStruct((tokens, 512), BF16),
            jax.ShapeDtypeStruct((8, 64, 512), F32),
        ),
        in_specs=[
            pl.BlockSpec(memory_space=pltpu.VMEM),
            pl.BlockSpec(memory_space=pl.ANY),
            pl.BlockSpec(memory_space=pltpu.VMEM),
            pl.BlockSpec(memory_space=pltpu.VMEM),
        ],
        out_specs=[pl.BlockSpec(memory_space=pltpu.VMEM)] * 3,
        scratch_shapes=[
            vm(8192, 512),
            vm(4, 4, tokens, 512),
            vm(tokens, 512, dtype=F32),
            vm(4, 4, tokens, 512, dtype=F32),
            vm(4, 2, 64, LANES, dtype=F32),
            vm(4, 2, 64, LANES, dtype=F32),
            chunks, chunks, chunks, chunks, chunks, chunks,
            chunks, vm(4, 4, 64, LANES, dtype=F32),
            vm(4, 2, tokens, 256),
            vm(4, 2, tokens, 256),
            chunks, chunks, chunks, chunks, chunks,
            chunks, chunks, chunks, chunks, chunks,
            block,
            blocks, blocks, blocks, blocks, blocks, blocks,
            block, block, block, block, block, block,
            vm(2048, 128, dtype=F32),
            vm(4, 128, 128, dtype=F32),
            vm(4, 128, 128, dtype=F32),
            vm(2048, 128),
            vm(16, 96, 128),
            vm(16, 32, 128),
            vm(96, 128),
            vm(32, 128),
            vm(2048, 128),
            vm(5, 2, 2, 256, 256),
            vm(2, 2, 2, 256, 256),
            vm(2, 2, 2, 256, 256),
            pltpu.SemaphoreType.DMA((N_SEMS,)),
            pltpu.SemaphoreType.DMA((N_SEMS,)),
            pltpu.SemaphoreType.DMA,
        ],
        compiler_params=pltpu.CompilerParams(
            collective_id=0, has_side_effects=True, vmem_limit_bytes=VMEM_BYTES
        ),
        cost_estimate=pl.CostEstimate(
            flops=flops, bytes_accessed=12 * 1024 * 1024, transcendentals=0
        ),
        name="adapt",
    )(hidden, weight, generators, cotangent)


def copy_kernel(*refs):
    count = len(refs) // 2
    for source, target in zip(refs[:count], refs[count:]):
        target[...] = source[...]


def copy_call(*arrays):
    whole = pl.BlockSpec(memory_space=pltpu.VMEM)
    return pl.pallas_call(
        copy_kernel,
        out_shape=tuple(jax.ShapeDtypeStruct(a.shape, a.dtype) for a in arrays),
        in_specs=[whole] * len(arrays),
        out_specs=[whole] * len(arrays),
        name="results",
    )(*arrays)


def on_device(hidden, base_weight, generators, cotangent):
    n = lax.axis_size("dp")
    scale = 1.0 / math.sqrt(hidden.shape[0] * n)
    return copy_call(*main_call(hidden, base_weight, generators, cotangent, n, scale))


def solution(mesh):
    placed = (P("dp", "tensor"), P(None, "tensor"), P(None, None, "tensor"), P("dp", "tensor"))
    return jax.shard_map(
        on_device,
        mesh=mesh,
        in_specs=placed,
        out_specs=(P("dp", "tensor"), P("dp", "tensor"), P(None, None, "tensor")),
        check_vma=False,
    )
```
